32 devices in a mesh: rows: 8 (over z, y), seq: 4 (over x, core).
Axes of the slice: x: 2, y: 2, z: 4, core: 2. Of those that a mesh axis runs over, the one named last changes fastest.
Arguments:
- tokens: bfloat16 [16, 2048, 768], P('rows', 'seq'), may hold values from -6 to 6
- segments: int32 [16, 2048], P('rows'), may hold values from 0 to 1022, as said below
- query_weight: bfloat16 [768, 768], replicated, may hold values from -0.21875 to 0.21875
- query_bias: float32 [768], replicated, may hold values from -1.75 to 1.75
- key_weight: bfloat16 [768, 768], replicated, may hold values from -0.21875 to 0.21875
- value_weight: bfloat16 [768, 768], replicated, may hold values from -0.21875 to 0.21875
- value_bias: float32 [768], replicated, may hold values from -1.75 to 1.75
- out_weight: bfloat16 [768, 768], replicated, may hold values from -0.875 to 0.875
- out_bias: float32 [768], replicated, may hold values from -1.75 to 1.75
- first_gain: float32 [768], replicated, may hold values from 0.5 to 1.5
- first_shift: float32 [768], replicated, may hold values from -1.75 to 1.75
- up_weight: bfloat16 [768, 3072], replicated, may hold values from -0.21875 to 0.21875
- up_bias: float32 [3072], replicated, may hold values from -1.75 to 1.75
- down_weight: bfloat16 [3072, 768], replicated, may hold values from -0.109375 to 0.109375
- down_bias: float32 [768], replicated, may hold values from -1.75 to 1.75
- second_gain: float32 [768], replicated, may hold values from 0.5 to 1.5
- second_shift: float32 [768], replicated, may hold values from -1.75 to 1.75
- cotangent: bfloat16 [16, 2048, 768], P('rows', 'seq'), may hold values from -18 to 18
Outputs:
- output: bfloat16 [16, 2048, 768], P('rows', 'seq')
- input_grad: float32 [16, 2048, 768], P('rows', 'seq')
- queryweight_grad: float32 [768, 768], replicated
- querybias_grad: float32 [768], replicated
- keyweight_grad: float32 [768, 768], replicated
- valueweight_grad: float32 [768, 768], replicated
- valuebias_grad: float32 [768], replicated
- outweight_grad: float32 [768, 768], replicated
- outbias_grad: float32 [768], replicated
- firstgain_grad: float32 [768], replicated
- firstshift_grad: float32 [768], replicated
- upweight_grad: float32 [768, 3072], replicated
- upbias_grad: float32 [3072], replicated
- downweight_grad: float32 [3072, 768], replicated
- downbias_grad: float32 [768], replicated
- secondgain_grad: float32 [768], replicated
- secondshift_grad: float32 [768], replicated
The draws below stay inside these ranges and needn't reach their ends.
Inputs may be any that keep to these rules, and one draw needn't show every extreme that they name: `segments`: within each row the numbers start at 0 and never fall; in each row one segment covers a position among the first 512 and one among the last 512; some row reaches the most, 1022.
All inputs are finite; a program needn't handle non-finite values.
Results may differ from the reference program's by a relative error of at most 0.013.
Values may be sent and summed in bfloat16 or wider, within the bound.
No kernel may reach another device: no remote copies, remote signals or barrier semaphores. Data moves between devices by JAX's collectives and lax.ppermute only.
A program may use at most 512 MiB of HBM per device.

```python
import math
import jax
import jax.numpy as jnp
from jax import lax

D = 768
HEADS = 12
HEAD = 64
FF = 3072
POS_DEV = 512
ROWS = 16
LENGTH = 2048


def draw_segments(key, part):
    key = jax.random.fold_in(key, 7)
    first_key, second_key, third_key, fourth_key = jax.random.split(key, 4)
    chosen = jax.random.randint(fourth_key, (), 0, ROWS)
    is_full = (jnp.arange(ROWS, dtype=jnp.int32) == chosen)[:, None]
    starts = jax.random.randint(first_key, (ROWS, 1), 1, POS_DEV)
    stops = jax.random.randint(second_key, (ROWS, 1), LENGTH - POS_DEV + 1, LENGTH)
    starts = jnp.where(is_full, POS_DEV - 1, starts).astype(jnp.int32)
    stops = jnp.where(is_full, LENGTH - POS_DEV + 1, stops).astype(jnp.int32)
    places = jnp.arange(LENGTH, dtype=jnp.int32)[None, :]
    coins = jax.random.randint(third_key, (ROWS, LENGTH), 0, 6)
    coins = jnp.where(is_full, 0, coins)
    outside = ((places < starts) | (places > stops)) & (places > 0)
    random_cut = jnp.where(outside & (coins == 0), 1, 0)
    forced = jnp.where((places == starts) | (places == stops), 1, 0)
    boundary = jnp.maximum(random_cut, forced).astype(jnp.int32)
    return jnp.cumsum(boundary, axis=1).astype(jnp.int32)


def draw_cotangent(key, part):
    key = jax.random.fold_in(key, 11)
    first_key = jax.random.fold_in(key, 0)
    row_place = jnp.arange(ROWS, dtype=jnp.float32) / max(ROWS - 1, 1)
    col_place = jnp.arange(LENGTH, dtype=jnp.float32) / (LENGTH - 1)
    scaling = jnp.exp(math.log(3.0) * row_place)[:, None, None] * jnp.exp(math.log(3.0) * col_place)[None, :, None] / 3.0
    base = jnp.clip(jax.random.normal(first_key, (ROWS, LENGTH, D), jnp.float32), -6.0, 6.0)
    return (base * scaling).astype(jnp.bfloat16)


def steps_of(key, extent, shards, smallest, top_value):
    gain = 1.0
    for dim, parts in shards:
        draws = jax.random.uniform(jax.random.fold_in(jax.random.fold_in(key, 6), dim), (parts,), jnp.float32, smallest / len(shards), top_value / len(shards))
        gain = gain * jnp.repeat(jnp.exp(draws), extent[dim] // parts).reshape((-1,) + (1,) * (len(extent) - 1 - dim))
    return gain


def scatter_about(own_key, dims, spread, most, pieces=(), kind=jnp.bfloat16):
    entries = jax.random.normal(own_key, dims, jnp.float32) * spread
    if len(pieces) > 0:
        entries = steps_of(own_key, dims, pieces, -0.22, 0.18) * entries
    return jnp.clip(entries, min=-most, max=most).astype(kind)


def setup_inputs(seed: int = 0) -> dict:
    seeds = jax.random.split(jax.random.key(seed), 19)
    tokens = scatter_about(seeds[0], (ROWS, LENGTH, D), 1.0, 6.0, ((0, 8), (1, 4)))
    segments = draw_segments(jax.random.fold_in(seeds[18], 71), 0)
    query_weight = scatter_about(seeds[2], (D, D), D ** -0.5, 0.21875)
    query_bias = scatter_about(seeds[3], (D,), 0.3, 1.75, (), jnp.float32)
    key_weight = scatter_about(seeds[4], (D, D), D ** -0.5, 0.21875)
    value_weight = scatter_about(seeds[5], (D, D), D ** -0.5, 0.21875)
    value_bias = scatter_about(seeds[6], (D,), 0.3, 1.75, (), jnp.float32)
    out_weight = scatter_about(seeds[7], (D, D), (D // 16) ** -0.5, 0.875)
    out_bias = scatter_about(seeds[8], (D,), 0.3, 1.75, (), jnp.float32)
    first_gain = jnp.clip(1.0 + 0.1 * jax.random.normal(seeds[9], (D,), jnp.float32), 0.5, 1.5)
    first_shift = scatter_about(seeds[10], (D,), 0.3, 1.75, (), jnp.float32)
    up_weight = scatter_about(seeds[11], (D, FF), D ** -0.5, 0.21875)
    up_bias = scatter_about(seeds[12], (FF,), 0.3, 1.75, (), jnp.float32)
    down_weight = scatter_about(seeds[13], (FF, D), FF ** -0.5, 0.109375)
    down_bias = scatter_about(seeds[14], (D,), 0.3, 1.75, (), jnp.float32)
    second_gain = jnp.clip(1.0 + 0.1 * jax.random.normal(seeds[15], (D,), jnp.float32), 0.5, 1.5)
    second_shift = scatter_about(seeds[16], (D,), 0.3, 1.75, (), jnp.float32)
    cotangent = draw_cotangent(jax.random.fold_in(seeds[18], 71), 0)
    return dict(tokens=tokens, segments=segments, query_weight=query_weight, query_bias=query_bias, key_weight=key_weight, value_weight=value_weight, value_bias=value_bias, out_weight=out_weight, out_bias=out_bias, first_gain=first_gain, first_shift=first_shift, up_weight=up_weight, up_bias=up_bias, down_weight=down_weight, down_bias=down_bias, second_gain=second_gain, second_shift=second_shift, cotangent=cotangent)


@jax.custom_vjp
def low(v):
    return lax.optimization_barrier(v.astype(jnp.bfloat16)).astype(jnp.float32)

@jax.custom_vjp
def low_back(v):
    return v

def low_keep(v):
    return (low(v), None)

def low_pass(kept, grad):
    return (grad,)

def back_keep(v):
    return (v, None)

def back_low(kept, grad):
    return (low(grad),)
low.defvjp(low_keep, low_pass)
low_back.defvjp(back_keep, back_low)
EPSILON = 1e-06

def matmul_high(left, right):
    return jnp.matmul(left, right, precision=lax.Precision.HIGHEST)

def normalize(values, gain_vec, shift_vec):
    centered = values - lax.optimization_barrier(jnp.mean(values, axis=-1, keepdims=True))
    variance = lax.optimization_barrier(jnp.mean(centered * centered, axis=-1, keepdims=True))
    return centered * lax.rsqrt(variance + EPSILON) * gain_vec + shift_vec

def forward(inputs, seg_rows, params):
    query_weight, query_bias, key_weight, value_weight, value_bias, out_weight, out_bias, first_gain, first_shift, up_weight, up_bias, down_weight, down_bias, second_gain, second_shift = params
    row_count = inputs.shape[0]
    seq_length = inputs.shape[1]
    scale = HEAD ** (-0.5)
    queries = low_back(low(matmul_high(inputs, query_weight) + query_bias)).reshape(row_count, seq_length, HEADS, HEAD)
    keys_all = low_back(low(matmul_high(inputs, key_weight))).reshape(row_count, seq_length, HEADS, HEAD)
    values_all = low_back(low(matmul_high(inputs, value_weight) + value_bias)).reshape(row_count, seq_length, HEADS, HEAD)
    scores = low_back(jnp.einsum('gqhe,gkhe->ghqk', queries, keys_all, precision=lax.Precision.HIGHEST) * scale)
    allowed = seg_rows[:, None, :, None] == seg_rows[:, None, None, :]
    scores = jnp.where(allowed, scores, -1e+30)
    scores = scores - lax.optimization_barrier(jnp.max(scores, axis=-1, keepdims=True))
    raised = jnp.exp(scores)
    attention = low(raised / lax.optimization_barrier(jnp.sum(raised, axis=-1, keepdims=True)))
    context = low_back(low(jnp.einsum('ghqk,gkhe->gqhe', attention, values_all, precision=lax.Precision.HIGHEST)))
    context = context.reshape(row_count, seq_length, HEADS * HEAD)
    branch = low_back(matmul_high(context, out_weight) + out_bias)
    hidden = normalize(inputs + branch, first_gain, first_shift)
    pre_act = low_back(matmul_high(low(hidden), up_weight) + up_bias)
    activated = low(jax.nn.gelu(pre_act, approximate=False))
    feed = low_back(matmul_high(activated, down_weight) + down_bias)
    return normalize(hidden + feed, second_gain, second_shift)

def reference(tokens, segments, query_weight, query_bias, key_weight, value_weight, value_bias, out_weight, out_bias, first_gain, first_shift, up_weight, up_bias, down_weight, down_bias, second_gain, second_shift, cotangent):
    params = tuple((item.astype(jnp.float32) for item in (query_weight, query_bias, key_weight, value_weight, value_bias, out_weight, out_bias, first_gain, first_shift, up_weight, up_bias, down_weight, down_bias, second_gain, second_shift)))
    group = max(1, min(ROWS, 4096 // LENGTH))
    groups = ROWS // group
    inputs_all = tokens.astype(jnp.float32).reshape(groups, group, LENGTH, D)
    segs_all = segments.reshape(groups, group, LENGTH)
    incoming_all = cotangent.astype(jnp.float32).reshape(groups, group, LENGTH, D)

    def advance(carry, item):
        inputs_group, segs_group, incoming_group = item
        result, puller = jax.vjp(lambda values_in, params_in: forward(values_in, segs_group, params_in), inputs_group, params)
        input_part, param_part = puller(incoming_group)
        carry = jax.tree.map(lambda total, extra: total + extra, carry, param_part)
        return (carry, (result.astype(jnp.bfloat16), input_part))
    zeros = jax.tree.map(jnp.zeros_like, params)
    totals, (outputs, input_grads) = lax.scan(advance, zeros, (inputs_all, segs_all, incoming_all))
    output = outputs.reshape(ROWS, LENGTH, D)
    input_grad = input_grads.reshape(ROWS, LENGTH, D)
    return (output, input_grad, totals[0], totals[1], totals[2], totals[3], totals[4], totals[5], totals[6], totals[7], totals[8], totals[9], totals[10], totals[11], totals[12], totals[13], totals[14])
```

```python
import functools
import math

import jax
import jax.numpy as jnp
from jax import lax
from jax.experimental import pallas as pl
from jax.experimental.pallas import tpu as pltpu
from jax.sharding import PartitionSpec as P

HEADS = 12
HEAD = 64
PAIR = 2 * HEAD
EPSILON = 1e-06
BLOCKED = -(2.0**100)
VMEM_LIMIT = 60 * 2**20
bf16 = jnp.bfloat16
f32 = jnp.float32


def dot(left, right, over_left, over_right):
    return lax.dot_general(
        left, right, (((over_left,), (over_right,)), ((), ())), preferred_element_type=f32
    )


def attention_forward_kernel(
    block, piece, q_ref, k_ref, v_ref, qmark_ref, kmark_ref, segq_ref, segk_ref,
    ctx_ref, prob_ref, inv_ref, keys, vals, scores,
):
    step = pl.program_id(1)
    lane = lax.broadcasted_iota(jnp.int32, (1, PAIR), 1)
    low = lane < HEAD
    factor = HEAD**-0.5 * math.log2(math.e)

    @pl.when(step == 0)
    def _():
        k, v, mark = k_ref[...], v_ref[...], kmark_ref[...]
        one = jnp.ones_like(v)
        keys[0] = jnp.where(low, k, mark)
        keys[1] = jnp.where(low, mark, k)
        vals[0] = jnp.where(low, v, one)
        vals[1] = jnp.where(low, one, v)

    q, mark = q_ref[...], qmark_ref[...]
    zero = jnp.zeros_like(q)
    own = (step * block) // piece
    start = pl.multiple_of(own * piece, piece)
    same = segq_ref[...] == segk_ref[0, pl.ds(own, 1), :]
    for h in range(2):
        keep = low if h == 0 else jnp.logical_not(low)
        scores[h] = dot(jnp.where(keep, q, mark), keys[h], 1, 1)
        near = dot(jnp.where(keep, q, zero), keys[h, pl.ds(start, piece), :], 1, 1)
        scores[h, :, pl.ds(start, piece)] = jnp.where(same, near, BLOCKED)
    sums = []
    for h in range(2):
        highest = jnp.max(scores[h], axis=1, keepdims=True) * factor
        prob = jnp.exp2(scores[h] * factor - highest).astype(bf16)
        prob_ref[h] = prob
        sums.append(dot(prob, vals[h], 1, 0))
    total = pltpu.roll(jnp.where(low, sums[1], sums[0]), HEAD, 1)
    inverse = 1.0 / total
    ctx_ref[...] = (jnp.where(low, sums[0], sums[1]) * inverse).astype(bf16)
    inv_ref[...] = inverse


def attention_forward(qkv, qmark, kmark, segq, segk, block=512):
    length, width = qkv.shape[0], qkv.shape[1] // 3
    pairs, piece = width // PAIR, segk.shape[-1]
    row = pl.BlockSpec((block, PAIR), lambda p, b: (b, p))
    return pl.pallas_call(
        functools.partial(attention_forward_kernel, block, piece),
        grid=(pairs, length // block),
        in_specs=[
            row,
            pl.BlockSpec((length, PAIR), lambda p, b: (0, pairs + p)),
            pl.BlockSpec((length, PAIR), lambda p, b: (0, 2 * pairs + p)),
            pl.BlockSpec((block, PAIR), lambda p, b: (b, 0)),
            pl.BlockSpec((length, PAIR), lambda p, b: (0, 0)),
            pl.BlockSpec((block, 1), lambda p, b: (b, 0)),
            pl.BlockSpec((1, length // piece, piece), lambda p, b: (0, 0, 0)),
        ],
        out_specs=[row, pl.BlockSpec((2, block, length), lambda p, b: (p, b, 0)), row],
        out_shape=[
            jax.ShapeDtypeStruct((length, width), bf16),
            jax.ShapeDtypeStruct((width // HEAD, length, length), bf16),
            jax.ShapeDtypeStruct((length, width), f32),
        ],
        scratch_shapes=[
            pltpu.VMEM((2, length, PAIR), bf16),
            pltpu.VMEM((2, length, PAIR), bf16),
            pltpu.VMEM((2, block, length), f32),
        ],
        compiler_params=pltpu.CompilerParams(vmem_limit_bytes=VMEM_LIMIT),
        cost_estimate=pl.CostEstimate(
            flops=16 * length * length * width,
            bytes_accessed=2 * length * length * (width // HEAD),
            transcendentals=length * length * (width // HEAD),
        ),
        name="attention_forward",
    )(qkv, qkv, qkv, qmark, kmark, segq, segk)


def attention_backward_kernel(
    chunk, do_ref, ctx_ref, inv_ref, q_ref, k_ref, v_ref, prob_ref,
    dq_ref, dk_ref, dv_ref, vals, dkeys, dvals,
):
    step, steps = pl.program_id(1), pl.num_programs(1)
    length = k_ref.shape[0]
    lane = lax.broadcasted_iota(jnp.int32, (1, PAIR), 1)
    low = lane < HEAD
    slot = jnp.bitwise_and(lane, HEAD - 1)
    scale = HEAD**-0.5

    @pl.when(step == 0)
    def _():
        v = v_ref[...]
        mark = jnp.broadcast_to((slot < 3).astype(f32), v.shape).astype(bf16)
        vals[0] = jnp.where(low, v, mark)
        vals[1] = jnp.where(low, mark, v)
        dkeys[...] = jnp.zeros_like(dkeys)
        dvals[...] = jnp.zeros_like(dvals)

    grad = (do_ref[...].astype(f32) * inv_ref[...]).astype(bf16)
    product = grad.astype(f32) * ctx_ref[...].astype(f32)
    grad_t, q_t = grad.T, q_ref[...].T
    dqs = []
    for h in range(2):
        keep = low if h == 0 else jnp.logical_not(low)
        inner = jnp.sum(jnp.where(keep, product, 0.0), axis=1, keepdims=True)
        top = inner.astype(bf16).astype(f32)
        mid = (inner - top).astype(bf16).astype(f32)
        rest = inner - top - mid
        mark = jnp.where(slot == 0, -top, jnp.where(slot == 1, -mid, jnp.where(slot == 2, -rest, 0.0)))
        left = jnp.where(keep, grad, mark.astype(bf16))
        part = slice(h * HEAD, (h + 1) * HEAD)
        dq = None
        for j in range(length // chunk):
            cols = slice(j * chunk, (j + 1) * chunk)
            prob = prob_ref[h, :, cols]
            ds = prob * dot(left, vals[h, cols, :], 1, 1).astype(bf16)
            dvals[part, cols] += dot(grad_t[part], prob, 1, 0)
            dkeys[part, cols] += dot(q_t[part], ds, 1, 0)
            term = dot(ds, k_ref[cols, :], 1, 0)
            dq = term if dq is None else dq + term
        dqs.append(dq)
    dq_ref[...] = (jnp.where(low, dqs[0], dqs[1]) * scale).astype(bf16)

    @pl.when(step == steps - 1)
    def _():
        dk_ref[...] = (dkeys[...] * scale).T.astype(bf16)
        dv_ref[...] = dvals[...].T.astype(bf16)


def attention_backward(pair, grad, ctx, inv, qkv, prob, block=512, chunk=512):
    length, width = ctx.shape
    pairs = width // PAIR
    row = pl.BlockSpec((block, PAIR), lambda p, b: (b, pair))
    full = pl.BlockSpec((length, PAIR), lambda p, b: (0, 0))
    shape = jax.ShapeDtypeStruct((length, PAIR), bf16)
    return pl.pallas_call(
        functools.partial(attention_backward_kernel, chunk),
        grid=(1, length // block),
        in_specs=[
            row,
            row,
            row,
            row,
            pl.BlockSpec((length, PAIR), lambda p, b: (0, pairs + pair)),
            pl.BlockSpec((length, PAIR), lambda p, b: (0, 2 * pairs + pair)),
            pl.BlockSpec((2, block, length), lambda p, b: (pair, b, 0)),
        ],
        out_specs=[pl.BlockSpec((block, PAIR), lambda p, b: (b, 0)), full, full],
        out_shape=[shape, shape, shape],
        scratch_shapes=[
            pltpu.VMEM((2, length, PAIR), bf16),
            pltpu.VMEM((PAIR, length), f32),
            pltpu.VMEM((PAIR, length), f32),
        ],
        compiler_params=pltpu.CompilerParams(vmem_limit_bytes=VMEM_LIMIT),
        cost_estimate=pl.CostEstimate(
            flops=32 * length * length * PAIR,
            bytes_accessed=4 * length * length,
            transcendentals=0,
        ),
        name="attention_backward",
    )(grad, ctx, inv, qkv, qkv, qkv, prob)


def norm_stats(values):
    centered = values - jnp.mean(values, axis=-1, keepdims=True)
    inverse = lax.rsqrt(jnp.mean(centered * centered, axis=-1, keepdims=True) + EPSILON)
    return centered * inverse, inverse


def norm_backward(grad, gain, normed, inverse):
    t = grad * gain
    return (
        t - jnp.mean(t, axis=-1, keepdims=True) - normed * jnp.mean(t * normed, axis=-1, keepdims=True)
    ) * inverse


def row_sum(values):
    return jnp.sum(values, axis=0, keepdims=True)


def feed_forward_kernel(
    chunk, ctx_a_ref, ctx_b_ref, tok_ref, cot_ref, wo_ref, wu_ref, wd_ref, bo_ref, g1_ref, s1_ref,
    bu_ref, bd_ref, g2_ref, s2_ref, out_ref, act_ref, slope_ref, r2_ref, feed_ref, n1_ref, hid_ref, inv_ref,
    sums_ref,
):
    @pl.when(pl.program_id(0) == 0)
    def _():
        sums_ref[...] = jnp.zeros_like(sums_ref)

    split = ctx_a_ref.shape[1]
    branch = dot(ctx_a_ref[...], wo_ref[:split], 1, 0)
    if split < wo_ref.shape[0]:
        branch += dot(ctx_b_ref[...], wo_ref[split:], 1, 0)
    n1, inv1 = norm_stats(tok_ref[...].astype(f32) + branch + bo_ref[...])
    hidden = n1 * g1_ref[...] + s1_ref[...]
    low = hidden.astype(bf16)
    n1_ref[...] = n1
    inv_ref[...] = inv1
    hid_ref[...] = low
    total = hidden + bd_ref[...]
    for j in range(wu_ref.shape[1] // chunk):
        cols = slice(j * chunk, (j + 1) * chunk)
        pre = dot(low, wu_ref[:, cols], 1, 0) + bu_ref[:, cols]
        phi = jnp.exp(pre * pre * -0.5) * (1.0 / math.sqrt(2.0 * math.pi))
        cdf = 0.5 + 0.5 * lax.erf(pre * math.sqrt(0.5))
        act = (pre * cdf).astype(bf16)
        act_ref[:, cols] = act
        slope_ref[:, cols] = (cdf + pre * phi).astype(bf16)
        total += dot(act, wd_ref[cols, :], 1, 0)
    n2, inv2 = norm_stats(total)
    out_ref[...] = (n2 * g2_ref[...] + s2_ref[...]).astype(bf16)
    grad = cot_ref[...].astype(f32)
    r2 = norm_backward(grad, g2_ref[...], n2, inv2)
    feed = r2.astype(bf16)
    r2_ref[...] = r2
    feed_ref[...] = feed
    sums_ref[0:1] += row_sum(grad * n2)
    sums_ref[1:2] += row_sum(grad)
    sums_ref[2:3] += row_sum(feed.astype(f32))


def feed_backward_kernel(
    chunk, r2_ref, feed_ref, slope_ref, n1_ref, inv_ref, wo_ref, wu_ref, wd_ref, g1_ref,
    pre_ref, r1_ref, branch_ref, dctx_ref, sums_ref, upsum_ref,
):
    @pl.when(pl.program_id(0) == 0)
    def _():
        sums_ref[...] = jnp.zeros_like(sums_ref)
        upsum_ref[...] = jnp.zeros_like(upsum_ref)

    feed = feed_ref[...]
    grad = r2_ref[...]
    for j in range(wu_ref.shape[1] // chunk):
        cols = slice(j * chunk, (j + 1) * chunk)
        pre = (dot(feed, wd_ref[cols, :], 1, 1) * slope_ref[:, cols].astype(f32)).astype(bf16)
        pre_ref[:, cols] = pre
        upsum_ref[0:1, cols] += row_sum(pre.astype(f32))
        grad += dot(pre, wu_ref[:, cols], 1, 1)
    n1 = n1_ref[...]
    r1 = norm_backward(grad, g1_ref[...], n1, inv_ref[...])
    branch = r1.astype(bf16)
    r1_ref[...] = r1
    branch_ref[...] = branch
    dctx_ref[...] = dot(branch, wo_ref[...], 1, 1).astype(bf16)
    sums_ref[0:1] += row_sum(grad * n1)
    sums_ref[1:2] += row_sum(grad)
    sums_ref[2:3] += row_sum(branch.astype(f32))


def whole(shape):
    return pl.BlockSpec(shape, lambda i: (0,) * len(shape), pipeline_mode=pl.Buffered(1))


def feed_forward(ctx_a, ctx_b, tok, cot, wo, wu, wd, bo, g1, s1, bu, bd, g2, s2, block=256):
    count, width = tok.shape
    hidden = wu.shape[1]
    rows = lambda n: pl.BlockSpec((block, n), lambda i: (i, 0))
    return pl.pallas_call(
        functools.partial(feed_forward_kernel, 768),
        grid=(count // block,),
        in_specs=[rows(ctx_a.shape[1]), rows(ctx_b.shape[1]), rows(width), rows(width)]
        + [whole(x.shape) for x in (wo, wu, wd, bo, g1, s1, bu, bd, g2, s2)],
        out_specs=[rows(width), rows(hidden), rows(hidden), rows(width), rows(width), rows(width), rows(width), rows(1),
                   pl.BlockSpec((8, width), lambda i: (0, 0))],
        out_shape=[
            jax.ShapeDtypeStruct((count, width), bf16),
            jax.ShapeDtypeStruct((count, hidden), bf16),
            jax.ShapeDtypeStruct((count, hidden), bf16),
            jax.ShapeDtypeStruct((count, width), f32),
            jax.ShapeDtypeStruct((count, width), bf16),
            jax.ShapeDtypeStruct((count, width), f32),
            jax.ShapeDtypeStruct((count, width), bf16),
            jax.ShapeDtypeStruct((count, 1), f32),
            jax.ShapeDtypeStruct((8, width), f32),
        ],
        compiler_params=pltpu.CompilerParams(vmem_limit_bytes=VMEM_LIMIT),
        cost_estimate=pl.CostEstimate(
            flops=2 * count * width * (width + 2 * hidden), bytes_accessed=40 * 2**20, transcendentals=2 * count * hidden
        ),
        name="feed_forward",
    )(ctx_a, ctx_b, tok, cot, wo, wu, wd, bo, g1, s1, bu, bd, g2, s2)


def feed_backward(r2, feed, slope, n1, inv, wo, wu, wd, g1, block=256):
    count, width = r2.shape
    hidden = wu.shape[1]
    rows = lambda n: pl.BlockSpec((block, n), lambda i: (i, 0))
    return pl.pallas_call(
        functools.partial(feed_backward_kernel, 768),
        grid=(count // block,),
        in_specs=[rows(width), rows(width), rows(hidden), rows(width), rows(1)]
        + [whole(x.shape) for x in (wo, wu, wd, g1)],
        out_specs=[rows(hidden), rows(width), rows(width), rows(width),
                   pl.BlockSpec((8, width), lambda i: (0, 0)), pl.BlockSpec((8, hidden), lambda i: (0, 0))],
        out_shape=[
            jax.ShapeDtypeStruct((count, hidden), bf16),
            jax.ShapeDtypeStruct((count, width), f32),
            jax.ShapeDtypeStruct((count, width), bf16),
            jax.ShapeDtypeStruct((count, width), bf16),
            jax.ShapeDtypeStruct((8, width), f32),
            jax.ShapeDtypeStruct((8, hidden), f32),
        ],
        compiler_params=pltpu.CompilerParams(vmem_limit_bytes=VMEM_LIMIT),
        cost_estimate=pl.CostEstimate(
            flops=2 * count * width * (width + 2 * hidden), bytes_accessed=40 * 2**20, transcendentals=0
        ),
        name="feed_backward",
    )(r2, feed, slope, n1, inv, wo, wu, wd, g1)


def bit_of(axis, k):
    return lax.bitwise_and(lax.shift_right_logical(lax.axis_index(axis), k), 1)


def swap(values, axis, k, size):
    return lax.ppermute(values, axis, [(i, i ^ (1 << k)) for i in range(size)])


def add_low(left, right):
    return (left.astype(f32) + right.astype(f32)).astype(bf16)


def part_of(values, index, count):
    size = values.shape[0] // count
    return lax.dynamic_slice_in_dim(values, index * size, size, 0)


def scatter_sum(values, halving, whole_sums):
    for axis, k, size in halving:
        bit = bit_of(axis, k)
        got = swap(part_of(values, 1 - bit, 2), axis, k, size)
        values = add_low(part_of(values, bit, 2), got)
    for axis, k, size in whole_sums:
        values = add_low(values, swap(values, axis, k, size))
    return values


def gather_back(values, halving):
    for axis, k, size in reversed(halving):
        first = bit_of(axis, k) == 0
        got = swap(values, axis, k, size)
        values = jnp.concatenate([jnp.where(first, values, got), jnp.where(first, got, values)], axis=0)
    return values


def on_device(
    sizes, tokens, segments, query_weight, query_bias, key_weight, value_weight, value_bias, out_weight, out_bias,
    first_gain, first_shift, up_weight, up_bias, down_weight, down_bias, second_gain, second_shift, cotangent,
):
    row_size, seq_size = sizes
    row_count, pos, width = tokens.shape
    groups = math.gcd(row_count, seq_size)
    subs = seq_size // groups
    if row_count != groups or subs != 2:
        raise ValueError("unsupported split")
    me = lax.axis_index("seq")
    group, sub = me // subs, lax.rem(me, subs)
    length = pos * seq_size
    half = length // 2
    local = width // subs

    def send_rows(values):
        pieces = [lax.dynamic_index_in_dim(values, group, 0, keepdims=False)]
        for s in range(1, groups):
            block = lax.dynamic_index_in_dim(values, lax.rem(group + s, groups), 0, keepdims=False)
            pieces.append(lax.ppermute(block, "seq", [(i, (i + s * subs) % seq_size) for i in range(seq_size)]))
        return pieces

    def return_rows(values):
        pieces = [values[:pos]]
        for s in range(1, groups):
            pieces.append(
                lax.ppermute(values[s * pos : (s + 1) * pos], "seq", [(i, (i - s * subs) % seq_size) for i in range(seq_size)])
            )
        rows = []
        for r in range(groups):
            picked = pieces[0]
            for s in range(1, groups):
                picked = jnp.where(lax.rem(group + s, groups) == r, pieces[s], picked)
            rows.append(picked)
        return jnp.stack(rows)

    def core_swap(values):
        return swap(values, "seq", 0, seq_size)

    token_pieces = send_rows(tokens)
    tok_half = jnp.concatenate(token_pieces, axis=0)
    tok_full = jnp.concatenate(token_pieces + [core_swap(piece) for piece in token_pieces], axis=0)
    cot_half = jnp.concatenate(send_rows(cotangent), axis=0)

    seg_row = lax.dynamic_index_in_dim(segments, group, 0, keepdims=False)
    middle = seg_row[length // 2]
    seg_pieces = []
    for u in range(subs):
        for s in range(groups):
            quarter = lax.rem(group + groups - s, groups) * subs + lax.rem(sub + u, subs)
            seg_pieces.append(lax.dynamic_slice_in_dim(seg_row, quarter * pos, pos, 0))
    seg_k = jnp.stack(seg_pieces)[None]
    seg_q = seg_k.reshape(length, 1)
    outside = jnp.where(seg_q == middle, 0.0, BLOCKED)
    slot = (jnp.arange(PAIR) % HEAD)[None, :]
    q_mark = jnp.where(slot == 0, 1.0, jnp.where(slot == 1, outside, 0.0)).astype(bf16)
    k_mark = jnp.where(slot == 0, outside, jnp.where(slot == 1, 1.0, 0.0)).astype(bf16)

    def columns(weight):
        return lax.dynamic_slice_in_dim(weight, sub * local, local, weight.ndim - 1)

    w_qkv = jnp.concatenate([columns(query_weight), columns(key_weight), columns(value_weight)], axis=1)
    b_qkv = jnp.concatenate([columns(query_bias), jnp.zeros((local,), f32), columns(value_bias)])
    qkv = (jnp.dot(tok_full, w_qkv, preferred_element_type=f32) + b_qkv).astype(bf16)
    ctx, prob, inv = attention_forward(qkv, q_mark, k_mark, seg_q, seg_k)
    ctx_got = core_swap(ctx[half:])
    ctx_own = ctx[:half]
    wo = jnp.roll(out_weight, -sub * local, axis=0)
    line = lambda vec: vec.reshape(1, -1)
    out, act, slope, r2, feed, n1, hid, inv1, sums_two = feed_forward(
        ctx_own, ctx_got, tok_half, cot_half, wo, up_weight, down_weight, line(out_bias), line(first_gain),
        line(first_shift), line(up_bias), line(down_bias), line(second_gain), line(second_shift),
    )
    output = return_rows(out)

    x_bit, y_bit = ("seq", 1, seq_size), ("rows", 0, row_size)
    row_bits = row_size.bit_length() - 1
    z_bits = [("rows", k, row_size) for k in range(1, min(3, row_bits))]
    more = [("rows", k, row_size) for k in range(3, row_bits)]
    x_first, y_first = [x_bit, y_bit] + z_bits, [y_bit, x_bit] + z_bits

    def total_of(values, order):
        return gather_back(scatter_sum(values, order, more), order)

    def over_rows(left, right):
        return dot(left, right, 0, 0).astype(bf16)

    def cols_of(values, index):
        size = values.shape[1] // 2
        return lax.dynamic_slice_in_dim(values, index * size, size, 1)

    def core_sum(make):
        got = core_swap(make(1 - sub))
        return add_low(make(sub), got)

    def both_halves(values):
        got = core_swap(values)
        first = sub == 0
        return jnp.where(first, values, got), jnp.where(first, got, values)

    down = core_sum(lambda i: over_rows(cols_of(act, i), feed))
    down = jnp.concatenate([total_of(down[:, :local], x_first), total_of(down[:, local:], y_first)], axis=1)
    downweight_grad = jnp.concatenate(both_halves(down), axis=0).astype(f32)

    pre, r1, branch, dctx, sums_one, sums_up = feed_backward(r2, feed, slope, n1, inv1, wo, up_weight, down_weight, line(first_gain))
    dctx_got = core_swap(dctx[:, local:])
    grad = jnp.concatenate([dctx[:, :local], dctx_got], axis=0)

    up = core_sum(lambda i: over_rows(hid, cols_of(pre, i)))
    up = jnp.concatenate([total_of(up[:, :width], x_first), total_of(up[:, width:], y_first)], axis=1)
    upweight_grad = jnp.concatenate(both_halves(up), axis=1).astype(f32)

    ctx_both = jnp.concatenate([ctx_own, ctx_got], axis=1)
    outw = core_sum(lambda i: over_rows(ctx_both, cols_of(branch, i)))

    del outw

    def out_half(i):
        rows = over_rows(ctx_both, cols_of(branch, i))
        return jnp.roll(rows, sub * local, axis=0)

    outw = total_of(core_sum(out_half), y_first)
    outweight_grad = jnp.concatenate(both_halves(outw), axis=1).astype(f32)

    grads, dqkv = [], []
    for p in range(local // PAIR):
        dq, dk, dv = attention_backward(p, grad, ctx, inv, qkv, prob)
        dqkv.append((dq, dk, dv))
        wide = jnp.concatenate([dq, dk, dv], axis=1)
        summed = total_of(over_rows(tok_full, wide), x_first if p == 1 else y_first)
        grads.append(both_halves(summed))
    qkv_grads = []
    for i in range(3):
        cols = slice(i * PAIR, (i + 1) * PAIR)
        qkv_grads.append(
            jnp.concatenate([g[0][:, cols] for g in grads] + [g[1][:, cols] for g in grads], axis=1).astype(f32)
        )
    dall = jnp.concatenate([d[i] for i in range(3) for d in dqkv], axis=1)
    share = dot(dall, w_qkv, 1, 1)
    share_got = core_swap(share[half:].astype(bf16))
    in_half = r1 + share[:half] + share_got.astype(f32)
    kept = in_half[:pos]
    pieces = [kept]
    for s in range(1, groups):
        low = in_half[s * pos : (s + 1) * pos].astype(bf16)
        pieces.append(
            lax.ppermute(low, "seq", [(i, (i - s * subs) % seq_size) for i in range(seq_size)]).astype(f32)
        )
    in_rows = []
    for r in range(groups):
        picked = pieces[0]
        for s in range(1, groups):
            picked = jnp.where(lax.rem(group + s, groups) == r, pieces[s], picked)
        in_rows.append(picked)
    input_grad = jnp.stack(in_rows)

    bias_sums = jnp.sum(dall.astype(f32), axis=0)
    place = lambda part: lax.dynamic_update_slice_in_dim(jnp.zeros((width,), f32), part, sub * local, 0)
    small = lax.psum(
        jnp.concatenate(
            [
                sums_two[0], sums_two[1], sums_two[2], sums_one[0], sums_one[1], sums_one[2], sums_up[0],
                place(bias_sums[:local]), place(bias_sums[2 * local :]),
            ]
        ),
        ("rows", "seq"),
    )
    gain_two, shift_two, down_bias_grad, gain_one, shift_one, out_bias_grad = [
        small[i * width : (i + 1) * width] for i in range(6)
    ]
    hidden = up_bias.shape[0]
    up_bias_grad = small[6 * width : 6 * width + hidden]
    query_bias_grad = small[6 * width + hidden : 7 * width + hidden]
    value_bias_grad = small[7 * width + hidden :]
    return (
        output, input_grad, qkv_grads[0], query_bias_grad, qkv_grads[1], qkv_grads[2], value_bias_grad, outweight_grad,
        out_bias_grad, gain_one, shift_one, upweight_grad, up_bias_grad, downweight_grad, down_bias_grad, gain_two, shift_two,
    )


def solution(mesh):
    split = P("rows", "seq", None)
    return jax.shard_map(
        functools.partial(on_device, (mesh.shape["rows"], mesh.shape["seq"])),
        mesh=mesh,
        in_specs=(split, P("rows", None)) + (P(),) * 15 + (split,),
        out_specs=(split, split) + (P(),) * 15,
        check_vma=False,
    )
```

```python
import functools
import math

import jax
import jax.numpy as jnp
from jax import lax
from jax.experimental import pallas as pl
from jax.experimental.pallas import tpu as pltpu
from jax.sharding import PartitionSpec as P

HEAD = 64
PAIR = 2 * HEAD
TRIO = 3 * PAIR
EPSILON = 1e-06
BLOCKED = -(2.0**100)
VMEM_LIMIT = 60 * 2**20
BOTH = ("rows", "seq")
bf16 = jnp.bfloat16
f32 = jnp.float32


def dot(left, right, over_left, over_right):
    return lax.dot_general(
        left, right, (((over_left,), (over_right,)), ((), ())), preferred_element_type=f32
    )


def shape_of(rows, cols, kind):
    return jax.ShapeDtypeStruct((rows, cols), kind)


def params():
    return pltpu.CompilerParams(vmem_limit_bytes=VMEM_LIMIT)


def tie(values, *others):
    return lax.optimization_barrier((values, others))[0]


def piece_specs(block, pieces):
    each = pieces[0].shape[0] // block
    return [
        pl.BlockSpec((block, x.shape[1]), lambda i, s=s: (jnp.clip(i - s * each, 0, each - 1), 0))
        for s, x in enumerate(pieces)
    ]


def pick(index, refs):
    value = refs[0][...]
    for s in range(1, len(refs)):
        value = jnp.where(index == s, refs[s][...], value)
    return value


def gather_columns_kernel(place_ref, q_ref, k_ref, v_ref, qb_ref, vb_ref, w_ref, b_ref):
    width = w_ref.shape[1] // 3
    for p in range(width // PAIR):
        source = pl.ds(pl.multiple_of(place_ref[0] * width + p * PAIR, PAIR), PAIR)
        for i, (weight, bias) in enumerate(((q_ref, qb_ref), (k_ref, None), (v_ref, vb_ref))):
            target = slice(p * TRIO + i * PAIR, p * TRIO + (i + 1) * PAIR)
            w_ref[:, target] = weight[:, source]
            b_ref[:, target] = jnp.zeros((1, PAIR), f32) if bias is None else bias[:, source]


def gather_columns(sub, wq, wk, wv, bq, bv, local):
    full = lambda x: pl.BlockSpec(x.shape, lambda i, ref: (0, 0))
    width = wq.shape[0]
    return pl.pallas_call(
        gather_columns_kernel,
        grid_spec=pltpu.PrefetchScalarGridSpec(
            num_scalar_prefetch=1,
            grid=(1,),
            in_specs=[full(x) for x in (wq, wk, wv, bq, bv)],
            out_specs=[
                pl.BlockSpec((width, 3 * local), lambda i, ref: (0, 0)),
                pl.BlockSpec((1, 3 * local), lambda i, ref: (0, 0)),
            ],
        ),
        out_shape=[shape_of(width, 3 * local, bf16), shape_of(1, 3 * local, f32)],
        compiler_params=params(),
        cost_estimate=pl.CostEstimate(flops=0, bytes_accessed=0, transcendentals=0),
        name="gather_columns",
    )(sub.reshape(1).astype(jnp.int32), wq, wk, wv, bq, bv)


def attention_forward_kernel(count, block, piece, *refs):
    tokens = refs[:count]
    (w_ref, b_ref, qmark_ref, kmark_ref, segq_ref, segk_ref, ctx_a_ref, ctx_b_ref, prob_ref, inv_ref, qkv_ref,
     keys, vals, scores_a, scores_b) = refs[count:]
    step = pl.program_id(1)
    lane = lax.broadcasted_iota(jnp.int32, (1, PAIR), 1)
    low = lane < HEAD
    factor = HEAD**-0.5 * math.log2(math.e)

    @pl.when(step == 0)
    def _():
        for s in range(count):
            rows = slice(s * piece, (s + 1) * piece)
            made = (dot(tokens[s][...], w_ref[...], 1, 0) + b_ref[...]).astype(bf16)
            qkv_ref[rows] = made
            k, v, mark = made[:, PAIR : 2 * PAIR], made[:, 2 * PAIR :], kmark_ref[rows]
            one = jnp.ones_like(v)
            keys[0, rows] = jnp.where(low, k, mark)
            keys[1, rows] = jnp.where(low, mark, k)
            vals[0, rows] = jnp.where(low, v, one)
            vals[1, rows] = jnp.where(low, one, v)

    def body(own):
        rows = slice(own * block, (own + 1) * block)
        q, mark = qkv_ref[rows, :PAIR], qmark_ref[...]
        zero = jnp.zeros_like(q)
        piece_of = own * block // piece
        near = slice(piece_of * piece, (piece_of + 1) * piece)
        same = segq_ref[...] == segk_ref[piece_of : piece_of + 1, :]
        spans = [x for x in (slice(0, near.start), slice(near.stop, count * piece)) if x.stop > x.start]
        for h, scores in enumerate((scores_a, scores_b)):
            keep = low if h == 0 else jnp.logical_not(low)
            left = jnp.where(keep, q, mark)
            for span in spans:
                scores[:, span] = dot(left, keys[h, span, :], 1, 1)
            scores[:, near] = jnp.where(same, dot(jnp.where(keep, q, zero), keys[h, near, :], 1, 1), BLOCKED)
        sums = []
        for h, scores in enumerate((scores_a, scores_b)):
            highest = jnp.max(scores[...], axis=1, keepdims=True) * factor
            prob = jnp.exp2(scores[...] * factor - highest).astype(bf16)
            prob_ref[h] = prob
            sums.append(dot(prob, vals[h], 1, 0))
        total = pltpu.roll(jnp.where(low, sums[1], sums[0]), HEAD, 1)
        inverse = 1.0 / total
        inv_ref[...] = inverse
        ctx = ctx_a_ref if 2 * own * block < count * piece else ctx_b_ref
        ctx[...] = (jnp.where(low, sums[0], sums[1]) * inverse).astype(bf16)

    for own in range(count * piece // block):
        pl.when(step == own)(functools.partial(body, own))


def half_specs(block, steps, column):
    near = lambda p, b: (jnp.minimum(b, steps // 2 - 1), column(p))
    far = lambda p, b: (jnp.maximum(b - steps // 2, 0), column(p))
    return [pl.BlockSpec((block, PAIR), near), pl.BlockSpec((block, PAIR), far)]


def attention_forward(tokens, w_qkv, b_qkv, qmark, kmark, segq, segk, block=512):
    piece, width = tokens[0].shape
    length, local = piece * len(tokens), w_qkv.shape[1] // 3
    pairs, steps = local // PAIR, length // block
    once = pl.Buffered(1)
    return pl.pallas_call(
        functools.partial(attention_forward_kernel, len(tokens), block, piece),
        grid=(pairs, steps),
        in_specs=[pl.BlockSpec((piece, width), lambda p, b: (0, 0), pipeline_mode=once) for _ in tokens]
        + [
            pl.BlockSpec((width, TRIO), lambda p, b: (0, p)),
            pl.BlockSpec((1, TRIO), lambda p, b: (0, p)),
            pl.BlockSpec((block, PAIR), lambda p, b: (b, 0)),
            pl.BlockSpec((length, PAIR), lambda p, b: (0, 0), pipeline_mode=once),
            pl.BlockSpec((block, 1), lambda p, b: (b, 0)),
            pl.BlockSpec((length // piece, piece), lambda p, b: (0, 0)),
        ],
        out_specs=half_specs(block, steps, lambda p: p)
        + [
            pl.BlockSpec((2, block, length), lambda p, b: (p, b, 0)),
            pl.BlockSpec((block, PAIR), lambda p, b: (b, p)),
            pl.BlockSpec((length, TRIO), lambda p, b: (0, p)),
        ],
        out_shape=[
            shape_of(length // 2, local, bf16),
            shape_of(length // 2, local, bf16),
            jax.ShapeDtypeStruct((local // HEAD, length, length), bf16),
            shape_of(length, local, f32),
            shape_of(length, 3 * local, bf16),
        ],
        scratch_shapes=[
            pltpu.VMEM((2, length, PAIR), bf16),
            pltpu.VMEM((2, length, PAIR), bf16),
            pltpu.VMEM((block, length), f32),
            pltpu.VMEM((block, length), f32),
        ],
        compiler_params=params(),
        cost_estimate=pl.CostEstimate(flops=0, bytes_accessed=0, transcendentals=0),
        name="attention_forward",
    )(*tokens, w_qkv, b_qkv, qmark, kmark, segq, segk)


def attention_backward_kernel(
    chunk, grad_a_ref, grad_b_ref, ctx_a_ref, ctx_b_ref, inv_ref, qkv_ref, prob_ref, *rest
):
    dqkv_ref, sums_ref, vals, dkeys, dvals = rest[-5:]
    step, steps = pl.program_id(0), pl.num_programs(0)
    length = qkv_ref.shape[0]
    block = grad_a_ref.shape[0]
    lane = lax.broadcasted_iota(jnp.int32, (1, PAIR), 1)
    low = lane < HEAD
    slot = jnp.bitwise_and(lane, HEAD - 1)
    scale = HEAD**-0.5

    @pl.when(step == 0)
    def _():
        v = qkv_ref[:, 2 * PAIR :]
        mark = jnp.broadcast_to((slot < 3).astype(f32), v.shape).astype(bf16)
        vals[0] = jnp.where(low, v, mark)
        vals[1] = jnp.where(low, mark, v)
        dkeys[...] = jnp.zeros_like(dkeys)
        dvals[...] = jnp.zeros_like(dvals)
        sums_ref[...] = jnp.zeros_like(sums_ref)

    near = step < steps // 2
    incoming = jnp.where(near, grad_a_ref[...], grad_b_ref[...])
    ctx = jnp.where(near, ctx_a_ref[...], ctx_b_ref[...])
    rows = pl.ds(pl.multiple_of(step * block, block), block)
    grad = (incoming.astype(f32) * inv_ref[...]).astype(bf16)
    product = grad.astype(f32) * ctx.astype(f32)
    grad_t, q_t = grad.T, qkv_ref[rows, :PAIR].T
    dqs = []
    for h in range(2):
        keep = low if h == 0 else jnp.logical_not(low)
        inner = jnp.sum(jnp.where(keep, product, 0.0), axis=1, keepdims=True)
        top = inner.astype(bf16).astype(f32)
        mid = (inner - top).astype(bf16).astype(f32)
        last = inner - top - mid
        mark = jnp.where(slot == 0, -top, jnp.where(slot == 1, -mid, jnp.where(slot == 2, -last, 0.0)))
        left = jnp.where(keep, grad, mark.astype(bf16))
        part = slice(h * HEAD, (h + 1) * HEAD)
        dq = None
        for j in range(length // chunk):
            cols = slice(j * chunk, (j + 1) * chunk)
            prob = prob_ref[h, :, cols]
            ds = prob * dot(left, vals[h, cols, :], 1, 1).astype(bf16)
            dvals[part, cols] += dot(grad_t[part], prob, 1, 0)
            dkeys[part, cols] += dot(q_t[part], ds, 1, 0)
            term = dot(ds, qkv_ref[cols, PAIR : 2 * PAIR], 1, 0)
            dq = term if dq is None else dq + term
        dqs.append(dq)
    dq = (jnp.where(low, dqs[0], dqs[1]) * scale).astype(bf16)
    dqkv_ref[rows, :PAIR] = dq
    sums_ref[0:1, :PAIR] += jnp.sum(dq.astype(f32), axis=0, keepdims=True)

    @pl.when(step == steps - 1)
    def _():
        dqkv_ref[:, PAIR : 2 * PAIR] = (dkeys[...] * scale).T.astype(bf16)
        dv = dvals[...].T.astype(bf16)
        dqkv_ref[:, 2 * PAIR :] = dv
        sums_ref[0:1, 2 * PAIR :] = jnp.sum(dv.astype(f32), axis=0, keepdims=True)


def attention_backward(pair, grads, ctxs, inv, qkv, prob, before, block=512, chunk=512):
    length = qkv.shape[0]
    steps = length // block
    halves = [pl.BlockSpec(s.block_shape, lambda b, s=s: s.index_map(pair, b)) for s in half_specs(block, steps, lambda p: p)]
    return pl.pallas_call(
        functools.partial(attention_backward_kernel, chunk),
        grid=(steps,),
        in_specs=halves
        + halves
        + [
            pl.BlockSpec((block, PAIR), lambda b: (b, pair)),
            pl.BlockSpec((length, TRIO), lambda b: (0, pair)),
            pl.BlockSpec((2, block, length), lambda b: (pair, b, 0)),
        ]
        + [pl.BlockSpec(memory_space=pl.ANY)] * len(before),
        out_specs=[pl.BlockSpec((length, TRIO), lambda b: (0, pair)), pl.BlockSpec((8, TRIO), lambda b: (0, 0))],
        out_shape=[shape_of(length, qkv.shape[1], bf16), shape_of(8, TRIO, f32)],
        scratch_shapes=[
            pltpu.VMEM((2, length, PAIR), bf16),
            pltpu.VMEM((PAIR, length), f32),
            pltpu.VMEM((PAIR, length), f32),
        ],
        input_output_aliases={7: 0} if before else {},
        compiler_params=params(),
        cost_estimate=pl.CostEstimate(flops=0, bytes_accessed=0, transcendentals=0),
        name="attention_backward",
    )(*grads, *ctxs, inv, qkv, prob, *before)


def norm_stats(values):
    centered = values - jnp.mean(values, axis=-1, keepdims=True)
    inverse = lax.rsqrt(jnp.mean(centered * centered, axis=-1, keepdims=True) + EPSILON)
    return centered * inverse, inverse


def norm_backward(grad, gain, normed, inverse):
    t = grad * gain
    return (
        t - jnp.mean(t, axis=-1, keepdims=True) - normed * jnp.mean(t * normed, axis=-1, keepdims=True)
    ) * inverse


def row_sum(values):
    return jnp.sum(values, axis=0, keepdims=True)


def normal(u):
    return 0.5 + 0.5 * lax.erf(u * math.sqrt(0.5)), jnp.exp(u * u * -0.5) * (1.0 / math.sqrt(2.0 * math.pi))


def feed_forward_kernel(count, chunk, *refs):
    toks, cots = refs[:count], refs[count : 2 * count]
    (ctx_a_ref, ctx_b_ref, wo_ref, wu_ref, wd_ref, vec_ref, bu_ref) = refs[2 * count : 2 * count + 7]
    outs = refs[2 * count + 7 : 3 * count + 7]
    act_ref, slope_ref, r2_ref, feed_ref, n1_ref, hid_ref, inv_ref, sums_ref = refs[3 * count + 7 :]
    step, steps = pl.program_id(0), pl.num_programs(0)
    index = step // (steps // count)

    @pl.when(step == 0)
    def _():
        sums_ref[...] = jnp.zeros_like(sums_ref)

    bo, g1, s1, bd, g2, s2 = [vec_ref[i : i + 1] for i in range(6)]
    split = ctx_a_ref.shape[1]
    branch = dot(ctx_a_ref[...], wo_ref[:split], 1, 0) + dot(ctx_b_ref[...], wo_ref[split:], 1, 0)
    n1, inv1 = norm_stats(pick(index, toks).astype(f32) + branch + bo)
    hidden = n1 * g1 + s1
    low = hidden.astype(bf16)
    n1_ref[...] = n1
    inv_ref[...] = inv1
    hid_ref[...] = low
    total = hidden + bd
    for j in range(wu_ref.shape[1] // chunk):
        cols = slice(j * chunk, (j + 1) * chunk)
        pre = dot(low, wu_ref[:, cols], 1, 0) + bu_ref[:, cols]
        cdf, phi = normal(pre)
        act = (pre * cdf).astype(bf16)
        act_ref[:, cols] = act
        slope_ref[:, cols] = (cdf + pre * phi).astype(bf16)
        total += dot(act, wd_ref[cols, :], 1, 0)
    n2, inv2 = norm_stats(total)
    result = (n2 * g2 + s2).astype(bf16)
    for s in range(count):

        @pl.when(index == s)
        def _(s=s):
            outs[s][...] = result

    grad = pick(index, cots).astype(f32)
    r2 = norm_backward(grad, g2, n2, inv2)
    feed = r2.astype(bf16)
    r2_ref[...] = r2
    feed_ref[...] = feed
    sums_ref[0:1] += row_sum(grad * n2)
    sums_ref[1:2] += row_sum(grad)
    sums_ref[2:3] += row_sum(feed.astype(f32))


def feed_backward_kernel(
    chunk, r2_ref, feed_ref, slope_ref, n1_ref, inv_ref, wo_ref, wu_ref, wd_ref, vec_ref,
    pre_ref, r1_ref, branch_ref, dctx_a_ref, dctx_b_ref, sums_ref, upsum_ref,
):
    @pl.when(pl.program_id(0) == 0)
    def _():
        sums_ref[...] = jnp.zeros_like(sums_ref)
        upsum_ref[...] = jnp.zeros_like(upsum_ref)

    feed = feed_ref[...]
    grad = r2_ref[...]
    for j in range(wu_ref.shape[1] // chunk):
        cols = slice(j * chunk, (j + 1) * chunk)
        pre = (dot(feed, wd_ref[cols, :], 1, 1) * slope_ref[:, cols].astype(f32)).astype(bf16)
        pre_ref[:, cols] = pre
        upsum_ref[0:1, cols] += row_sum(pre.astype(f32))
        grad += dot(pre, wu_ref[:, cols], 1, 1)
    n1 = n1_ref[...]
    r1 = norm_backward(grad, vec_ref[1:2], n1, inv_ref[...])
    branch = r1.astype(bf16)
    r1_ref[...] = r1
    branch_ref[...] = branch
    split = dctx_a_ref.shape[1]
    dctx_a_ref[...] = dot(branch, wo_ref[:split], 1, 1).astype(bf16)
    dctx_b_ref[...] = dot(branch, wo_ref[split:], 1, 1).astype(bf16)
    sums_ref[0:1] += row_sum(grad * n1)
    sums_ref[1:2] += row_sum(grad)
    sums_ref[2:3] += row_sum(branch.astype(f32))


def whole(values):
    return pl.BlockSpec(values.shape, lambda i: (0,) * values.ndim, pipeline_mode=pl.Buffered(1))


def row_blocks(block, *widths):
    return [pl.BlockSpec((block, n), lambda i: (i, 0)) for n in widths]


def feed_forward(toks, cots, ctx_a, ctx_b, wo, wu, wd, vec, bu, block=256):
    width, hidden = wu.shape
    count = ctx_a.shape[0]
    outs = [shape_of(x.shape[0], width, bf16) for x in toks]
    total = pl.BlockSpec((8, width), lambda i: (0, 0))
    return pl.pallas_call(
        functools.partial(feed_forward_kernel, len(toks), 768),
        grid=(count // block,),
        in_specs=piece_specs(block, toks)
        + piece_specs(block, cots)
        + row_blocks(block, ctx_a.shape[1], ctx_b.shape[1])
        + [whole(x) for x in (wo, wu, wd, vec, bu)],
        out_specs=piece_specs(block, outs) + row_blocks(block, hidden, hidden, width, width, width, width, 1) + [total],
        out_shape=outs
        + [
            shape_of(count, hidden, bf16),
            shape_of(count, hidden, bf16),
            shape_of(count, width, f32),
            shape_of(count, width, bf16),
            shape_of(count, width, f32),
            shape_of(count, width, bf16),
            shape_of(count, 1, f32),
            shape_of(8, width, f32),
        ],
        compiler_params=params(),
        cost_estimate=pl.CostEstimate(flops=0, bytes_accessed=0, transcendentals=0),
        name="feed_forward",
    )(*toks, *cots, ctx_a, ctx_b, wo, wu, wd, vec, bu)


def feed_backward(r2, feed, slope, n1, inv, wo, wu, wd, vec, local, block=256):
    count, width = r2.shape
    hidden = wu.shape[1]
    return pl.pallas_call(
        functools.partial(feed_backward_kernel, 768),
        grid=(count // block,),
        in_specs=row_blocks(block, width, width, hidden, width, 1) + [whole(x) for x in (wo, wu, wd, vec)],
        out_specs=row_blocks(block, hidden, width, width, local, width - local)
        + [pl.BlockSpec((8, width), lambda i: (0, 0)), pl.BlockSpec((8, hidden), lambda i: (0, 0))],
        out_shape=[
            shape_of(count, hidden, bf16),
            shape_of(count, width, f32),
            shape_of(count, width, bf16),
            shape_of(count, local, bf16),
            shape_of(count, width - local, bf16),
            shape_of(8, width, f32),
            shape_of(8, hidden, f32),
        ],
        compiler_params=params(),
        cost_estimate=pl.CostEstimate(flops=0, bytes_accessed=0, transcendentals=0),
        name="feed_backward",
    )(r2, feed, slope, n1, inv, wo, wu, wd, vec)


def assemble_kernel(cuts, place_ref, *refs):
    count = (len(refs) - len(cuts)) // 2
    own, got, outs = refs[:count], refs[count : 2 * count], refs[2 * count :]
    low = jnp.bitwise_and(jnp.where(pl.program_id(0) == place_ref[0], place_ref[1], place_ref[2]), 3)
    size = own[0].shape[0] // 4

    def write(sources):
        for t in range(4):
            start = pl.multiple_of(jnp.bitwise_xor(low, t) * size, 16)
            for out, pieces in zip(outs, cuts, strict=True):
                for which, source, target, width in pieces:
                    out[t * size : (t + 1) * size, target : target + width] = sources[which][
                        pl.ds(start, size), source : source + width
                    ].astype(f32)

    @pl.when(pl.program_id(0) == place_ref[0])
    def _():
        write(own)

    @pl.when(pl.program_id(0) != place_ref[0])
    def _():
        write(got)


def assemble(place, own, got, cuts, by_rows):
    rows = own[0].shape[0]
    quarter = rows // 4
    mine = lambda h, j, ref: (jnp.where(h == ref[0], jnp.bitwise_xor(j, ref[1] // 4), 0), 0)
    other = lambda h, j, ref: (jnp.where(h == ref[0], 0, jnp.bitwise_xor(j, ref[2] // 4)), 0)
    outs, specs = [], []
    for pieces in cuts:
        width = sum(piece[-1] for piece in pieces)
        if by_rows:
            outs.append(shape_of(2 * rows, width, f32))
            specs.append(pl.BlockSpec((quarter, width), lambda h, j, ref: (4 * h + j, 0)))
        else:
            outs.append(shape_of(rows, 2 * width, f32))
            specs.append(pl.BlockSpec((quarter, width), lambda h, j, ref: (j, h)))
    return pl.pallas_call(
        functools.partial(assemble_kernel, cuts),
        grid_spec=pltpu.PrefetchScalarGridSpec(
            num_scalar_prefetch=1,
            grid=(2, 4),
            in_specs=[pl.BlockSpec((quarter, x.shape[1]), mine) for x in own]
            + [pl.BlockSpec((quarter, x.shape[1]), other) for x in got],
            out_specs=specs,
        ),
        out_shape=outs,
        compiler_params=params(),
        cost_estimate=pl.CostEstimate(flops=0, bytes_accessed=0, transcendentals=0),
        name="assemble",
    )(place, *own, *got)


def cut(values, index, axis=0):
    size = values.shape[axis] // 2
    return lax.dynamic_slice_in_dim(values, index * size, size, axis)


def total_of(terms):
    value = terms[0].astype(f32)
    for term in terms[1:]:
        value += term.astype(f32)
    return value.astype(bf16)


class Exchange:
    def __init__(self, row_size, seq_size):
        seq_bits, row_bits = seq_size.bit_length() - 1, row_size.bit_length() - 1
        x, rows = list(range(1, seq_bits)), list(range(seq_bits, seq_bits + row_bits))
        first = (rows[:2] + x + rows[2:])[:4]
        second = [first[1], first[0]] + first[2:]
        self.orders = (first, second)
        self.rest = (rows[:2] + x + rows[2:])[4:]
        self.size = row_size * seq_size
        self.token = None
        self.phases = len(first)
        here = lax.axis_index("rows") * seq_size + lax.axis_index("seq")
        self.core = jnp.bitwise_and(here, 1)
        bit = lambda k: jnp.bitwise_and(lax.shift_right_logical(here, k), 1)
        self.bits = [jnp.where(self.core == 0, bit(a), bit(b)) for a, b in zip(first, second)]
        places = []
        for order in self.orders:
            place = 0
            for k in order:
                place = 2 * place + bit(k)
            places.append(place)
        own = jnp.where(self.core == 0, places[0], places[1])
        other = jnp.where(self.core == 0, places[1], places[0])
        self.place = jnp.stack([self.core, own, other]).astype(jnp.int32)

    def send(self, values, phase):
        pairs = [(d, d ^ (1 << self.orders[d & 1][phase])) for d in range(self.size)]
        return lax.ppermute(values, BOTH, pairs)

    def after(self, values):
        return values if self.token is None else tie(values, self.token)

    def start(self, phase, *terms):
        bit = self.bits[phase]
        terms = self.after(terms)
        out = self.token = total_of([cut(x, 1 - bit) for x in terms])
        keep = total_of([cut(x, bit) for x in terms])
        return keep, self.send(out, phase)

    def finish(self, *terms):
        value = total_of(terms)
        for k in self.rest:
            value = total_of([value, lax.ppermute(value, BOTH, [(d, d ^ (1 << k)) for d in range(self.size)])])
        return value

    def widen(self, values, phase):
        values = self.token = self.after(values)
        return jnp.concatenate([values, self.send(values, phase)], axis=0)

    def other_core(self, values):
        values = self.token = self.after(values)
        return lax.ppermute(values, BOTH, [(d, d ^ 1) for d in range(self.size)])


def on_device(
    sizes, tokens, segments, query_weight, query_bias, key_weight, value_weight, value_bias, out_weight, out_bias,
    first_gain, first_shift, up_weight, up_bias, down_weight, down_bias, second_gain, second_shift, cotangent,
):
    row_size, seq_size = sizes
    row_count, pos, width = tokens.shape
    groups = math.gcd(row_count, seq_size)
    subs = seq_size // groups
    if row_count != groups or subs != 2:
        raise ValueError("unsupported split")
    me = lax.axis_index("seq")
    group, sub = me // subs, lax.rem(me, subs)
    length = pos * seq_size
    half = length // 2
    local = width // subs
    pairs = local // PAIR
    exchange = Exchange(row_size, seq_size)

    def shifted(values, s):
        return lax.ppermute(values, "seq", [(i, (i + s * subs) % seq_size) for i in range(seq_size)])

    def cut_rows(values):
        return [lax.dynamic_index_in_dim(values, lax.rem(group + s, groups), 0, keepdims=False) for s in range(groups)]

    def trade(blocks):
        return blocks[:1] + [shifted(x, s) for s, x in enumerate(blocks[1:], 1)]

    def place_rows(pieces):
        rows = []
        for r in range(groups):
            picked = pieces[0]
            for s in range(1, groups):
                picked = jnp.where(lax.rem(group + s, groups) == r, pieces[s], picked)
            rows.append(picked)
        return jnp.stack(rows)

    def core_swap(values):
        return lax.ppermute(values, "seq", [(i, i ^ 1) for i in range(seq_size)])

    tok_blocks = cut_rows(tokens)
    toks = trade(tok_blocks)
    late_group, late = tie((group, sub), tok_blocks[1:])
    cot_blocks = [lax.dynamic_index_in_dim(cotangent, lax.rem(late_group + s, groups), 0, keepdims=False) for s in range(groups)]

    seg_row = lax.dynamic_index_in_dim(segments, late_group, 0, keepdims=False)
    middle = seg_row[length // 2]
    seg_pieces = []
    for u in range(subs):
        for s in range(groups):
            quarter = lax.rem(late_group + groups - s, groups) * subs + lax.rem(late + u, subs)
            seg_pieces.append(lax.dynamic_slice_in_dim(seg_row, quarter * pos, pos, 0))
    seg_k = jnp.stack(seg_pieces)
    seg_q = seg_k.reshape(length, 1)
    outside = jnp.where(seg_q == middle, 0.0, BLOCKED)
    slot = (jnp.arange(PAIR) % HEAD)[None, :]
    q_mark = jnp.where(slot == 0, 1.0, jnp.where(slot == 1, outside, 0.0)).astype(bf16)
    k_mark = jnp.where(slot == 0, outside, jnp.where(slot == 1, 1.0, 0.0)).astype(bf16)

    w_qkv, b_qkv = gather_columns(
        late, query_weight, key_weight, value_weight, query_bias.reshape(1, -1), value_bias.reshape(1, -1), local
    )
    wo = jnp.concatenate([lax.dynamic_slice_in_dim(out_weight, i * local, local, 0) for i in (late, 1 - late)], axis=0)
    vec = jnp.stack([out_bias, first_gain, first_shift, down_bias, second_gain, second_shift, second_shift, second_shift])
    bu = up_bias.reshape(1, -1)

    prepared = (wo, vec, bu, w_qkv, b_qkv, q_mark, k_mark, seg_q, seg_k, cot_blocks)
    far = [core_swap(toks[0])] + [core_swap(tie(x, prepared)) for x in toks[1:]]
    toks_all = toks + far
    ctx_a, ctx_b, prob, inv, qkv = attention_forward(toks_all, w_qkv, b_qkv, q_mark, k_mark, seg_q, seg_k)
    cots = trade(cot_blocks)
    tok_full = jnp.concatenate(toks_all, axis=0)
    ctx_got = core_swap(ctx_b)
    made = feed_forward(toks, cots, ctx_a, ctx_got, wo, up_weight, down_weight, vec, bu)
    outs, (act, slope, r2, feed, n1, hid, inv1, sums_two) = made[:groups], made[groups:]

    def over_rows(left, right):
        return dot(left, right, 0, 0).astype(bf16)

    whole_down = over_rows(act, feed)
    down_got = exchange.other_core(cut(whole_down, 1 - sub))
    down = exchange.start(0, cut(whole_down, sub), down_got)
    r2, feed = exchange.after((r2, feed))
    pre, r1, branch, dctx_a, dctx_b, sums_one, sums_up = feed_backward(
        r2, feed, slope, n1, inv1, wo, up_weight, down_weight, vec, local
    )
    down = exchange.start(1, *tie(down, pre))
    grads = (dctx_a, exchange.other_core(dctx_b))

    ctx_both = jnp.concatenate([jnp.where(sub == 0, ctx_a, ctx_got), jnp.where(sub == 0, ctx_got, ctx_a)], axis=1)
    sums = jnp.concatenate([sums_two[:3], sums_one[:3], sums_up[0].reshape(-1, width)], axis=0)
    vectors = sums.shape[0]
    sums = jnp.pad(sums.T.astype(bf16), ((0, 0), (0, vectors % 2)))
    each = sums.shape[1] // 2
    whole_up, whole_out = over_rows(exchange.after(hid), pre), over_rows(ctx_both, branch)

    def up_out(index):
        extra = jnp.pad(cut(sums, index, 1), ((0, 0), (0, PAIR - each)))
        return jnp.concatenate([cut(whole_up, index, 1), cut(whole_out, index, 1), extra], axis=1)

    up_got = exchange.other_core(up_out(1 - sub))
    down = exchange.start(2, *down)
    up = exchange.start(0, up_out(sub), up_got)
    dqkv, biases = (), []
    out_back = []
    for p in range(pairs):
        made, bias = attention_backward(p, exchange.after(grads), (ctx_a, ctx_b), inv, qkv, prob, dqkv)
        dqkv = (made,)
        biases.append(bias[0])
        if p == 0:
            down = exchange.start(3, *tie(down, made))
            up = exchange.start(1, *tie(up, made))
            out_sent = exchange.token = exchange.after(outs[1:])
            out_back = [shifted(x, -s) for s, x in enumerate(out_sent, 1)]
        elif p == 1:
            output = place_rows([outs[0]] + tie(out_back, made))
            down = exchange.widen(exchange.finish(*tie(down, made)), 3)
            up = exchange.start(2, *tie(up, output))
    output = output if out_back else outs[0][None]
    dqkv = dqkv[0]

    bias_q = jnp.concatenate([b[:PAIR] for b in biases])
    bias_v = jnp.concatenate([b[2 * PAIR :] for b in biases])
    bias_col = jnp.pad(jnp.concatenate([bias_q, bias_v]).astype(bf16)[:, None], ((0, 0), (0, PAIR - 1)))
    three = exchange.start(0, jnp.concatenate([over_rows(tok_full, dqkv), bias_col], axis=1))
    up = exchange.start(3, *up)
    down = exchange.widen(down, 2)
    dqkv_now, w_now = exchange.after((dqkv, w_qkv))
    share_got = exchange.other_core(dot(dqkv_now[half:], w_now, 1, 1).astype(bf16))
    three = exchange.start(1, *three)
    dqkv_now, w_now, share_got = exchange.after((dqkv, w_qkv, share_got))
    in_half = r1 + dot(dqkv_now[:half], w_now, 1, 1) + share_got.astype(f32)
    exchange.token = in_sent = [in_half[s * pos : (s + 1) * pos].astype(bf16) for s in range(1, groups)]
    in_sent = [shifted(x, -s) for s, x in enumerate(in_sent, 1)]
    up = exchange.widen(exchange.finish(*exchange.after(up)), 3)
    down = exchange.widen(down, 1)
    three = exchange.start(2, *three)
    up = exchange.widen(up, 2)
    three = exchange.start(3, *three)
    down = exchange.widen(down, 0)
    exchange.token = in_back = exchange.after(in_sent)
    input_grad = place_rows([in_half[:pos]] + [x.astype(f32) for x in in_back])
    up = exchange.widen(up, 1)
    three = exchange.widen(exchange.finish(*exchange.after(three)), 3)
    up = exchange.widen(up, 0)
    three = exchange.widen(three, 2)
    down_got = exchange.other_core(down)
    three = exchange.widen(three, 1)
    up_got = exchange.other_core(up)
    three = exchange.widen(three, 0)
    (downweight_grad,) = assemble(exchange.place, [exchange.after(down)], [down_got], [[(0, 0, 0, width)]], True)
    three_got = exchange.other_core(tie(three, downweight_grad))
    hidden = up_bias.shape[0]
    upweight_grad, outweight_grad, vector_grads = assemble(
        exchange.place,
        [exchange.after(up)],
        [up_got],
        [[(0, 0, 0, hidden // 2)], [(0, hidden // 2, 0, local)], [(0, hidden // 2 + local, 0, PAIR)]],
        False,
    )
    three_got = tie(three_got, upweight_grad)
    cuts = [[(0, p * TRIO + i * PAIR, p * PAIR, PAIR) for p in range(pairs)] for i in range(3)]
    queryweight_grad, keyweight_grad, valueweight_grad, bias_out = assemble(
        exchange.place, [three], [three_got], cuts + [[(0, 3 * local, 0, PAIR)]], False
    )
    bias_out = bias_out.reshape(2, local, 2, PAIR)[:, :, :, 0]
    query_bias_grad = bias_out[0].T.reshape(width)
    value_bias_grad = bias_out[1].T.reshape(width)

    small = jnp.concatenate([vector_grads[:, :each], vector_grads[:, PAIR : PAIR + each]], axis=1).T
    return (
        output, input_grad, queryweight_grad, query_bias_grad, keyweight_grad, valueweight_grad, value_bias_grad,
        outweight_grad, small[5], small[3], small[4], upweight_grad, small[6:vectors].reshape(-1),
        downweight_grad, small[2], small[0], small[1],
    )


def solution(mesh):
    split = P("rows", "seq", None)
    return jax.shard_map(
        functools.partial(on_device, (mesh.shape["rows"], mesh.shape["seq"])),
        mesh=mesh,
        in_specs=(split, P("rows", None)) + (P(),) * 15 + (split,),
        out_specs=(split, split) + (P(),) * 15,
        check_vma=False,
    )
```

```python
import functools
import math

import jax
import jax.numpy as jnp
from jax import lax
from jax.experimental import pallas as pl
from jax.experimental.pallas import tpu as pltpu
from jax.sharding import PartitionSpec as P

HEAD = 64
PAIR = 2 * HEAD
TRIO = 3 * PAIR
EPSILON = 1e-06
BLOCKED = -(2.0**100)
VMEM_LIMIT = 60 * 2**20
BOTH = ("rows", "seq")
bf16 = jnp.bfloat16
f32 = jnp.float32


def dot(left, right, over_left, over_right):
    return lax.dot_general(
        left, right, (((over_left,), (over_right,)), ((), ())), preferred_element_type=f32
    )


def shape_of(rows, cols, kind):
    return jax.ShapeDtypeStruct((rows, cols), kind)


def params():
    return pltpu.CompilerParams(vmem_limit_bytes=VMEM_LIMIT)


def tie(values, *others):
    return lax.optimization_barrier((values, others))[0]


def piece_specs(block, pieces):
    each = pieces[0].shape[0] // block
    return [
        pl.BlockSpec((block, x.shape[1]), lambda i, _, s=s: (jnp.clip(i - s * each, 0, each - 1), 0))
        for s, x in enumerate(pieces)
    ]


def pick(index, refs):
    value = refs[0][...]
    for s in range(1, len(refs)):
        value = jnp.where(index == s, refs[s][...], value)
    return value


def gather_columns_kernel(place_ref, q_ref, k_ref, v_ref, qb_ref, vb_ref, w_ref, b_ref):
    width = w_ref.shape[1] // 3
    for p in range(width // PAIR):
        source = pl.ds(pl.multiple_of(place_ref[0] * width + p * PAIR, PAIR), PAIR)
        for i, (weight, bias) in enumerate(((q_ref, qb_ref), (k_ref, None), (v_ref, vb_ref))):
            target = slice(p * TRIO + i * PAIR, p * TRIO + (i + 1) * PAIR)
            w_ref[:, target] = weight[:, source]
            b_ref[:, target] = jnp.zeros((1, PAIR), f32) if bias is None else bias[:, source]


def gather_columns(sub, wq, wk, wv, bq, bv, local):
    full = lambda x: pl.BlockSpec(x.shape, lambda i, ref: (0, 0))
    width = wq.shape[0]
    return pl.pallas_call(
        gather_columns_kernel,
        grid_spec=pltpu.PrefetchScalarGridSpec(
            num_scalar_prefetch=1,
            grid=(1,),
            in_specs=[full(x) for x in (wq, wk, wv, bq, bv)],
            out_specs=[
                pl.BlockSpec((width, 3 * local), lambda i, ref: (0, 0)),
                pl.BlockSpec((1, 3 * local), lambda i, ref: (0, 0)),
            ],
        ),
        out_shape=[shape_of(width, 3 * local, bf16), shape_of(1, 3 * local, f32)],
        compiler_params=params(),
        cost_estimate=pl.CostEstimate(flops=0, bytes_accessed=0, transcendentals=0),
        name="gather_columns",
    )(sub.reshape(1).astype(jnp.int32), wq, wk, wv, bq, bv)


def attention_forward_kernel(count, block, piece, *refs):
    tokens = refs[:count]
    (w_ref, b_ref, qmark_ref, kmark_ref, segq_ref, segk_ref, ctx_a_ref, ctx_b_ref, prob_ref, inv_ref, qkv_ref,
     keys, vals, scores_a, scores_b) = refs[count:]
    step = pl.program_id(1)
    lane = lax.broadcasted_iota(jnp.int32, (1, PAIR), 1)
    low = lane < HEAD
    factor = HEAD**-0.5 * math.log2(math.e)

    @pl.when(step == 0)
    def _():
        for s in range(count):
            rows = slice(s * piece, (s + 1) * piece)
            made = (dot(tokens[s][...], w_ref[...], 1, 0) + b_ref[...]).astype(bf16)
            qkv_ref[rows] = made
            k, v, mark = made[:, PAIR : 2 * PAIR], made[:, 2 * PAIR :], kmark_ref[rows]
            one = jnp.ones_like(v)
            keys[0, rows] = jnp.where(low, k, mark)
            keys[1, rows] = jnp.where(low, mark, k)
            vals[0, rows] = jnp.where(low, v, one)
            vals[1, rows] = jnp.where(low, one, v)

    def body(own):
        rows = slice(own * block, (own + 1) * block)
        q, mark = qkv_ref[rows, :PAIR], qmark_ref[...]
        zero = jnp.zeros_like(q)
        piece_of = own * block // piece
        near = slice(piece_of * piece, (piece_of + 1) * piece)
        same = segq_ref[...] == segk_ref[piece_of : piece_of + 1, :]
        spans = [x for x in (slice(0, near.start), slice(near.stop, count * piece)) if x.stop > x.start]
        for h, scores in enumerate((scores_a, scores_b)):
            keep = low if h == 0 else jnp.logical_not(low)
            left = jnp.where(keep, q, mark)
            for span in spans:
                scores[:, span] = dot(left, keys[h, span, :], 1, 1)
            scores[:, near] = jnp.where(same, dot(jnp.where(keep, q, zero), keys[h, near, :], 1, 1), BLOCKED)
        sums = []
        for h, scores in enumerate((scores_a, scores_b)):
            highest = jnp.max(scores[...], axis=1, keepdims=True) * factor
            prob = jnp.exp2(scores[...] * factor - highest).astype(bf16)
            prob_ref[h] = prob
            sums.append(dot(prob, vals[h], 1, 0))
        total = pltpu.roll(jnp.where(low, sums[1], sums[0]), HEAD, 1)
        inverse = 1.0 / total
        inv_ref[...] = inverse
        ctx = ctx_a_ref if 2 * own * block < count * piece else ctx_b_ref
        ctx[...] = (jnp.where(low, sums[0], sums[1]) * inverse).astype(bf16)

    for own in range(count * piece // block):
        pl.when(step == own)(functools.partial(body, own))


def half_specs(block, steps, column):
    near = lambda p, b: (jnp.minimum(b, steps // 2 - 1), column(p))
    far = lambda p, b: (jnp.maximum(b - steps // 2, 0), column(p))
    return [pl.BlockSpec((block, PAIR), near), pl.BlockSpec((block, PAIR), far)]


def attention_forward(tokens, w_qkv, b_qkv, qmark, kmark, segq, segk, block=512):
    piece, width = tokens[0].shape
    length, local = piece * len(tokens), w_qkv.shape[1] // 3
    pairs, steps = local // PAIR, length // block
    once = pl.Buffered(1)
    return pl.pallas_call(
        functools.partial(attention_forward_kernel, len(tokens), block, piece),
        grid=(pairs, steps),
        in_specs=[pl.BlockSpec((piece, width), lambda p, b: (0, 0), pipeline_mode=once) for _ in tokens]
        + [
            pl.BlockSpec((width, TRIO), lambda p, b: (0, p)),
            pl.BlockSpec((1, TRIO), lambda p, b: (0, p)),
            pl.BlockSpec((block, PAIR), lambda p, b: (b, 0)),
            pl.BlockSpec((length, PAIR), lambda p, b: (0, 0), pipeline_mode=once),
            pl.BlockSpec((block, 1), lambda p, b: (b, 0)),
            pl.BlockSpec((length // piece, piece), lambda p, b: (0, 0)),
        ],
        out_specs=half_specs(block, steps, lambda p: p)
        + [
            pl.BlockSpec((2, block, length), lambda p, b: (p, b, 0)),
            pl.BlockSpec((block, PAIR), lambda p, b: (b, p)),
            pl.BlockSpec((length, TRIO), lambda p, b: (0, p)),
        ],
        out_shape=[
            shape_of(length // 2, local, bf16),
            shape_of(length // 2, local, bf16),
            jax.ShapeDtypeStruct((local // HEAD, length, length), bf16),
            shape_of(length, local, f32),
            shape_of(length, 3 * local, bf16),
        ],
        scratch_shapes=[
            pltpu.VMEM((2, length, PAIR), bf16),
            pltpu.VMEM((2, length, PAIR), bf16),
            pltpu.VMEM((block, length), f32),
            pltpu.VMEM((block, length), f32),
        ],
        compiler_params=params(),
        cost_estimate=pl.CostEstimate(flops=0, bytes_accessed=0, transcendentals=0),
        name="attention_forward",
    )(*tokens, w_qkv, b_qkv, qmark, kmark, segq, segk)


def attention_backward_kernel(
    chunk, grad_a_ref, grad_b_ref, ctx_a_ref, ctx_b_ref, inv_ref, qkv_ref, prob_ref, *rest
):
    dqkv_ref, sums_ref, vals, dkeys, dvals = rest[-5:]
    step, steps = pl.program_id(0), pl.num_programs(0)
    length = qkv_ref.shape[0]
    block = grad_a_ref.shape[0]
    lane = lax.broadcasted_iota(jnp.int32, (1, PAIR), 1)
    low = lane < HEAD
    slot = jnp.bitwise_and(lane, HEAD - 1)
    scale = HEAD**-0.5

    @pl.when(step == 0)
    def _():
        v = qkv_ref[:, 2 * PAIR :]
        mark = jnp.broadcast_to((slot < 3).astype(f32), v.shape).astype(bf16)
        vals[0] = jnp.where(low, v, mark)
        vals[1] = jnp.where(low, mark, v)
        dkeys[...] = jnp.zeros_like(dkeys)
        dvals[...] = jnp.zeros_like(dvals)
        sums_ref[...] = jnp.zeros_like(sums_ref)

    near = step < steps // 2
    incoming = jnp.where(near, grad_a_ref[...], grad_b_ref[...])
    ctx = jnp.where(near, ctx_a_ref[...], ctx_b_ref[...])
    rows = pl.ds(pl.multiple_of(step * block, block), block)
    grad = (incoming.astype(f32) * inv_ref[...]).astype(bf16)
    product = grad.astype(f32) * ctx.astype(f32)
    grad_t, q_t = grad.T, qkv_ref[rows, :PAIR].T
    dqs = []
    for h in range(2):
        keep = low if h == 0 else jnp.logical_not(low)
        inner = jnp.sum(jnp.where(keep, product, 0.0), axis=1, keepdims=True)
        top = inner.astype(bf16).astype(f32)
        mid = (inner - top).astype(bf16).astype(f32)
        last = inner - top - mid
        mark = jnp.where(slot == 0, -top, jnp.where(slot == 1, -mid, jnp.where(slot == 2, -last, 0.0)))
        left = jnp.where(keep, grad, mark.astype(bf16))
        part = slice(h * HEAD, (h + 1) * HEAD)
        dq = None
        for j in range(length // chunk):
            cols = slice(j * chunk, (j + 1) * chunk)
            prob = prob_ref[h, :, cols]
            ds = prob * dot(left, vals[h, cols, :], 1, 1).astype(bf16)
            dvals[part, cols] += dot(grad_t[part], prob, 1, 0)
            dkeys[part, cols] += dot(q_t[part], ds, 1, 0)
            term = dot(ds, qkv_ref[cols, PAIR : 2 * PAIR], 1, 0)
            dq = term if dq is None else dq + term
        dqs.append(dq)
    dq = (jnp.where(low, dqs[0], dqs[1]) * scale).astype(bf16)
    dqkv_ref[rows, :PAIR] = dq
    sums_ref[0:1, :PAIR] += jnp.sum(dq.astype(f32), axis=0, keepdims=True)

    @pl.when(step == steps - 1)
    def _():
        dqkv_ref[:, PAIR : 2 * PAIR] = (dkeys[...] * scale).T.astype(bf16)
        dv = dvals[...].T.astype(bf16)
        dqkv_ref[:, 2 * PAIR :] = dv
        sums_ref[0:1, 2 * PAIR :] = jnp.sum(dv.astype(f32), axis=0, keepdims=True)


def attention_backward(pair, grads, ctxs, inv, qkv, prob, before, block=512, chunk=512):
    length = qkv.shape[0]
    steps = length // block
    halves = [pl.BlockSpec(s.block_shape, lambda b, s=s: s.index_map(pair, b)) for s in half_specs(block, steps, lambda p: p)]
    return pl.pallas_call(
        functools.partial(attention_backward_kernel, chunk),
        grid=(steps,),
        in_specs=halves
        + halves
        + [
            pl.BlockSpec((block, PAIR), lambda b: (b, pair)),
            pl.BlockSpec((length, TRIO), lambda b: (0, pair)),
            pl.BlockSpec((2, block, length), lambda b: (pair, b, 0)),
        ]
        + [pl.BlockSpec(memory_space=pl.ANY)] * len(before),
        out_specs=[pl.BlockSpec((length, TRIO), lambda b: (0, pair)), pl.BlockSpec((8, TRIO), lambda b: (0, 0))],
        out_shape=[shape_of(length, qkv.shape[1], bf16), shape_of(8, TRIO, f32)],
        scratch_shapes=[
            pltpu.VMEM((2, length, PAIR), bf16),
            pltpu.VMEM((PAIR, length), f32),
            pltpu.VMEM((PAIR, length), f32),
        ],
        input_output_aliases={7: 0} if before else {},
        compiler_params=params(),
        cost_estimate=pl.CostEstimate(flops=0, bytes_accessed=0, transcendentals=0),
        name="attention_backward",
    )(*grads, *ctxs, inv, qkv, prob, *before)


def norm_stats(values):
    centered = values - jnp.mean(values, axis=-1, keepdims=True)
    inverse = lax.rsqrt(jnp.mean(centered * centered, axis=-1, keepdims=True) + EPSILON)
    return centered * inverse, inverse


def norm_backward(grad, gain, normed, inverse):
    t = grad * gain
    return (
        t - jnp.mean(t, axis=-1, keepdims=True) - normed * jnp.mean(t * normed, axis=-1, keepdims=True)
    ) * inverse


def row_sum(values):
    return jnp.sum(values, axis=0, keepdims=True)


def normal(u):
    return 0.5 + 0.5 * lax.erf(u * math.sqrt(0.5)), jnp.exp(u * u * -0.5) * (1.0 / math.sqrt(2.0 * math.pi))


def feed_forward_kernel(count, chunk, core_ref, *refs):
    toks, cots = refs[:count], refs[count : 2 * count]
    (ctx_a_ref, ctx_b_ref, wo_ref, wu_ref, wd_ref, vec_ref, bu_ref) = refs[2 * count : 2 * count + 7]
    outs = refs[2 * count + 7 : 3 * count + 7]
    (slope_ref, r2_ref, feed_ref, n1_ref, hid_ref, inv_ref, sums_ref, sent_ref, kept_ref, act, total_down) = refs[3 * count + 7 :]
    step, steps = pl.program_id(0), pl.num_programs(0)
    index = step // (steps // count)

    @pl.when(step == 0)
    def _():
        sums_ref[...] = jnp.zeros_like(sums_ref)
        total_down[...] = jnp.zeros_like(total_down)

    bo, g1, s1, bd, g2, s2 = [vec_ref[i : i + 1] for i in range(6)]
    split = ctx_a_ref.shape[1]
    branch = dot(ctx_a_ref[...], wo_ref[:split], 1, 0) + dot(ctx_b_ref[...], wo_ref[split:], 1, 0)
    n1, inv1 = norm_stats(pick(index, toks).astype(f32) + branch + bo)
    hidden = n1 * g1 + s1
    low = hidden.astype(bf16)
    n1_ref[...] = n1
    inv_ref[...] = inv1
    hid_ref[...] = low
    total = hidden + bd
    slices = [slice(j * chunk, (j + 1) * chunk) for j in range(wu_ref.shape[1] // chunk)]
    for cols in slices:
        pre = dot(low, wu_ref[:, cols], 1, 0) + bu_ref[:, cols]
        cdf, phi = normal(pre)
        part = (pre * cdf).astype(bf16)
        act[:, cols] = part
        slope_ref[:, cols] = (cdf + pre * phi).astype(bf16)
        total += dot(part, wd_ref[cols, :], 1, 0)
    n2, inv2 = norm_stats(total)
    result = (n2 * g2 + s2).astype(bf16)
    for s in range(count):

        @pl.when(index == s)
        def _(s=s):
            outs[s][...] = result

    grad = pick(index, cots).astype(f32)
    r2 = norm_backward(grad, g2, n2, inv2)
    feed = r2.astype(bf16)
    r2_ref[...] = r2
    feed_ref[...] = feed
    sums_ref[0:1] += row_sum(grad * n2)
    sums_ref[1:2] += row_sum(grad)
    sums_ref[2:3] += row_sum(feed.astype(f32))
    for cols in slices:
        total_down[cols] += dot(act[:, cols], feed, 0, 0)

    @pl.when(step == steps - 1)
    def _():
        half = sent_ref.shape[0]
        for ref, place in ((sent_ref, 1 - core_ref[0]), (kept_ref, core_ref[0])):
            ref[...] = total_down[pl.ds(pl.multiple_of(place * half, half), half)].astype(bf16)


def feed_backward_kernel(
    chunk, core_ref, r2_ref, feed_ref, slope_ref, n1_ref, inv_ref, hid_ref, ctx_a_ref, ctx_b_ref, first_sums_ref,
    wo_ref, wu_ref, wd_ref, vec_ref, r1_ref, dctx_a_ref, dctx_b_ref, sent_ref, kept_ref,
    sums, upsum, total_up, total_out,
):
    step, steps = pl.program_id(0), pl.num_programs(0)

    @pl.when(step == 0)
    def _():
        for ref in (sums, upsum, total_up, total_out):
            ref[...] = jnp.zeros_like(ref)

    feed, low = feed_ref[...], hid_ref[...]
    width, hidden = wu_ref.shape
    grad = r2_ref[...]
    for j in range(hidden // chunk):
        cols = slice(j * chunk, (j + 1) * chunk)
        pre = (dot(feed, wd_ref[cols, :], 1, 1) * slope_ref[:, cols].astype(f32)).astype(bf16)
        upsum[0:1, cols] += row_sum(pre.astype(f32))
        grad += dot(pre, wu_ref[:, cols], 1, 1)
        total_up[:, cols] += dot(low, pre, 0, 0)
    n1 = n1_ref[...]
    r1 = norm_backward(grad, vec_ref[1:2], n1, inv_ref[...])
    branch = r1.astype(bf16)
    r1_ref[...] = r1
    split = dctx_a_ref.shape[1]
    dctx_a_ref[...] = dot(branch, wo_ref[:split], 1, 1).astype(bf16)
    dctx_b_ref[...] = dot(branch, wo_ref[split:], 1, 1).astype(bf16)
    total_out[:split] += dot(ctx_a_ref[...], branch, 0, 0)
    total_out[split:] += dot(ctx_b_ref[...], branch, 0, 0)
    sums[0:1] += row_sum(grad * n1)
    sums[1:2] += row_sum(grad)
    sums[2:3] += row_sum(branch.astype(f32))

    @pl.when(step == steps - 1)
    def _():
        core = core_ref[0]
        vectors = [first_sums_ref[i : i + 1] for i in range(3)] + [sums[i : i + 1] for i in range(3)]
        vectors += [upsum[0:1, i * width : (i + 1) * width] for i in range(hidden // width)]
        each = (len(vectors) + 1) // 2
        vectors += [jnp.zeros_like(vectors[0])] * (2 * each - len(vectors))
        blank = jnp.zeros((PAIR - each, width), f32)
        blocks = [jnp.concatenate(vectors[i * each : (i + 1) * each] + [blank], axis=0).T for i in range(2)]
        half = hidden // 2
        for ref, place in ((sent_ref, 1 - core), (kept_ref, core)):
            ref[:, :half] = total_up[:, pl.ds(pl.multiple_of(place * half, PAIR), half)].astype(bf16)
            columns = pl.ds(pl.multiple_of(place * split, PAIR), split)
            for g in range(2):
                rows = pl.ds(pl.multiple_of(jnp.bitwise_xor(core, g) * split, split), split)
                ref[g * split : (g + 1) * split, half : half + split] = total_out[rows, columns].astype(bf16)
            ref[:, half + split :] = jnp.where(place == 0, blocks[0], blocks[1]).astype(bf16)


def whole(values):
    return pl.BlockSpec(values.shape, lambda i, _: (0,) * values.ndim, pipeline_mode=pl.Buffered(1))


def fixed(rows, cols):
    return pl.BlockSpec((rows, cols), lambda i, _: (0, 0))


def row_blocks(block, *widths):
    return [pl.BlockSpec((block, n), lambda i, _: (i, 0)) for n in widths]


def feed_forward(core, toks, cots, ctx_a, ctx_b, wo, wu, wd, vec, bu, block=256):
    width, hidden = wu.shape
    count = ctx_a.shape[0]
    outs = [shape_of(x.shape[0], width, bf16) for x in toks]
    return pl.pallas_call(
        functools.partial(feed_forward_kernel, len(toks), 768),
        grid_spec=pltpu.PrefetchScalarGridSpec(
            num_scalar_prefetch=1,
            grid=(count // block,),
            in_specs=piece_specs(block, toks)
            + piece_specs(block, cots)
            + row_blocks(block, ctx_a.shape[1], ctx_b.shape[1])
            + [whole(x) for x in (wo, wu, wd, vec, bu)],
            out_specs=piece_specs(block, outs)
            + row_blocks(block, hidden, width, width, width, width, 1)
            + [fixed(8, width), fixed(hidden // 2, width), fixed(hidden // 2, width)],
            scratch_shapes=[pltpu.VMEM((block, hidden), bf16), pltpu.VMEM((hidden, width), f32)],
        ),
        out_shape=outs
        + [
            shape_of(count, hidden, bf16),
            shape_of(count, width, f32),
            shape_of(count, width, bf16),
            shape_of(count, width, f32),
            shape_of(count, width, bf16),
            shape_of(count, 1, f32),
            shape_of(8, width, f32),
            shape_of(hidden // 2, width, bf16),
            shape_of(hidden // 2, width, bf16),
        ],
        compiler_params=params(),
        cost_estimate=pl.CostEstimate(flops=0, bytes_accessed=0, transcendentals=0),
        name="feed_forward",
    )(core, *toks, *cots, ctx_a, ctx_b, wo, wu, wd, vec, bu)


def feed_backward(core, r2, feed, slope, n1, inv, hid, ctx_a, ctx_b, first_sums, wo, wu, wd, vec, block=256):
    count, width = r2.shape
    hidden, local = wu.shape[1], ctx_a.shape[1]
    out = hidden // 2 + local + PAIR
    return pl.pallas_call(
        functools.partial(feed_backward_kernel, 768),
        grid_spec=pltpu.PrefetchScalarGridSpec(
            num_scalar_prefetch=1,
            grid=(count // block,),
            in_specs=row_blocks(block, width, width, hidden, width, 1, width, local, local)
            + [whole(x) for x in (first_sums, wo, wu, wd, vec)],
            out_specs=row_blocks(block, width, local, local) + [fixed(width, out), fixed(width, out)],
            scratch_shapes=[
                pltpu.VMEM((8, width), f32),
                pltpu.VMEM((8, hidden), f32),
                pltpu.VMEM((width, hidden), f32),
                pltpu.VMEM((width, width), f32),
            ],
        ),
        out_shape=[
            shape_of(count, width, f32),
            shape_of(count, local, bf16),
            shape_of(count, local, bf16),
            shape_of(width, out, bf16),
            shape_of(width, out, bf16),
        ],
        compiler_params=params(),
        cost_estimate=pl.CostEstimate(flops=0, bytes_accessed=0, transcendentals=0),
        name="feed_backward",
    )(core, r2, feed, slope, n1, inv, hid, ctx_a, ctx_b, first_sums, wo, wu, wd, vec)


def assemble_kernel(cuts, place_ref, *refs):
    count = (len(refs) - len(cuts)) // 2
    own, got, outs = refs[:count], refs[count : 2 * count], refs[2 * count :]
    low = jnp.bitwise_and(jnp.where(pl.program_id(0) == place_ref[0], place_ref[1], place_ref[2]), 3)
    size = own[0].shape[0] // 4

    def write(sources):
        for t in range(4):
            start = pl.multiple_of(jnp.bitwise_xor(low, t) * size, 16)
            for out, pieces in zip(outs, cuts, strict=True):
                for which, source, target, width in pieces:
                    out[t * size : (t + 1) * size, target : target + width] = sources[which][
                        pl.ds(start, size), source : source + width
                    ].astype(f32)

    @pl.when(pl.program_id(0) == place_ref[0])
    def _():
        write(own)

    @pl.when(pl.program_id(0) != place_ref[0])
    def _():
        write(got)


def assemble(place, own, got, cuts, by_rows):
    rows = own[0].shape[0]
    quarter = rows // 4
    mine = lambda h, j, ref: (jnp.where(h == ref[0], jnp.bitwise_xor(j, ref[1] // 4), 0), 0)
    other = lambda h, j, ref: (jnp.where(h == ref[0], 0, jnp.bitwise_xor(j, ref[2] // 4)), 0)
    outs, specs = [], []
    for pieces in cuts:
        width = sum(piece[-1] for piece in pieces)
        if by_rows:
            outs.append(shape_of(2 * rows, width, f32))
            specs.append(pl.BlockSpec((quarter, width), lambda h, j, ref: (4 * h + j, 0)))
        else:
            outs.append(shape_of(rows, 2 * width, f32))
            specs.append(pl.BlockSpec((quarter, width), lambda h, j, ref: (j, h)))
    return pl.pallas_call(
        functools.partial(assemble_kernel, cuts),
        grid_spec=pltpu.PrefetchScalarGridSpec(
            num_scalar_prefetch=1,
            grid=(2, 4),
            in_specs=[pl.BlockSpec((quarter, x.shape[1]), mine) for x in own]
            + [pl.BlockSpec((quarter, x.shape[1]), other) for x in got],
            out_specs=specs,
        ),
        out_shape=outs,
        compiler_params=params(),
        cost_estimate=pl.CostEstimate(flops=0, bytes_accessed=0, transcendentals=0),
        name="assemble",
    )(place, *own, *got)


def cut(values, index, axis=0):
    size = values.shape[axis] // 2
    return lax.dynamic_slice_in_dim(values, index * size, size, axis)


def total_of(terms):
    value = terms[0].astype(f32)
    for term in terms[1:]:
        value += term.astype(f32)
    return value.astype(bf16)


class Exchange:
    def __init__(self, row_size, seq_size, x_second=False):
        seq_bits, row_bits = seq_size.bit_length() - 1, row_size.bit_length() - 1
        x, rows = list(range(1, seq_bits)), list(range(seq_bits, seq_bits + row_bits))
        every = rows[:2] + x + rows[2:]
        first = every[:4]
        second = [first[1], first[0]] + first[2:]
        if x_second:
            first = [first[0], first[2], first[1], first[3]]
            second = [first[2], first[1], first[0], first[3]]
        self.orders = (first, second)
        self.rest = every[4:]
        self.size = row_size * seq_size
        self.phases = len(first)
        here = lax.axis_index("rows") * seq_size + lax.axis_index("seq")
        self.core = jnp.bitwise_and(here, 1)
        bit = lambda k: jnp.bitwise_and(lax.shift_right_logical(here, k), 1)
        self.bits = [jnp.where(self.core == 0, bit(a), bit(b)) for a, b in zip(first, second)]
        places = []
        for order in self.orders:
            place = 0
            for k in order:
                place = 2 * place + bit(k)
            places.append(place)
        own = jnp.where(self.core == 0, places[0], places[1])
        other = jnp.where(self.core == 0, places[1], places[0])
        self.place = jnp.stack([self.core, own, other]).astype(jnp.int32)

    def send(self, values, phase):
        pairs = [(d, d ^ (1 << self.orders[d & 1][phase])) for d in range(self.size)]
        return lax.ppermute(values, BOTH, pairs)

    def halves(self, phase, *terms):
        bit = self.bits[phase]
        return total_of([cut(x, 1 - bit) for x in terms]), total_of([cut(x, bit) for x in terms])

    def finish(self, *terms):
        value = total_of(terms)
        for k in self.rest:
            value = total_of([value, lax.ppermute(value, BOTH, [(d, d ^ (1 << k)) for d in range(self.size)])])
        return value

    def by(self, phase):
        return lambda values: self.send(values, phase)


def step(*operands, work=None, carry=()):
    values = lax.optimization_barrier(tuple(x for x, _ in operands))
    got = [how(x) for x, (_, how) in zip(values, operands)]
    done = None if work is None else work(values)
    return lax.optimization_barrier((tuple(values), tuple(got), done, carry))


def joined(own, got):
    return jnp.concatenate([own, got], axis=0)


def on_device(
    sizes, tokens, segments, query_weight, query_bias, key_weight, value_weight, value_bias, out_weight, out_bias,
    first_gain, first_shift, up_weight, up_bias, down_weight, down_bias, second_gain, second_shift, cotangent,
):
    row_size, seq_size = sizes
    row_count, pos, width = tokens.shape
    groups = math.gcd(row_count, seq_size)
    subs = seq_size // groups
    if row_count != 2 or groups != 2 or subs != 2:
        raise ValueError("unsupported split")
    me = lax.axis_index("seq")
    group, sub = me // subs, lax.rem(me, subs)
    length = pos * seq_size
    half = length // 2
    local = width // subs
    pairs = local // PAIR
    exchange, up_exchange = Exchange(row_size, seq_size), Exchange(row_size, seq_size, True)

    def shifted(values, s):
        return lax.ppermute(values, "seq", [(i, (i + s * subs) % seq_size) for i in range(seq_size)])

    def cut_rows(values):
        return [lax.dynamic_index_in_dim(values, lax.rem(group + s, groups), 0, keepdims=False) for s in range(groups)]

    def trade(blocks):
        return blocks[:1] + [shifted(x, s) for s, x in enumerate(blocks[1:], 1)]

    def place_rows(pieces):
        rows = []
        for r in range(groups):
            picked = pieces[0]
            for s in range(1, groups):
                picked = jnp.where(lax.rem(group + s, groups) == r, pieces[s], picked)
            rows.append(picked)
        return jnp.stack(rows)

    def core_swap(values):
        return lax.ppermute(values, "seq", [(i, i ^ 1) for i in range(seq_size)])

    tok_blocks = cut_rows(tokens)
    trade_back = lambda values: shifted(values, 1)
    toks = trade(tok_blocks)
    late_group, late = tie((group, sub), tok_blocks[1:])
    cot_blocks = [lax.dynamic_index_in_dim(cotangent, lax.rem(late_group + s, groups), 0, keepdims=False) for s in range(groups)]

    seg_row = lax.dynamic_index_in_dim(segments, late_group, 0, keepdims=False)
    middle = seg_row[length // 2]
    seg_pieces = []
    for u in range(subs):
        for s in range(groups):
            quarter = lax.rem(late_group + groups - s, groups) * subs + lax.rem(late + u, subs)
            seg_pieces.append(lax.dynamic_slice_in_dim(seg_row, quarter * pos, pos, 0))
    seg_k = jnp.stack(seg_pieces)
    seg_q = seg_k.reshape(length, 1)
    outside = jnp.where(seg_q == middle, 0.0, BLOCKED)
    slot = (jnp.arange(PAIR) % HEAD)[None, :]
    q_mark = jnp.where(slot == 0, 1.0, jnp.where(slot == 1, outside, 0.0)).astype(bf16)
    k_mark = jnp.where(slot == 0, outside, jnp.where(slot == 1, 1.0, 0.0)).astype(bf16)

    w_qkv, b_qkv = gather_columns(
        late, query_weight, key_weight, value_weight, query_bias.reshape(1, -1), value_bias.reshape(1, -1), local
    )
    wo = jnp.concatenate([lax.dynamic_slice_in_dim(out_weight, i * local, local, 0) for i in (late, 1 - late)], axis=0)
    vec = jnp.stack([out_bias, first_gain, first_shift, down_bias, second_gain, second_shift, second_shift, second_shift])
    bu = up_bias.reshape(1, -1)

    prepared = (wo, vec, bu, w_qkv, b_qkv, q_mark, k_mark, seg_q, seg_k, cot_blocks)
    far = [core_swap(toks[0])] + [core_swap(tie(x, prepared)) for x in toks[1:]]
    toks_all = toks + far
    ctx_a, ctx_b, prob, inv, qkv = attention_forward(toks_all, w_qkv, b_qkv, q_mark, k_mark, seg_q, seg_k)
    cots = trade(cot_blocks)
    tok_full = jnp.concatenate(toks_all, axis=0)
    ctx_got = core_swap(ctx_b)
    core = sub.reshape(1).astype(jnp.int32)
    made = feed_forward(core, toks, cots, ctx_a, ctx_got, wo, up_weight, down_weight, vec, bu)
    outs, (slope, r2, feed, n1, hid, inv1, sums_two, down_sent, down_kept) = made[:groups], made[groups:]
    (_,), (down_got,), _, _ = step((down_sent, core_swap))
    send_down, down = exchange.halves(0, down_kept, down_got)

    def backward(sent):
        r2_now, feed_now = tie((r2, feed), sent)
        return feed_backward(
            core, r2_now, feed_now, slope, n1, inv1, hid, ctx_a, ctx_got, sums_two, wo, up_weight, down_weight, vec
        )

    _, (down_got,), made, down = step((send_down, exchange.by(0)), work=backward, carry=down)
    r1, dctx_a, dctx_b, up_sent, up_kept = made
    send_down, down = exchange.halves(1, down, down_got)
    _, (up_got, dctx_got), _, up_kept = step((up_sent, core_swap), (dctx_b, core_swap), carry=up_kept)
    send_up, up = up_exchange.halves(0, up_kept, up_got)
    grads, ctxs = (dctx_a, dctx_got), (ctx_a, ctx_b)
    dqkv, biases = (), []
    output = None
    for p in range(pairs):

        def work(sent, p=p, dqkv=dqkv):
            held = grads if p != 1 else tie(grads, output)
            return attention_backward(p, tie(held, sent), ctxs, inv, qkv, prob, dqkv)

        operands = [(send_down, exchange.by(p + 1)), (send_up, up_exchange.by(p))] + ([(outs[1], trade_back)] if p == 0 else [])
        _, got, (made, bias), (down, up) = step(*operands, work=work, carry=(down, up))
        if p == 0:
            output = place_rows([outs[0], got[2]])
        dqkv = (made,)
        biases.append(bias[0])
        if p + 2 < exchange.phases:
            send_down, down = exchange.halves(p + 2, down, got[0])
        else:
            down = exchange.finish(down, got[0])
            send_down = down
        send_up, up = up_exchange.halves(p + 1, up, got[1])
    dqkv = dqkv[0]
    bias_q = jnp.concatenate([b[:PAIR] for b in biases])
    bias_v = jnp.concatenate([b[2 * PAIR :] for b in biases])
    bias_col = jnp.pad(jnp.concatenate([bias_q, bias_v]).astype(bf16)[:, None], ((0, 0), (0, PAIR - 1)))
    three = jnp.concatenate([dot(tok_full, dqkv, 0, 0).astype(bf16), bias_col], axis=1)
    send_three, three = exchange.halves(0, three)

    def share_far(sent):
        d, w = tie((dqkv, w_qkv), sent)
        return dot(d[half:], w, 1, 1).astype(bf16)

    _, (got, up_got, down_got), far, (three, up, down) = step(
        (send_three, exchange.by(0)), (send_up, up_exchange.by(3)), (down, exchange.by(3)), work=share_far, carry=(three, up, down)
    )
    send_three, three = exchange.halves(1, three, got)
    up, down = up_exchange.finish(up, up_got), joined(down, down_got)

    def share_near(sent):
        d, w = tie((dqkv, w_qkv), sent)
        return r1 + dot(d[:half], w, 1, 1)

    (_, _, _, far), (got, up_got, down_got, far_got), near, (three, up, down) = step(
        (send_three, exchange.by(1)), (up, up_exchange.by(3)), (down, exchange.by(2)), (far, core_swap), work=share_near, carry=(three, up, down)
    )
    in_half = near + far_got.astype(f32)
    in_sent = in_half[pos:].astype(bf16)
    send_three, three = exchange.halves(2, three, got)
    up, down = joined(up, up_got), joined(down, down_got)
    _, (got, up_got, down_got), _, (three, up, down) = step(
        (send_three, exchange.by(2)), (up, up_exchange.by(2)), (down, exchange.by(1)), carry=(three, up, down)
    )
    send_three, three = exchange.halves(3, three, got)
    up, down = joined(up, up_got), joined(down, down_got)
    _, (got, up_got, down_got), _, (three, up, down) = step(
        (send_three, exchange.by(3)), (up, up_exchange.by(1)), (down, exchange.by(0)), carry=(three, up, down)
    )
    three = exchange.finish(three, got)
    up, down = joined(up, up_got), joined(down, down_got)
    _, (got, up_got, down_got, in_got), _, (three, up, down) = step(
        (three, exchange.by(3)), (up, up_exchange.by(0)), (down, core_swap), (in_sent, trade_back), carry=(three, up, down)
    )
    three, up = joined(three, got), joined(up, up_got)

    def assemble_down(sent):
        made = assemble(exchange.place, [tie(down, sent)], [down_got], [[(0, 0, 0, width)]], True)[0]
        return made, place_rows([tie(in_half, sent)[:pos], in_got.astype(f32)])

    _, (got, up_got), (downweight_grad, input_grad), (three, up) = step(
        (three, exchange.by(2)), (up, core_swap), work=assemble_down, carry=(three, up)
    )
    three = joined(three, got)
    _, (got,), _, three = step((three, exchange.by(1)), carry=three)
    three = joined(three, got)
    hidden = up_bias.shape[0]
    vectors = 6 + hidden // width
    each = (vectors + 1) // 2

    def assemble_up(sent):
        cuts = [[(0, 0, 0, hidden // 2)], [(0, hidden // 2, 0, local)], [(0, hidden // 2 + local, 0, PAIR)]]
        return assemble(up_exchange.place, [tie(up, sent)], [up_got], cuts, False)

    _, (got,), (upweight_grad, outweight_grad, vector_grads), three = step(
        (three, exchange.by(0)), work=assemble_up, carry=three
    )
    three = joined(three, got)
    _, (three_got,), _, three = step((three, core_swap), carry=three)
    cuts = [[(0, p * TRIO + i * PAIR, p * PAIR, PAIR) for p in range(pairs)] for i in range(3)]
    queryweight_grad, keyweight_grad, valueweight_grad, bias_out = assemble(
        exchange.place, [three], [three_got], cuts + [[(0, 3 * local, 0, PAIR)]], False
    )
    bias_out = bias_out.reshape(2, local, 2, PAIR)[:, :, :, 0]
    query_bias_grad = bias_out[0].T.reshape(width)
    value_bias_grad = bias_out[1].T.reshape(width)

    small = jnp.concatenate([vector_grads[:, :each], vector_grads[:, PAIR : PAIR + each]], axis=1).T
    return (
        output, input_grad, queryweight_grad, query_bias_grad, keyweight_grad, valueweight_grad, value_bias_grad,
        outweight_grad, small[5], small[3], small[4], upweight_grad, small[6:vectors].reshape(-1),
        downweight_grad, small[2], small[0], small[1],
    )


def solution(mesh):
    split = P("rows", "seq", None)
    return jax.shard_map(
        functools.partial(on_device, (mesh.shape["rows"], mesh.shape["seq"])),
        mesh=mesh,
        in_specs=(split, P("rows", None)) + (P(),) * 15 + (split,),
        out_specs=(split, split) + (P(),) * 15,
        check_vma=False,
    )
```

```python
import functools
import math

import jax
import jax.numpy as jnp
from jax import lax
from jax.experimental import pallas as pl
from jax.experimental.pallas import tpu as pltpu
from jax.sharding import PartitionSpec as P

HEAD = 64
PAIR = 2 * HEAD
TRIO = 3 * PAIR
EPSILON = 1e-06
BLOCKED = -(2.0**100)
VMEM_LIMIT = 60 * 2**20
BOTH = ("rows", "seq")
bf16 = jnp.bfloat16
f32 = jnp.float32


def dot(left, right, over_left, over_right):
    return lax.dot_general(
        left, right, (((over_left,), (over_right,)), ((), ())), preferred_element_type=f32
    )


def shape_of(rows, cols, kind):
    return jax.ShapeDtypeStruct((rows, cols), kind)


def params():
    return pltpu.CompilerParams(vmem_limit_bytes=VMEM_LIMIT)


def tie(values, *others):
    return lax.optimization_barrier((values, others))[0]


def piece_specs(block, pieces):
    each = pieces[0].shape[0] // block
    return [
        pl.BlockSpec((block, x.shape[1]), lambda i, _, s=s: (jnp.clip(i - s * each, 0, each - 1), 0))
        for s, x in enumerate(pieces)
    ]


def pick(index, refs):
    value = refs[0][...]
    for s in range(1, len(refs)):
        value = jnp.where(index == s, refs[s][...], value)
    return value


def gather_columns_kernel(place_ref, q_ref, k_ref, v_ref, qb_ref, vb_ref, w_ref, b_ref):
    width = w_ref.shape[1] // 3
    for p in range(width // PAIR):
        source = pl.ds(pl.multiple_of(place_ref[0] * width + p * PAIR, PAIR), PAIR)
        for i, (weight, bias) in enumerate(((q_ref, qb_ref), (k_ref, None), (v_ref, vb_ref))):
            target = slice(p * TRIO + i * PAIR, p * TRIO + (i + 1) * PAIR)
            w_ref[:, target] = weight[:, source]
            b_ref[:, target] = jnp.zeros((1, PAIR), f32) if bias is None else bias[:, source]


def gather_columns(sub, wq, wk, wv, bq, bv, local):
    full = lambda x: pl.BlockSpec(x.shape, lambda i, ref: (0, 0))
    width = wq.shape[0]
    return pl.pallas_call(
        gather_columns_kernel,
        grid_spec=pltpu.PrefetchScalarGridSpec(
            num_scalar_prefetch=1,
            grid=(1,),
            in_specs=[full(x) for x in (wq, wk, wv, bq, bv)],
            out_specs=[
                pl.BlockSpec((width, 3 * local), lambda i, ref: (0, 0)),
                pl.BlockSpec((1, 3 * local), lambda i, ref: (0, 0)),
            ],
        ),
        out_shape=[shape_of(width, 3 * local, bf16), shape_of(1, 3 * local, f32)],
        compiler_params=params(),
        cost_estimate=pl.CostEstimate(flops=0, bytes_accessed=0, transcendentals=0),
        name="gather_columns",
    )(sub.reshape(1).astype(jnp.int32), wq, wk, wv, bq, bv)


def attention_forward_kernel(count, block, piece, *refs):
    tokens = refs[:count]
    (w_ref, b_ref, qmark_ref, kmark_ref, segq_ref, segk_ref, ctx_a_ref, ctx_b_ref, prob_ref, inv_ref, qkv_ref,
     keys, vals, scores_a, scores_b) = refs[count:]
    step = pl.program_id(1)
    lane = lax.broadcasted_iota(jnp.int32, (1, PAIR), 1)
    low = lane < HEAD
    factor = HEAD**-0.5 * math.log2(math.e)

    @pl.when(step == 0)
    def _():
        for s in range(count):
            rows = slice(s * piece, (s + 1) * piece)
            made = (dot(tokens[s][...], w_ref[...], 1, 0) + b_ref[...]).astype(bf16)
            qkv_ref[rows] = made
            k, v, mark = made[:, PAIR : 2 * PAIR], made[:, 2 * PAIR :], kmark_ref[rows]
            one = jnp.ones_like(v)
            keys[0, rows] = jnp.where(low, k, mark)
            keys[1, rows] = jnp.where(low, mark, k)
            vals[0, rows] = jnp.where(low, v, one)
            vals[1, rows] = jnp.where(low, one, v)

    def body(own):
        rows = slice(own * block, (own + 1) * block)
        q, mark = qkv_ref[rows, :PAIR], qmark_ref[...]
        zero = jnp.zeros_like(q)
        piece_of = own * block // piece
        near = slice(piece_of * piece, (piece_of + 1) * piece)
        same = segq_ref[...] == segk_ref[piece_of : piece_of + 1, :]
        spans = [x for x in (slice(0, near.start), slice(near.stop, count * piece)) if x.stop > x.start]

        def score(h, scores):
            keep = low if h == 0 else jnp.logical_not(low)
            left = jnp.where(keep, q, mark)
            for span in spans:
                scores[:, span] = dot(left, keys[h, span, :], 1, 1)
            scores[:, near] = jnp.where(same, dot(jnp.where(keep, q, zero), keys[h, near, :], 1, 1), BLOCKED)

        def weigh(h, scores):
            chunks = [slice(s * piece, (s + 1) * piece) for s in range(count)]
            highest = functools.reduce(jnp.maximum, [jnp.max(scores[:, c], axis=1, keepdims=True) for c in chunks]) * factor
            total = 0.0
            for c in chunks:
                prob = jnp.exp2(scores[:, c] * factor - highest).astype(bf16)
                prob_ref[h, :, c] = prob
                total += dot(prob, vals[h, c, :], 1, 0)
            return total

        score(0, scores_a)
        score(1, scores_b)
        sums = [weigh(0, scores_a), weigh(1, scores_b)]
        total = pltpu.roll(jnp.where(low, sums[1], sums[0]), HEAD, 1)
        inverse = 1.0 / total
        inv_ref[...] = inverse
        ctx = ctx_a_ref if 2 * own * block < count * piece else ctx_b_ref
        ctx[...] = (jnp.where(low, sums[0], sums[1]) * inverse).astype(bf16)

    for own in range(count * piece // block):
        pl.when(step == own)(functools.partial(body, own))


def half_specs(block, steps, column):
    near = lambda p, b: (jnp.minimum(b, steps // 2 - 1), column(p))
    far = lambda p, b: (jnp.maximum(b - steps // 2, 0), column(p))
    return [pl.BlockSpec((block, PAIR), near), pl.BlockSpec((block, PAIR), far)]


def attention_forward(tokens, w_qkv, b_qkv, qmark, kmark, segq, segk, block=512):
    piece, width = tokens[0].shape
    length, local = piece * len(tokens), w_qkv.shape[1] // 3
    pairs, steps = local // PAIR, length // block
    once = pl.Buffered(1)
    return pl.pallas_call(
        functools.partial(attention_forward_kernel, len(tokens), block, piece),
        grid=(pairs, steps),
        in_specs=[pl.BlockSpec((piece, width), lambda p, b: (0, 0), pipeline_mode=once) for _ in tokens]
        + [
            pl.BlockSpec((width, TRIO), lambda p, b: (0, p)),
            pl.BlockSpec((1, TRIO), lambda p, b: (0, p)),
            pl.BlockSpec((block, PAIR), lambda p, b: (b, 0)),
            pl.BlockSpec((length, PAIR), lambda p, b: (0, 0), pipeline_mode=once),
            pl.BlockSpec((block, 1), lambda p, b: (b, 0)),
            pl.BlockSpec((length // piece, piece), lambda p, b: (0, 0)),
        ],
        out_specs=half_specs(block, steps, lambda p: p)
        + [
            pl.BlockSpec((2, block, length), lambda p, b: (p, b, 0)),
            pl.BlockSpec((block, PAIR), lambda p, b: (b, p)),
            pl.BlockSpec((length, TRIO), lambda p, b: (0, p)),
        ],
        out_shape=[
            shape_of(length // 2, local, bf16),
            shape_of(length // 2, local, bf16),
            jax.ShapeDtypeStruct((local // HEAD, length, length), bf16),
            shape_of(length, local, f32),
            shape_of(length, 3 * local, bf16),
        ],
        scratch_shapes=[
            pltpu.VMEM((2, length, PAIR), bf16),
            pltpu.VMEM((2, length, PAIR), bf16),
            pltpu.VMEM((block, length), f32),
            pltpu.VMEM((block, length), f32),
        ],
        compiler_params=params(),
        cost_estimate=pl.CostEstimate(flops=0, bytes_accessed=0, transcendentals=0),
        name="attention_forward",
    )(*tokens, w_qkv, b_qkv, qmark, kmark, segq, segk)


def attention_backward_kernel(
    chunk, grad_a_ref, grad_b_ref, ctx_a_ref, ctx_b_ref, inv_ref, qkv_ref, prob_ref, *rest
):
    dqkv_ref, sums_ref, vals, dkeys, dvals = rest[-5:]
    step, steps = pl.program_id(0), pl.num_programs(0)
    length = qkv_ref.shape[0]
    block = grad_a_ref.shape[0]
    lane = lax.broadcasted_iota(jnp.int32, (1, PAIR), 1)
    low = lane < HEAD
    slot = jnp.bitwise_and(lane, HEAD - 1)
    scale = HEAD**-0.5

    @pl.when(step == 0)
    def _():
        v = qkv_ref[:, 2 * PAIR :]
        mark = jnp.broadcast_to((slot < 3).astype(f32), v.shape).astype(bf16)
        vals[0] = jnp.where(low, v, mark)
        vals[1] = jnp.where(low, mark, v)
        dkeys[...] = jnp.zeros_like(dkeys)
        dvals[...] = jnp.zeros_like(dvals)
        sums_ref[...] = jnp.zeros_like(sums_ref)

    near = step < steps // 2
    incoming = jnp.where(near, grad_a_ref[...], grad_b_ref[...])
    ctx = jnp.where(near, ctx_a_ref[...], ctx_b_ref[...])
    rows = pl.ds(pl.multiple_of(step * block, block), block)
    grad = (incoming.astype(f32) * inv_ref[...]).astype(bf16)
    product = grad.astype(f32) * ctx.astype(f32)
    grad_t, q_t = grad.T, qkv_ref[rows, :PAIR].T
    dqs = []
    for h in range(2):
        keep = low if h == 0 else jnp.logical_not(low)
        inner = jnp.sum(jnp.where(keep, product, 0.0), axis=1, keepdims=True)
        top = inner.astype(bf16).astype(f32)
        mid = (inner - top).astype(bf16).astype(f32)
        last = inner - top - mid
        mark = jnp.where(slot == 0, -top, jnp.where(slot == 1, -mid, jnp.where(slot == 2, -last, 0.0)))
        left = jnp.where(keep, grad, mark.astype(bf16))
        part = slice(h * HEAD, (h + 1) * HEAD)
        dq = None
        for j in range(length // chunk):
            cols = slice(j * chunk, (j + 1) * chunk)
            prob = prob_ref[h, :, cols]
            ds = prob * dot(left, vals[h, cols, :], 1, 1).astype(bf16)
            dvals[part, cols] += dot(grad_t[part], prob, 1, 0)
            dkeys[part, cols] += dot(q_t[part], ds, 1, 0)
            term = dot(ds, qkv_ref[cols, PAIR : 2 * PAIR], 1, 0)
            dq = term if dq is None else dq + term
        dqs.append(dq)
    dq = (jnp.where(low, dqs[0], dqs[1]) * scale).astype(bf16)
    dqkv_ref[rows, :PAIR] = dq
    sums_ref[0:1, :PAIR] += jnp.sum(dq.astype(f32), axis=0, keepdims=True)

    @pl.when(step == steps - 1)
    def _():
        dqkv_ref[:, PAIR : 2 * PAIR] = (dkeys[...] * scale).T.astype(bf16)
        dv = dvals[...].T.astype(bf16)
        dqkv_ref[:, 2 * PAIR :] = dv
        sums_ref[0:1, 2 * PAIR :] = jnp.sum(dv.astype(f32), axis=0, keepdims=True)


def attention_backward(pair, grads, ctxs, inv, qkv, prob, before, block=256, chunk=2048):
    length = qkv.shape[0]
    steps = length // block
    halves = [pl.BlockSpec(s.block_shape, lambda b, s=s: s.index_map(pair, b)) for s in half_specs(block, steps, lambda p: p)]
    return pl.pallas_call(
        functools.partial(attention_backward_kernel, min(chunk, length)),
        grid=(steps,),
        in_specs=halves
        + halves
        + [
            pl.BlockSpec((block, PAIR), lambda b: (b, pair)),
            pl.BlockSpec((length, TRIO), lambda b: (0, pair)),
            pl.BlockSpec((2, block, length), lambda b: (pair, b, 0)),
        ]
        + [pl.BlockSpec(memory_space=pl.ANY)] * len(before),
        out_specs=[pl.BlockSpec((length, TRIO), lambda b: (0, pair)), pl.BlockSpec((8, TRIO), lambda b: (0, 0))],
        out_shape=[shape_of(length, qkv.shape[1], bf16), shape_of(8, TRIO, f32)],
        scratch_shapes=[
            pltpu.VMEM((2, length, PAIR), bf16),
            pltpu.VMEM((PAIR, length), f32),
            pltpu.VMEM((PAIR, length), f32),
        ],
        input_output_aliases={7: 0} if before else {},
        compiler_params=params(),
        cost_estimate=pl.CostEstimate(flops=0, bytes_accessed=0, transcendentals=0),
        name="attention_backward",
    )(*grads, *ctxs, inv, qkv, prob, *before)


def norm_stats(values):
    centered = values - jnp.mean(values, axis=-1, keepdims=True)
    inverse = lax.rsqrt(jnp.mean(centered * centered, axis=-1, keepdims=True) + EPSILON)
    return centered * inverse, inverse


def norm_backward(grad, gain, normed, inverse):
    t = grad * gain
    return (
        t - jnp.mean(t, axis=-1, keepdims=True) - normed * jnp.mean(t * normed, axis=-1, keepdims=True)
    ) * inverse


def row_sum(values):
    return jnp.sum(values, axis=0, keepdims=True)


def normal(u):
    return 0.5 + 0.5 * lax.erf(u * math.sqrt(0.5)), jnp.exp(u * u * -0.5) * (1.0 / math.sqrt(2.0 * math.pi))


def feed_forward_kernel(count, chunk, core_ref, *refs):
    toks, cots = refs[:count], refs[count : 2 * count]
    (ctx_a_ref, ctx_b_ref, wo_ref, wu_ref, wd_ref, vec_ref, bu_ref) = refs[2 * count : 2 * count + 7]
    outs = refs[2 * count + 7 : 3 * count + 7]
    (slope_ref, r2_ref, feed_ref, n1_ref, hid_ref, inv_ref, sums_ref, sent_ref, kept_ref, act, total_down) = refs[3 * count + 7 :]
    step, steps = pl.program_id(0), pl.num_programs(0)
    index = step // (steps // count)

    @pl.when(step == 0)
    def _():
        sums_ref[...] = jnp.zeros_like(sums_ref)
        total_down[...] = jnp.zeros_like(total_down)

    bo, g1, s1, bd, g2, s2 = [vec_ref[i : i + 1] for i in range(6)]
    split = ctx_a_ref.shape[1]
    branch = dot(ctx_a_ref[...], wo_ref[:split], 1, 0) + dot(ctx_b_ref[...], wo_ref[split:], 1, 0)
    n1, inv1 = norm_stats(pick(index, toks).astype(f32) + branch + bo)
    hidden = n1 * g1 + s1
    low = hidden.astype(bf16)
    n1_ref[...] = n1
    inv_ref[...] = inv1
    hid_ref[...] = low
    total = hidden + bd
    slices = [slice(j * chunk, (j + 1) * chunk) for j in range(wu_ref.shape[1] // chunk)]
    for cols in slices:
        pre = dot(low, wu_ref[:, cols], 1, 0) + bu_ref[:, cols]
        cdf, phi = normal(pre)
        part = (pre * cdf).astype(bf16)
        act[:, cols] = part
        slope_ref[:, cols] = (cdf + pre * phi).astype(bf16)
        total += dot(part, wd_ref[cols, :], 1, 0)
    n2, inv2 = norm_stats(total)
    result = (n2 * g2 + s2).astype(bf16)
    for s in range(count):

        @pl.when(index == s)
        def _(s=s):
            outs[s][...] = result

    grad = pick(index, cots).astype(f32)
    r2 = norm_backward(grad, g2, n2, inv2)
    feed = r2.astype(bf16)
    r2_ref[...] = r2
    feed_ref[...] = feed
    sums_ref[0:1] += row_sum(grad * n2)
    sums_ref[1:2] += row_sum(grad)
    sums_ref[2:3] += row_sum(feed.astype(f32))
    for cols in slices:
        total_down[cols] += dot(act[:, cols], feed, 0, 0)

    @pl.when(step == steps - 1)
    def _():
        half = sent_ref.shape[0]
        for ref, place in ((sent_ref, 1 - core_ref[0]), (kept_ref, core_ref[0])):
            ref[...] = total_down[pl.ds(pl.multiple_of(place * half, half), half)].astype(bf16)


def feed_backward_kernel(
    chunk, core_ref, r2_ref, feed_ref, slope_ref, n1_ref, inv_ref, hid_ref, ctx_a_ref, ctx_b_ref, first_sums_ref,
    wo_ref, wu_ref, wd_ref, vec_ref, r1_ref, dctx_a_ref, dctx_b_ref, sent_ref, kept_ref,
    sums, upsum, total_up, total_out,
):
    step, steps = pl.program_id(0), pl.num_programs(0)

    @pl.when(step == 0)
    def _():
        for ref in (sums, upsum, total_up, total_out):
            ref[...] = jnp.zeros_like(ref)

    feed, low = feed_ref[...], hid_ref[...]
    width, hidden = wu_ref.shape
    grad = r2_ref[...]
    for j in range(hidden // chunk):
        cols = slice(j * chunk, (j + 1) * chunk)
        pre = (dot(feed, wd_ref[cols, :], 1, 1) * slope_ref[:, cols].astype(f32)).astype(bf16)
        upsum[0:1, cols] += row_sum(pre.astype(f32))
        grad += dot(pre, wu_ref[:, cols], 1, 1)
        total_up[:, cols] += dot(low, pre, 0, 0)
    n1 = n1_ref[...]
    r1 = norm_backward(grad, vec_ref[1:2], n1, inv_ref[...])
    branch = r1.astype(bf16)
    r1_ref[...] = r1
    split = dctx_a_ref.shape[1]
    dctx_a_ref[...] = dot(branch, wo_ref[:split], 1, 1).astype(bf16)
    dctx_b_ref[...] = dot(branch, wo_ref[split:], 1, 1).astype(bf16)
    total_out[:split] += dot(ctx_a_ref[...], branch, 0, 0)
    total_out[split:] += dot(ctx_b_ref[...], branch, 0, 0)
    sums[0:1] += row_sum(grad * n1)
    sums[1:2] += row_sum(grad)
    sums[2:3] += row_sum(branch.astype(f32))

    @pl.when(step == steps - 1)
    def _():
        core = core_ref[0]
        vectors = [first_sums_ref[i : i + 1] for i in range(3)] + [sums[i : i + 1] for i in range(3)]
        vectors += [upsum[0:1, i * width : (i + 1) * width] for i in range(hidden // width)]
        each = (len(vectors) + 1) // 2
        vectors += [jnp.zeros_like(vectors[0])] * (2 * each - len(vectors))
        blank = jnp.zeros((PAIR - each, width), f32)
        blocks = [jnp.concatenate(vectors[i * each : (i + 1) * each] + [blank], axis=0).T for i in range(2)]
        half = hidden // 2
        for ref, place in ((sent_ref, 1 - core), (kept_ref, core)):
            ref[:, :half] = total_up[:, pl.ds(pl.multiple_of(place * half, PAIR), half)].astype(bf16)
            columns = pl.ds(pl.multiple_of(place * split, PAIR), split)
            for g in range(2):
                rows = pl.ds(pl.multiple_of(jnp.bitwise_xor(core, g) * split, split), split)
                ref[g * split : (g + 1) * split, half : half + split] = total_out[rows, columns].astype(bf16)
            ref[:, half + split :] = jnp.where(place == 0, blocks[0], blocks[1]).astype(bf16)


def whole(values):
    return pl.BlockSpec(values.shape, lambda i, _: (0,) * values.ndim, pipeline_mode=pl.Buffered(1))


def fixed(rows, cols):
    return pl.BlockSpec((rows, cols), lambda i, _: (0, 0))


def row_blocks(block, *widths):
    return [pl.BlockSpec((block, n), lambda i, _: (i, 0)) for n in widths]


def feed_forward(core, toks, cots, ctx_a, ctx_b, wo, wu, wd, vec, bu, block=256):
    width, hidden = wu.shape
    count = ctx_a.shape[0]
    outs = [shape_of(x.shape[0], width, bf16) for x in toks]
    return pl.pallas_call(
        functools.partial(feed_forward_kernel, len(toks), 768),
        grid_spec=pltpu.PrefetchScalarGridSpec(
            num_scalar_prefetch=1,
            grid=(count // block,),
            in_specs=piece_specs(block, toks)
            + piece_specs(block, cots)
            + row_blocks(block, ctx_a.shape[1], ctx_b.shape[1])
            + [whole(x) for x in (wo, wu, wd, vec, bu)],
            out_specs=piece_specs(block, outs)
            + row_blocks(block, hidden, width, width, width, width, 1)
            + [fixed(8, width), fixed(hidden // 2, width), fixed(hidden // 2, width)],
            scratch_shapes=[pltpu.VMEM((block, hidden), bf16), pltpu.VMEM((hidden, width), f32)],
        ),
        out_shape=outs
        + [
            shape_of(count, hidden, bf16),
            shape_of(count, width, f32),
            shape_of(count, width, bf16),
            shape_of(count, width, f32),
            shape_of(count, width, bf16),
            shape_of(count, 1, f32),
            shape_of(8, width, f32),
            shape_of(hidden // 2, width, bf16),
            shape_of(hidden // 2, width, bf16),
        ],
        compiler_params=params(),
        cost_estimate=pl.CostEstimate(flops=0, bytes_accessed=0, transcendentals=0),
        name="feed_forward",
    )(core, *toks, *cots, ctx_a, ctx_b, wo, wu, wd, vec, bu)


def feed_backward(core, r2, feed, slope, n1, inv, hid, ctx_a, ctx_b, first_sums, wo, wu, wd, vec, block=256):
    count, width = r2.shape
    hidden, local = wu.shape[1], ctx_a.shape[1]
    out = hidden // 2 + local + PAIR
    return pl.pallas_call(
        functools.partial(feed_backward_kernel, 768),
        grid_spec=pltpu.PrefetchScalarGridSpec(
            num_scalar_prefetch=1,
            grid=(count // block,),
            in_specs=row_blocks(block, width, width, hidden, width, 1, width, local, local)
            + [whole(x) for x in (first_sums, wo, wu, wd, vec)],
            out_specs=row_blocks(block, width, local, local) + [fixed(width, out), fixed(width, out)],
            scratch_shapes=[
                pltpu.VMEM((8, width), f32),
                pltpu.VMEM((8, hidden), f32),
                pltpu.VMEM((width, hidden), f32),
                pltpu.VMEM((width, width), f32),
            ],
        ),
        out_shape=[
            shape_of(count, width, f32),
            shape_of(count, local, bf16),
            shape_of(count, local, bf16),
            shape_of(width, out, bf16),
            shape_of(width, out, bf16),
        ],
        compiler_params=params(),
        cost_estimate=pl.CostEstimate(flops=0, bytes_accessed=0, transcendentals=0),
        name="feed_backward",
    )(core, r2, feed, slope, n1, inv, hid, ctx_a, ctx_b, first_sums, wo, wu, wd, vec)


def assemble_kernel(parts, cuts, place_ref, *refs):
    count = (len(refs) - len(cuts)) // 2
    own, got, outs = refs[:count], refs[count : 2 * count], refs[2 * count :]
    low = jnp.bitwise_and(jnp.where(pl.program_id(0) == place_ref[0], place_ref[1], place_ref[2]), parts - 1)
    size = own[0].shape[0] // parts

    def write(sources):
        for t in range(parts):
            start = pl.multiple_of(jnp.bitwise_xor(low, t) * size, 16)
            for out, pieces in zip(outs, cuts, strict=True):
                for which, source, target, width in pieces:
                    out[t * size : (t + 1) * size, target : target + width] = sources[which][
                        pl.ds(start, size), source : source + width
                    ].astype(f32)

    @pl.when(pl.program_id(0) == place_ref[0])
    def _():
        write(own)

    @pl.when(pl.program_id(0) != place_ref[0])
    def _():
        write(got)


def assemble(place, own, got, cuts, by_rows, blocks=2):
    rows, parts = own[0].shape[0], 8 // blocks
    size = rows // blocks
    mine = lambda h, j, ref: (jnp.where(h == ref[0], jnp.bitwise_xor(j, ref[1] // parts), 0), 0)
    other = lambda h, j, ref: (jnp.where(h == ref[0], 0, jnp.bitwise_xor(j, ref[2] // parts)), 0)
    outs, specs = [], []
    for pieces in cuts:
        width = sum(piece[-1] for piece in pieces)
        if by_rows:
            outs.append(shape_of(2 * rows, width, f32))
            specs.append(pl.BlockSpec((size, width), lambda h, j, ref: (blocks * h + j, 0)))
        else:
            outs.append(shape_of(rows, 2 * width, f32))
            specs.append(pl.BlockSpec((size, width), lambda h, j, ref: (j, h)))
    return pl.pallas_call(
        functools.partial(assemble_kernel, parts, cuts),
        grid_spec=pltpu.PrefetchScalarGridSpec(
            num_scalar_prefetch=1,
            grid=(2, blocks),
            in_specs=[pl.BlockSpec((size, x.shape[1]), mine) for x in own]
            + [pl.BlockSpec((size, x.shape[1]), other) for x in got],
            out_specs=specs,
        ),
        out_shape=outs,
        compiler_params=params(),
        cost_estimate=pl.CostEstimate(flops=0, bytes_accessed=0, transcendentals=0),
        name="assemble",
    )(place, *own, *got)


def cut(values, index, axis=0):
    size = values.shape[axis] // 2
    return lax.dynamic_slice_in_dim(values, index * size, size, axis)


def total_of(terms):
    value = terms[0].astype(f32)
    for term in terms[1:]:
        value += term.astype(f32)
    return value.astype(bf16)


class Exchange:
    def __init__(self, row_size, seq_size, *orders):
        seq_bits, row_bits = seq_size.bit_length() - 1, row_size.bit_length() - 1
        x, rows = list(range(1, seq_bits)), list(range(seq_bits, seq_bits + row_bits))
        every = rows[:2] + x + rows[2:]
        first, second = [[every[i] for i in order] for order in orders]
        self.orders = (first, second)
        self.rest = every[3:]
        self.size = row_size * seq_size
        self.phases = len(first)
        here = lax.axis_index("rows") * seq_size + lax.axis_index("seq")
        self.core = jnp.bitwise_and(here, 1)
        bit = lambda k: jnp.bitwise_and(lax.shift_right_logical(here, k), 1)
        self.bits = [jnp.where(self.core == 0, bit(a), bit(b)) for a, b in zip(first, second)]
        places = []
        for order in self.orders:
            place = 0
            for k in order:
                place = 2 * place + bit(k)
            places.append(place)
        own = jnp.where(self.core == 0, places[0], places[1])
        other = jnp.where(self.core == 0, places[1], places[0])
        self.place = jnp.stack([self.core, own, other]).astype(jnp.int32)

    def send(self, values, phase):
        pairs = [(d, d ^ (1 << self.orders[d & 1][phase])) for d in range(self.size)]
        return lax.ppermute(values, BOTH, pairs)

    def halves(self, phase, *terms):
        bit = self.bits[phase]
        return total_of([cut(x, 1 - bit) for x in terms]), total_of([cut(x, bit) for x in terms])

    def finish(self, *terms):
        value = total_of(terms)
        for k in self.rest[1:]:
            value = total_of([value, self.whole(value, k)])
        return value

    def whole(self, values, k):
        return lax.ppermute(values, BOTH, [(d, d ^ (1 << k)) for d in range(self.size)])

    def by(self, phase):
        if phase == self.phases:
            return lambda values: self.whole(values, self.rest[0])
        return lambda values: self.send(values, phase)


def step(*operands, work=None, carry=()):
    values = lax.optimization_barrier(tuple(x for x, _ in operands))
    got = [how(x) for x, (_, how) in zip(values, operands)]
    done = None if work is None else work(values)
    return lax.optimization_barrier((tuple(values), tuple(got), done, carry))


def joined(own, got):
    return jnp.concatenate([own, got], axis=0)


def on_device(
    sizes, tokens, segments, query_weight, query_bias, key_weight, value_weight, value_bias, out_weight, out_bias,
    first_gain, first_shift, up_weight, up_bias, down_weight, down_bias, second_gain, second_shift, cotangent,
):
    row_size, seq_size = sizes
    row_count, pos, width = tokens.shape
    groups = math.gcd(row_count, seq_size)
    subs = seq_size // groups
    if row_count != 2 or groups != 2 or subs != 2:
        raise ValueError("unsupported split")
    me = lax.axis_index("seq")
    group, sub = me // subs, lax.rem(me, subs)
    length = pos * seq_size
    half = length // 2
    local = width // subs
    pairs = local // PAIR
    exchange = Exchange(row_size, seq_size, (0, 2, 1), (1, 0, 2))
    up_exchange = Exchange(row_size, seq_size, (0, 2, 1), (1, 2, 0))
    three_exchange = Exchange(row_size, seq_size, (0, 1, 2), (2, 0, 1))

    def shifted(values, s):
        return lax.ppermute(values, "seq", [(i, (i + s * subs) % seq_size) for i in range(seq_size)])

    def cut_rows(values):
        return [lax.dynamic_index_in_dim(values, lax.rem(group + s, groups), 0, keepdims=False) for s in range(groups)]

    def trade(blocks):
        return blocks[:1] + [shifted(x, s) for s, x in enumerate(blocks[1:], 1)]

    def place_rows(pieces):
        rows = []
        for r in range(groups):
            picked = pieces[0]
            for s in range(1, groups):
                picked = jnp.where(lax.rem(group + s, groups) == r, pieces[s], picked)
            rows.append(picked)
        return jnp.stack(rows)

    def core_swap(values):
        return lax.ppermute(values, "seq", [(i, i ^ 1) for i in range(seq_size)])

    tok_blocks = cut_rows(tokens)
    trade_back = lambda values: shifted(values, 1)
    toks = trade(tok_blocks)
    late_group, late = tie((group, sub), tok_blocks[1:])
    cot_blocks = [lax.dynamic_index_in_dim(cotangent, lax.rem(late_group + s, groups), 0, keepdims=False) for s in range(groups)]

    seg_row = lax.dynamic_index_in_dim(segments, late_group, 0, keepdims=False)
    middle = seg_row[length // 2]
    seg_pieces = []
    for u in range(subs):
        for s in range(groups):
            quarter = lax.rem(late_group + groups - s, groups) * subs + lax.rem(late + u, subs)
            seg_pieces.append(lax.dynamic_slice_in_dim(seg_row, quarter * pos, pos, 0))
    seg_k = jnp.stack(seg_pieces)
    seg_q = seg_k.reshape(length, 1)
    outside = jnp.where(seg_q == middle, 0.0, BLOCKED)
    slot = (jnp.arange(PAIR) % HEAD)[None, :]
    q_mark = jnp.where(slot == 0, 1.0, jnp.where(slot == 1, outside, 0.0)).astype(bf16)
    k_mark = jnp.where(slot == 0, outside, jnp.where(slot == 1, 1.0, 0.0)).astype(bf16)

    w_qkv, b_qkv = gather_columns(
        late, query_weight, key_weight, value_weight, query_bias.reshape(1, -1), value_bias.reshape(1, -1), local
    )
    wo = jnp.concatenate([lax.dynamic_slice_in_dim(out_weight, i * local, local, 0) for i in (late, 1 - late)], axis=0)
    vec = jnp.stack([out_bias, first_gain, first_shift, down_bias, second_gain, second_shift, second_shift, second_shift])
    bu = up_bias.reshape(1, -1)

    prepared = (wo, vec, bu, w_qkv, b_qkv, q_mark, k_mark, seg_q, seg_k, cot_blocks)
    far = [core_swap(toks[0])] + [core_swap(tie(x, prepared)) for x in toks[1:]]
    toks_all = toks + far
    ctx_a, ctx_b, prob, inv, qkv = attention_forward(toks_all, w_qkv, b_qkv, q_mark, k_mark, seg_q, seg_k)
    cots = trade(cot_blocks)
    tok_full = jnp.concatenate(toks_all, axis=0)
    ctx_got = core_swap(ctx_b)
    core = sub.reshape(1).astype(jnp.int32)
    made = feed_forward(core, toks, cots, ctx_a, ctx_got, wo, up_weight, down_weight, vec, bu)
    outs, (slope, r2, feed, n1, hid, inv1, sums_two, down_sent, down_kept) = made[:groups], made[groups:]

    def backward(sent):
        r2_now, feed_now = tie((r2, feed), sent)
        return feed_backward(
            core, r2_now, feed_now, slope, n1, inv1, hid, ctx_a, ctx_got, sums_two, wo, up_weight, down_weight, vec
        )

    _, (down_got,), made, down_kept = step((down_sent, core_swap), work=backward, carry=down_kept)
    r1, dctx_a, dctx_b, up_sent, up_kept = made
    _, (dctx_got,), (send_down, down), (up_sent, up_kept) = step(
        (dctx_b, core_swap), work=lambda sent: exchange.halves(0, *tie((down_kept, down_got), sent)), carry=(up_sent, up_kept)
    )
    grads, ctxs = (dctx_a, dctx_got), (ctx_a, ctx_b)
    dqkv, biases = (), []
    for p in range(pairs):

        def work(sent, p=p, dqkv=dqkv):
            return attention_backward(p, tie(grads, sent), ctxs, inv, qkv, prob, dqkv)

        operands = [(send_down, exchange.by(p)), (up_sent, core_swap) if p == 0 else (send_up, up_exchange.by(p - 1))]
        operands += [(outs[1], trade_back)] if p == 0 else []
        kept = (down, up_kept) if p == 0 else (down, up)
        _, got, (made, bias), (down, up) = step(*operands, work=work, carry=kept)
        out_got = got[2] if p == 0 else out_got
        dqkv = (made,)
        biases.append(bias[0])
        if p + 1 < exchange.phases:
            send_down, down = exchange.halves(p + 1, down, got[0])
        else:
            send_down = down = total_of([down, got[0]])
        send_up, up = up_exchange.halves(p, up, got[1])
    dqkv = dqkv[0]
    bias_q = jnp.concatenate([b[:PAIR] for b in biases])
    bias_v = jnp.concatenate([b[2 * PAIR :] for b in biases])
    bias_col = jnp.pad(jnp.concatenate([bias_q, bias_v]).astype(bf16)[:, None], ((0, 0), (0, PAIR - 1)))
    three = jnp.concatenate([dot(tok_full, dqkv, 0, 0).astype(bf16), bias_col], axis=1)
    send_three, three = three_exchange.halves(0, three)

    def share_far(sent):
        d, w = tie((dqkv, w_qkv), sent)
        return dot(d[half:], w, 1, 1).astype(bf16)

    _, (got, up_got, down_got), far, (three, up, down) = step(
        (send_three, three_exchange.by(0)), (send_up, up_exchange.by(2)), (send_down, exchange.by(3)), work=share_far,
        carry=(three, up, down),
    )
    send_three, three = three_exchange.halves(1, three, got)
    up, down = total_of([up, up_got]), exchange.finish(down, down_got)

    def share_near(sent):
        d, w = tie((dqkv, w_qkv), sent)
        return r1 + dot(d[:half], w, 1, 1)

    (_, _, _, far), (got, up_got, down_got, far_got), near, (three, up, down) = step(
        (send_three, three_exchange.by(1)), (up, up_exchange.by(3)), (down, exchange.by(2)), (far, core_swap),
        work=share_near, carry=(three, up, down),
    )
    in_half = near + far_got.astype(f32)
    in_sent = in_half[pos:].astype(bf16)
    send_three, three = three_exchange.halves(2, three, got)
    up, down = up_exchange.finish(up, up_got), joined(down, down_got)
    _, (got, up_got, down_got), output, (three, up, down) = step(
        (send_three, three_exchange.by(2)), (up, up_exchange.by(2)), (down, exchange.by(1)),
        work=lambda sent: place_rows([outs[0], tie(out_got, sent)]), carry=(three, up, down),
    )
    three = total_of([three, got])
    up, down = joined(up, up_got), joined(down, down_got)
    _, (got, up_got, down_got), _, (three, up, down) = step(
        (three, three_exchange.by(3)), (up, up_exchange.by(1)), (down, exchange.by(0)), carry=(three, up, down)
    )
    three = three_exchange.finish(three, got)
    up, down = joined(up, up_got), joined(down, down_got)
    _, (got, up_got, down_got, in_got), _, (three, up, down) = step(
        (three, three_exchange.by(2)), (up, up_exchange.by(0)), (down, core_swap), (in_sent, trade_back),
        carry=(three, up, down),
    )
    three, up = joined(three, got), joined(up, up_got)

    def assemble_down(sent):
        return assemble(exchange.place, [tie(down, sent)], [down_got], [[(0, 0, 0, width)]], True)[0]

    _, (got, up_got), downweight_grad, (three, up) = step(
        (three, three_exchange.by(1)), (up, core_swap), work=assemble_down, carry=(three, up)
    )
    three = joined(three, got)
    hidden = up_bias.shape[0]
    vectors = 6 + hidden // width
    each = (vectors + 1) // 2

    def assemble_up(sent):
        cuts = [[(0, 0, 0, hidden // 2)], [(0, hidden // 2, 0, local)], [(0, hidden // 2 + local, 0, PAIR)]]
        made = assemble(up_exchange.place, [tie(up, sent)], [up_got], cuts, False)
        return made, place_rows([in_half[:pos], tie(in_got, sent).astype(f32)])

    _, (got,), ((upweight_grad, outweight_grad, vector_grads), input_grad), three = step(
        (three, three_exchange.by(0)), work=assemble_up, carry=three
    )
    three = joined(three, got)
    _, (three_got,), _, three = step((three, core_swap), carry=three)
    cuts = [[(0, p * TRIO + i * PAIR, p * PAIR, PAIR) for p in range(pairs)] for i in range(3)]
    queryweight_grad, keyweight_grad, valueweight_grad, bias_out = assemble(
        three_exchange.place, [three], [three_got], cuts + [[(0, 3 * local, 0, PAIR)]], False
    )
    bias_out = bias_out.reshape(2, local, 2, PAIR)[:, :, :, 0]
    query_bias_grad = bias_out[0].T.reshape(width)
    value_bias_grad = bias_out[1].T.reshape(width)

    small = jnp.concatenate([vector_grads[:, :each], vector_grads[:, PAIR : PAIR + each]], axis=1).T
    return (
        output, input_grad, queryweight_grad, query_bias_grad, keyweight_grad, valueweight_grad, value_bias_grad,
        outweight_grad, small[5], small[3], small[4], upweight_grad, small[6:vectors].reshape(-1),
        downweight_grad, small[2], small[0], small[1],
    )


def solution(mesh):
    split = P("rows", "seq", None)
    return jax.shard_map(
        functools.partial(on_device, (mesh.shape["rows"], mesh.shape["seq"])),
        mesh=mesh,
        in_specs=(split, P("rows", None)) + (P(),) * 15 + (split,),
        out_specs=(split, split) + (P(),) * 15,
        check_vma=False,
    )
```

```python
import functools
import math

import jax
import jax.numpy as jnp
from jax import lax
from jax.experimental import pallas as pl
from jax.experimental.pallas import tpu as pltpu
from jax.sharding import PartitionSpec as P

HEAD = 64
PAIR = 2 * HEAD
TRIO = 3 * PAIR
EPSILON = 1e-06
BLOCKED = -(2.0**100)
VMEM_LIMIT = 60 * 2**20
BOTH = ("rows", "seq")
bf16 = jnp.bfloat16
f32 = jnp.float32


def dot(left, right, over_left, over_right):
    return lax.dot_general(
        left, right, (((over_left,), (over_right,)), ((), ())), preferred_element_type=f32
    )


def shape_of(rows, cols, kind):
    return jax.ShapeDtypeStruct((rows, cols), kind)


def params():
    return pltpu.CompilerParams(vmem_limit_bytes=VMEM_LIMIT)


def tie(values, *others):
    return lax.optimization_barrier((values, others))[0]


def piece_specs(block, pieces):
    each = pieces[0].shape[0] // block
    return [
        pl.BlockSpec((block, x.shape[1]), lambda i, _, s=s: (jnp.clip(i - s * each, 0, each - 1), 0))
        for s, x in enumerate(pieces)
    ]


def pick(index, refs):
    value = refs[0][...]
    for s in range(1, len(refs)):
        value = jnp.where(index == s, refs[s][...], value)
    return value


def gather_columns_kernel(place_ref, q_ref, k_ref, v_ref, qb_ref, vb_ref, w_ref, b_ref):
    width = w_ref.shape[1] // 3
    for p in range(width // PAIR):
        source = pl.ds(pl.multiple_of(place_ref[0] * width + p * PAIR, PAIR), PAIR)
        for i, (weight, bias) in enumerate(((q_ref, qb_ref), (k_ref, None), (v_ref, vb_ref))):
            target = slice(p * TRIO + i * PAIR, p * TRIO + (i + 1) * PAIR)
            w_ref[:, target] = weight[:, source]
            b_ref[:, target] = jnp.zeros((1, PAIR), f32) if bias is None else bias[:, source]


def gather_columns(sub, wq, wk, wv, bq, bv, local):
    full = lambda x: pl.BlockSpec(x.shape, lambda i, ref: (0, 0))
    width = wq.shape[0]
    return pl.pallas_call(
        gather_columns_kernel,
        grid_spec=pltpu.PrefetchScalarGridSpec(
            num_scalar_prefetch=1,
            grid=(1,),
            in_specs=[full(x) for x in (wq, wk, wv, bq, bv)],
            out_specs=[
                pl.BlockSpec((width, 3 * local), lambda i, ref: (0, 0)),
                pl.BlockSpec((1, 3 * local), lambda i, ref: (0, 0)),
            ],
        ),
        out_shape=[shape_of(width, 3 * local, bf16), shape_of(1, 3 * local, f32)],
        compiler_params=params(),
        cost_estimate=pl.CostEstimate(flops=0, bytes_accessed=0, transcendentals=0),
        name="gather_columns",
    )(sub.reshape(1).astype(jnp.int32), wq, wk, wv, bq, bv)


def attention_forward_kernel(count, block, piece, *refs):
    tokens = refs[:count]
    (w_ref, b_ref, qmark_ref, kmark_ref, segq_ref, segk_ref, ctx_a_ref, ctx_b_ref, prob_ref, inv_ref, qkv_ref,
     keys, vals, scores_a, scores_b) = refs[count:]
    step = pl.program_id(1)
    lane = lax.broadcasted_iota(jnp.int32, (1, PAIR), 1)
    low = lane < HEAD
    factor = HEAD**-0.5 * math.log2(math.e)

    @pl.when(step == 0)
    def _():
        for s in range(count):
            rows = slice(s * piece, (s + 1) * piece)
            made = (dot(tokens[s][...], w_ref[...], 1, 0) + b_ref[...]).astype(bf16)
            qkv_ref[rows] = made
            k, v, mark = made[:, PAIR : 2 * PAIR], made[:, 2 * PAIR :], kmark_ref[rows]
            one = jnp.ones_like(v)
            keys[0, rows] = jnp.where(low, k, mark)
            keys[1, rows] = jnp.where(low, mark, k)
            vals[0, rows] = jnp.where(low, v, one)
            vals[1, rows] = jnp.where(low, one, v)

    def body(own):
        rows = slice(own * block, (own + 1) * block)
        q, mark = qkv_ref[rows, :PAIR], qmark_ref[...]
        zero = jnp.zeros_like(q)
        piece_of = own * block // piece
        near = slice(piece_of * piece, (piece_of + 1) * piece)
        same = segq_ref[...] == segk_ref[piece_of : piece_of + 1, :]
        spans = [x for x in (slice(0, near.start), slice(near.stop, count * piece)) if x.stop > x.start]

        def score(h, scores):
            keep = low if h == 0 else jnp.logical_not(low)
            left = jnp.where(keep, q, mark)
            for span in spans:
                scores[:, span] = dot(left, keys[h, span, :], 1, 1)
            scores[:, near] = jnp.where(same, dot(jnp.where(keep, q, zero), keys[h, near, :], 1, 1), BLOCKED)

        def weigh(h, scores):
            chunks = [slice(s * piece, (s + 1) * piece) for s in range(count)]
            highest = functools.reduce(jnp.maximum, [jnp.max(scores[:, c], axis=1, keepdims=True) for c in chunks]) * factor
            total = 0.0
            for c in chunks:
                prob = jnp.exp2(scores[:, c] * factor - highest).astype(bf16)
                prob_ref[h, :, c] = prob
                total += dot(prob, vals[h, c, :], 1, 0)
            return total

        score(0, scores_a)
        score(1, scores_b)
        sums = [weigh(0, scores_a), weigh(1, scores_b)]
        total = pltpu.roll(jnp.where(low, sums[1], sums[0]), HEAD, 1)
        inverse = 1.0 / total
        inv_ref[...] = inverse
        ctx = ctx_a_ref if 2 * own * block < count * piece else ctx_b_ref
        ctx[...] = (jnp.where(low, sums[0], sums[1]) * inverse).astype(bf16)

    for own in range(count * piece // block):
        pl.when(step == own)(functools.partial(body, own))


def half_specs(block, steps, column):
    near = lambda p, b: (jnp.minimum(b, steps // 2 - 1), column(p))
    far = lambda p, b: (jnp.maximum(b - steps // 2, 0), column(p))
    return [pl.BlockSpec((block, PAIR), near), pl.BlockSpec((block, PAIR), far)]


def attention_forward(tokens, w_qkv, b_qkv, qmark, kmark, segq, segk, block=512):
    piece, width = tokens[0].shape
    length, local = piece * len(tokens), w_qkv.shape[1] // 3
    pairs, steps = local // PAIR, length // block
    once = pl.Buffered(1)
    return pl.pallas_call(
        functools.partial(attention_forward_kernel, len(tokens), block, piece),
        grid=(pairs, steps),
        in_specs=[pl.BlockSpec((piece, width), lambda p, b: (0, 0), pipeline_mode=once) for _ in tokens]
        + [
            pl.BlockSpec((width, TRIO), lambda p, b: (0, p)),
            pl.BlockSpec((1, TRIO), lambda p, b: (0, p)),
            pl.BlockSpec((block, PAIR), lambda p, b: (b, 0)),
            pl.BlockSpec((length, PAIR), lambda p, b: (0, 0), pipeline_mode=once),
            pl.BlockSpec((block, 1), lambda p, b: (b, 0)),
            pl.BlockSpec((length // piece, piece), lambda p, b: (0, 0)),
        ],
        out_specs=half_specs(block, steps, lambda p: p)
        + [
            pl.BlockSpec((2, block, length), lambda p, b: (p, b, 0)),
            pl.BlockSpec((block, PAIR), lambda p, b: (b, p)),
            pl.BlockSpec((length, TRIO), lambda p, b: (0, p)),
        ],
        out_shape=[
            shape_of(length // 2, local, bf16),
            shape_of(length // 2, local, bf16),
            jax.ShapeDtypeStruct((local // HEAD, length, length), bf16),
            shape_of(length, local, f32),
            shape_of(length, 3 * local, bf16),
        ],
        scratch_shapes=[
            pltpu.VMEM((2, length, PAIR), bf16),
            pltpu.VMEM((2, length, PAIR), bf16),
            pltpu.VMEM((block, length), f32),
            pltpu.VMEM((block, length), f32),
        ],
        compiler_params=params(),
        cost_estimate=pl.CostEstimate(flops=0, bytes_accessed=0, transcendentals=0),
        name="attention_forward",
    )(*tokens, w_qkv, b_qkv, qmark, kmark, segq, segk)


def attention_backward_kernel(
    chunk, grad_a_ref, grad_b_ref, ctx_a_ref, ctx_b_ref, inv_ref, qkv_ref, prob_ref, *rest
):
    dqkv_ref, sums_ref, vals, dkeys, dvals = rest[-5:]
    step, steps = pl.program_id(0), pl.num_programs(0)
    length = qkv_ref.shape[0]
    block = grad_a_ref.shape[0]
    lane = lax.broadcasted_iota(jnp.int32, (1, PAIR), 1)
    low = lane < HEAD
    slot = jnp.bitwise_and(lane, HEAD - 1)
    scale = HEAD**-0.5

    @pl.when(step == 0)
    def _():
        v = qkv_ref[:, 2 * PAIR :]
        mark = jnp.broadcast_to((slot < 3).astype(f32), v.shape).astype(bf16)
        vals[0] = jnp.where(low, v, mark)
        vals[1] = jnp.where(low, mark, v)
        dkeys[...] = jnp.zeros_like(dkeys)
        dvals[...] = jnp.zeros_like(dvals)
        sums_ref[...] = jnp.zeros_like(sums_ref)

    near = step < steps // 2
    incoming = jnp.where(near, grad_a_ref[...], grad_b_ref[...])
    ctx = jnp.where(near, ctx_a_ref[...], ctx_b_ref[...])
    rows = pl.ds(pl.multiple_of(step * block, block), block)
    grad = (incoming.astype(f32) * inv_ref[...]).astype(bf16)
    product = grad.astype(f32) * ctx.astype(f32)
    grad_t, q_t = grad.T, qkv_ref[rows, :PAIR].T
    dqs = []
    for h in range(2):
        keep = low if h == 0 else jnp.logical_not(low)
        inner = jnp.sum(jnp.where(keep, product, 0.0), axis=1, keepdims=True)
        top = inner.astype(bf16).astype(f32)
        mid = (inner - top).astype(bf16).astype(f32)
        last = inner - top - mid
        mark = jnp.where(slot == 0, -top, jnp.where(slot == 1, -mid, jnp.where(slot == 2, -last, 0.0)))
        left = jnp.where(keep, grad, mark.astype(bf16))
        part = slice(h * HEAD, (h + 1) * HEAD)
        dq = None
        for j in range(length // chunk):
            cols = slice(j * chunk, (j + 1) * chunk)
            prob = prob_ref[h, :, cols]
            ds = prob * dot(left, vals[h, cols, :], 1, 1).astype(bf16)
            dvals[part, cols] += dot(grad_t[part], prob, 1, 0)
            dkeys[part, cols] += dot(q_t[part], ds, 1, 0)
            term = dot(ds, qkv_ref[cols, PAIR : 2 * PAIR], 1, 0)
            dq = term if dq is None else dq + term
        dqs.append(dq)
    dq = (jnp.where(low, dqs[0], dqs[1]) * scale).astype(bf16)
    dqkv_ref[rows, :PAIR] = dq
    sums_ref[0:1, :PAIR] += jnp.sum(dq.astype(f32), axis=0, keepdims=True)

    @pl.when(step == steps - 1)
    def _():
        dqkv_ref[:, PAIR : 2 * PAIR] = (dkeys[...] * scale).T.astype(bf16)
        dv = dvals[...].T.astype(bf16)
        dqkv_ref[:, 2 * PAIR :] = dv
        sums_ref[0:1, 2 * PAIR :] = jnp.sum(dv.astype(f32), axis=0, keepdims=True)


def attention_backward(pair, grads, ctxs, inv, qkv, prob, before, block=256, chunk=2048):
    length = qkv.shape[0]
    steps = length // block
    halves = [pl.BlockSpec(s.block_shape, lambda b, s=s: s.index_map(pair, b)) for s in half_specs(block, steps, lambda p: p)]
    return pl.pallas_call(
        functools.partial(attention_backward_kernel, min(chunk, length)),
        grid=(steps,),
        in_specs=halves
        + halves
        + [
            pl.BlockSpec((block, PAIR), lambda b: (b, pair)),
            pl.BlockSpec((length, TRIO), lambda b: (0, pair)),
            pl.BlockSpec((2, block, length), lambda b: (pair, b, 0)),
        ]
        + [pl.BlockSpec(memory_space=pl.ANY)] * len(before),
        out_specs=[pl.BlockSpec((length, TRIO), lambda b: (0, pair)), pl.BlockSpec((8, TRIO), lambda b: (0, 0))],
        out_shape=[shape_of(length, qkv.shape[1], bf16), shape_of(8, TRIO, f32)],
        scratch_shapes=[
            pltpu.VMEM((2, length, PAIR), bf16),
            pltpu.VMEM((PAIR, length), f32),
            pltpu.VMEM((PAIR, length), f32),
        ],
        input_output_aliases={7: 0} if before else {},
        compiler_params=params(),
        cost_estimate=pl.CostEstimate(flops=0, bytes_accessed=0, transcendentals=0),
        name="attention_backward",
    )(*grads, *ctxs, inv, qkv, prob, *before)


def norm_stats(values):
    centered = values - jnp.mean(values, axis=-1, keepdims=True)
    inverse = lax.rsqrt(jnp.mean(centered * centered, axis=-1, keepdims=True) + EPSILON)
    return centered * inverse, inverse


def norm_backward(grad, gain, normed, inverse):
    t = grad * gain
    return (
        t - jnp.mean(t, axis=-1, keepdims=True) - normed * jnp.mean(t * normed, axis=-1, keepdims=True)
    ) * inverse


def row_sum(values):
    return jnp.sum(values, axis=0, keepdims=True)


def normal(u):
    return 0.5 + 0.5 * lax.erf(u * math.sqrt(0.5)), jnp.exp(u * u * -0.5) * (1.0 / math.sqrt(2.0 * math.pi))


def feed_forward_kernel(count, chunk, core_ref, *refs):
    toks, cots = refs[:count], refs[count : 2 * count]
    (ctx_a_ref, ctx_b_ref, wo_ref, wu_ref, wd_ref, vec_ref, bu_ref) = refs[2 * count : 2 * count + 7]
    outs = refs[2 * count + 7 : 3 * count + 7]
    slope_ref, r2_ref, n1_ref, inv_ref, sums_ref, sent_ref, kept_ref, act, total_down = refs[3 * count + 7 :]
    step, steps = pl.program_id(0), pl.num_programs(0)
    index = step // (steps // count)

    @pl.when(step == 0)
    def _():
        sums_ref[...] = jnp.zeros_like(sums_ref)
        total_down[...] = jnp.zeros_like(total_down)

    bo, g1, s1, bd, g2, s2 = [vec_ref[i : i + 1] for i in range(6)]
    split = ctx_a_ref.shape[1]
    branch = dot(ctx_a_ref[...], wo_ref[:split], 1, 0) + dot(ctx_b_ref[...], wo_ref[split:], 1, 0)
    n1, inv1 = norm_stats(pick(index, toks).astype(f32) + branch + bo)
    hidden = n1 * g1 + s1
    low = hidden.astype(bf16)
    n1_ref[...] = n1
    inv_ref[...] = jnp.broadcast_to(inv1, inv_ref.shape)
    total = hidden + bd
    slices = [slice(j * chunk, (j + 1) * chunk) for j in range(wu_ref.shape[1] // chunk)]
    for cols in slices:
        pre = dot(low, wu_ref[:, cols], 1, 0) + bu_ref[:, cols]
        cdf, phi = normal(pre)
        part = (pre * cdf).astype(bf16)
        act[:, cols] = part
        slope_ref[:, cols] = (cdf + pre * phi).astype(bf16)
        total += dot(part, wd_ref[cols, :], 1, 0)
    n2, inv2 = norm_stats(total)
    result = (n2 * g2 + s2).astype(bf16)
    for s in range(count):

        @pl.when(index == s)
        def _(s=s):
            outs[s][...] = result

    grad = pick(index, cots).astype(f32)
    r2 = norm_backward(grad, g2, n2, inv2)
    feed = r2.astype(bf16)
    r2_ref[...] = r2
    sums_ref[0:1] += row_sum(grad * n2)
    sums_ref[1:2] += row_sum(grad)
    sums_ref[2:3] += row_sum(feed.astype(f32))
    for cols in slices:
        total_down[cols] += dot(act[:, cols], feed, 0, 0)

    @pl.when(step == steps - 1)
    def _():
        half = sent_ref.shape[0]
        for ref, place in ((sent_ref, 1 - core_ref[0]), (kept_ref, core_ref[0])):
            ref[...] = total_down[pl.ds(pl.multiple_of(place * half, half), half)].astype(bf16)


def feed_backward_kernel(
    chunk, core_ref, r2_ref, slope_ref, n1_ref, inv_ref, ctx_a_ref, ctx_b_ref, first_sums_ref,
    wo_ref, wu_ref, wd_ref, vec_ref, r1_ref, dctx_a_ref, dctx_b_ref, sent_ref, kept_ref,
    sums, upsum, total_up, total_out,
):
    step, steps = pl.program_id(0), pl.num_programs(0)

    @pl.when(step == 0)
    def _():
        for ref in (sums, upsum, total_up, total_out):
            ref[...] = jnp.zeros_like(ref)

    width, hidden = wu_ref.shape
    grad, n1 = r2_ref[...], n1_ref[...]
    feed, low = grad.astype(bf16), (n1 * vec_ref[1:2] + vec_ref[2:3]).astype(bf16)
    for j in range(hidden // chunk):
        cols = slice(j * chunk, (j + 1) * chunk)
        pre = (dot(feed, wd_ref[cols, :], 1, 1) * slope_ref[:, cols].astype(f32)).astype(bf16)
        upsum[0:1, cols] += row_sum(pre.astype(f32))
        grad += dot(pre, wu_ref[:, cols], 1, 1)
        total_up[:, cols] += dot(low, pre, 0, 0)
    r1 = norm_backward(grad, vec_ref[1:2], n1, inv_ref[:, :1])
    branch = r1.astype(bf16)
    r1_ref[...] = r1
    split = dctx_a_ref.shape[1]
    dctx_a_ref[...] = dot(branch, wo_ref[:split], 1, 1).astype(bf16)
    dctx_b_ref[...] = dot(branch, wo_ref[split:], 1, 1).astype(bf16)
    total_out[:split] += dot(ctx_a_ref[...], branch, 0, 0)
    total_out[split:] += dot(ctx_b_ref[...], branch, 0, 0)
    sums[0:1] += row_sum(grad * n1)
    sums[1:2] += row_sum(grad)
    sums[2:3] += row_sum(branch.astype(f32))

    @pl.when(step == steps - 1)
    def _():
        core = core_ref[0]
        vectors = [first_sums_ref[i : i + 1] for i in range(3)] + [sums[i : i + 1] for i in range(3)]
        vectors += [upsum[0:1, i * width : (i + 1) * width] for i in range(hidden // width)]
        each = (len(vectors) + 1) // 2
        vectors += [jnp.zeros_like(vectors[0])] * (2 * each - len(vectors))
        blank = jnp.zeros((PAIR - each, width), f32)
        blocks = [jnp.concatenate(vectors[i * each : (i + 1) * each] + [blank], axis=0).T for i in range(2)]
        half = hidden // 2
        for ref, place in ((sent_ref, 1 - core), (kept_ref, core)):
            ref[:, :half] = total_up[:, pl.ds(pl.multiple_of(place * half, PAIR), half)].astype(bf16)
            columns = pl.ds(pl.multiple_of(place * split, PAIR), split)
            for g in range(2):
                rows = pl.ds(pl.multiple_of(jnp.bitwise_xor(core, g) * split, split), split)
                ref[g * split : (g + 1) * split, half : half + split] = total_out[rows, columns].astype(bf16)
            ref[:, half + split :] = jnp.where(place == 0, blocks[0], blocks[1]).astype(bf16)


def whole(values):
    return pl.BlockSpec(values.shape, lambda i, _: (0,) * values.ndim, pipeline_mode=pl.Buffered(1))


def fixed(rows, cols):
    return pl.BlockSpec((rows, cols), lambda i, _: (0, 0))


def row_blocks(block, *widths):
    return [pl.BlockSpec((block, n), lambda i, _: (i, 0)) for n in widths]


def feed_forward(core, toks, cots, ctx_a, ctx_b, wo, wu, wd, vec, bu, block=256):
    width, hidden = wu.shape
    count = ctx_a.shape[0]
    outs = [shape_of(x.shape[0], width, bf16) for x in toks]
    return pl.pallas_call(
        functools.partial(feed_forward_kernel, len(toks), 768),
        grid_spec=pltpu.PrefetchScalarGridSpec(
            num_scalar_prefetch=1,
            grid=(count // block,),
            in_specs=piece_specs(block, toks)
            + piece_specs(block, cots)
            + row_blocks(block, ctx_a.shape[1], ctx_b.shape[1])
            + [whole(x) for x in (wo, wu, wd, vec, bu)],
            out_specs=piece_specs(block, outs)
            + row_blocks(block, hidden, width, width, PAIR)
            + [fixed(8, width), fixed(hidden // 2, width), fixed(hidden // 2, width)],
            scratch_shapes=[pltpu.VMEM((block, hidden), bf16), pltpu.VMEM((hidden, width), f32)],
        ),
        out_shape=outs
        + [
            shape_of(count, hidden, bf16),
            shape_of(count, width, f32),
            shape_of(count, width, f32),
            shape_of(count, PAIR, f32),
            shape_of(8, width, f32),
            shape_of(hidden // 2, width, bf16),
            shape_of(hidden // 2, width, bf16),
        ],
        compiler_params=params(),
        cost_estimate=pl.CostEstimate(flops=0, bytes_accessed=0, transcendentals=0),
        name="feed_forward",
    )(core, *toks, *cots, ctx_a, ctx_b, wo, wu, wd, vec, bu)


def feed_backward(core, r2, slope, n1, inv, ctx_a, ctx_b, first_sums, wo, wu, wd, vec, block=256):
    count, width = r2.shape
    hidden, local = wu.shape[1], ctx_a.shape[1]
    out = hidden // 2 + local + PAIR
    return pl.pallas_call(
        functools.partial(feed_backward_kernel, 768),
        grid_spec=pltpu.PrefetchScalarGridSpec(
            num_scalar_prefetch=1,
            grid=(count // block,),
            in_specs=row_blocks(block, width, hidden, width, PAIR, local, local)
            + [whole(x) for x in (first_sums, wo, wu, wd, vec)],
            out_specs=row_blocks(block, width, local, local) + [fixed(width, out), fixed(width, out)],
            scratch_shapes=[
                pltpu.VMEM((8, width), f32),
                pltpu.VMEM((8, hidden), f32),
                pltpu.VMEM((width, hidden), f32),
                pltpu.VMEM((width, width), f32),
            ],
        ),
        out_shape=[
            shape_of(count, width, f32),
            shape_of(count, local, bf16),
            shape_of(count, local, bf16),
            shape_of(width, out, bf16),
            shape_of(width, out, bf16),
        ],
        compiler_params=params(),
        cost_estimate=pl.CostEstimate(flops=0, bytes_accessed=0, transcendentals=0),
        name="feed_backward",
    )(core, r2, slope, n1, inv, ctx_a, ctx_b, first_sums, wo, wu, wd, vec)


def assemble_kernel(parts, cuts, place_ref, *refs):
    count = (len(refs) - len(cuts)) // 2
    own, got, outs = refs[:count], refs[count : 2 * count], refs[2 * count :]
    low = jnp.bitwise_and(jnp.where(pl.program_id(0) == place_ref[0], place_ref[1], place_ref[2]), parts - 1)
    size = own[0].shape[0] // parts

    def write(sources):
        for t in range(parts):
            start = pl.multiple_of(jnp.bitwise_xor(low, t) * size, 16)
            for out, pieces in zip(outs, cuts, strict=True):
                for which, source, target, width in pieces:
                    out[t * size : (t + 1) * size, target : target + width] = sources[which][
                        pl.ds(start, size), source : source + width
                    ].astype(f32)

    @pl.when(pl.program_id(0) == place_ref[0])
    def _():
        write(own)

    @pl.when(pl.program_id(0) != place_ref[0])
    def _():
        write(got)


def assemble(place, own, got, cuts, by_rows, blocks=2):
    rows, parts = own[0].shape[0], 8 // blocks
    size = rows // blocks
    mine = lambda h, j, ref: (jnp.where(h == ref[0], jnp.bitwise_xor(j, ref[1] // parts), 0), 0)
    other = lambda h, j, ref: (jnp.where(h == ref[0], 0, jnp.bitwise_xor(j, ref[2] // parts)), 0)
    outs, specs = [], []
    for pieces in cuts:
        width = sum(piece[-1] for piece in pieces)
        if by_rows:
            outs.append(shape_of(2 * rows, width, f32))
            specs.append(pl.BlockSpec((size, width), lambda h, j, ref: (blocks * h + j, 0)))
        else:
            outs.append(shape_of(rows, 2 * width, f32))
            specs.append(pl.BlockSpec((size, width), lambda h, j, ref: (j, h)))
    return pl.pallas_call(
        functools.partial(assemble_kernel, parts, cuts),
        grid_spec=pltpu.PrefetchScalarGridSpec(
            num_scalar_prefetch=1,
            grid=(2, blocks),
            in_specs=[pl.BlockSpec((size, x.shape[1]), mine) for x in own]
            + [pl.BlockSpec((size, x.shape[1]), other) for x in got],
            out_specs=specs,
        ),
        out_shape=outs,
        compiler_params=params(),
        cost_estimate=pl.CostEstimate(flops=0, bytes_accessed=0, transcendentals=0),
        name="assemble",
    )(place, *own, *got)


def cut(values, index, axis=0):
    size = values.shape[axis] // 2
    return lax.dynamic_slice_in_dim(values, index * size, size, axis)


def total_of(terms):
    value = terms[0].astype(f32)
    for term in terms[1:]:
        value += term.astype(f32)
    return value.astype(bf16)


class Exchange:
    def __init__(self, row_size, seq_size, *orders):
        seq_bits, row_bits = seq_size.bit_length() - 1, row_size.bit_length() - 1
        x, rows = list(range(1, seq_bits)), list(range(seq_bits, seq_bits + row_bits))
        every = rows[:2] + x + rows[2:]
        first, second = [[every[i] for i in order] for order in orders]
        self.orders = (first, second)
        self.rest = every[3:]
        self.size = row_size * seq_size
        self.phases = len(first)
        here = lax.axis_index("rows") * seq_size + lax.axis_index("seq")
        self.core = jnp.bitwise_and(here, 1)
        bit = lambda k: jnp.bitwise_and(lax.shift_right_logical(here, k), 1)
        self.bits = [jnp.where(self.core == 0, bit(a), bit(b)) for a, b in zip(first, second)]
        places = []
        for order in self.orders:
            place = 0
            for k in order:
                place = 2 * place + bit(k)
            places.append(place)
        own = jnp.where(self.core == 0, places[0], places[1])
        other = jnp.where(self.core == 0, places[1], places[0])
        self.place = jnp.stack([self.core, own, other]).astype(jnp.int32)

    def send(self, values, phase):
        pairs = [(d, d ^ (1 << self.orders[d & 1][phase])) for d in range(self.size)]
        return lax.ppermute(values, BOTH, pairs)

    def halves(self, phase, *terms):
        bit = self.bits[phase]
        return total_of([cut(x, 1 - bit) for x in terms]), total_of([cut(x, bit) for x in terms])

    def finish(self, *terms):
        value = total_of(terms)
        for k in self.rest[1:]:
            value = total_of([value, self.whole(value, k)])
        return value

    def whole(self, values, k):
        return lax.ppermute(values, BOTH, [(d, d ^ (1 << k)) for d in range(self.size)])

    def by(self, phase):
        if phase == self.phases:
            return lambda values: self.whole(values, self.rest[0])
        return lambda values: self.send(values, phase)


def step(*operands, work=None, carry=()):
    values = lax.optimization_barrier(tuple(x for x, _ in operands))
    got = [how(x) for x, (_, how) in zip(values, operands)]
    done = None if work is None else work(values)
    return lax.optimization_barrier((tuple(values), tuple(got), done, carry))


def joined(own, got):
    return jnp.concatenate([own, got], axis=0)


def on_device(
    sizes, tokens, segments, query_weight, query_bias, key_weight, value_weight, value_bias, out_weight, out_bias,
    first_gain, first_shift, up_weight, up_bias, down_weight, down_bias, second_gain, second_shift, cotangent,
):
    row_size, seq_size = sizes
    row_count, pos, width = tokens.shape
    groups = math.gcd(row_count, seq_size)
    subs = seq_size // groups
    if row_count != 2 or groups != 2 or subs != 2:
        raise ValueError("unsupported split")
    me = lax.axis_index("seq")
    group, sub = me // subs, lax.rem(me, subs)
    length = pos * seq_size
    half = length // 2
    local = width // subs
    pairs = local // PAIR
    exchange = Exchange(row_size, seq_size, (0, 2, 1), (1, 0, 2))
    up_exchange = Exchange(row_size, seq_size, (0, 2, 1), (1, 2, 0))
    three_exchange = Exchange(row_size, seq_size, (0, 2, 1), (2, 1, 0))

    def shifted(values, s):
        return lax.ppermute(values, "seq", [(i, (i + s * subs) % seq_size) for i in range(seq_size)])

    def cut_rows(values):
        return [lax.dynamic_index_in_dim(values, lax.rem(group + s, groups), 0, keepdims=False) for s in range(groups)]

    def trade(blocks):
        return blocks[:1] + [shifted(x, s) for s, x in enumerate(blocks[1:], 1)]

    def place_rows(pieces):
        rows = []
        for r in range(groups):
            picked = pieces[0]
            for s in range(1, groups):
                picked = jnp.where(lax.rem(group + s, groups) == r, pieces[s], picked)
            rows.append(picked)
        return jnp.stack(rows)

    def core_swap(values):
        return lax.ppermute(values, "seq", [(i, i ^ 1) for i in range(seq_size)])

    tok_blocks = cut_rows(tokens)
    trade_back = lambda values: shifted(values, 1)
    toks = trade(tok_blocks)
    late_group, late = tie((group, sub), tok_blocks[1:])
    cot_blocks = [lax.dynamic_index_in_dim(cotangent, lax.rem(late_group + s, groups), 0, keepdims=False) for s in range(groups)]

    seg_row = lax.dynamic_index_in_dim(segments, late_group, 0, keepdims=False)
    middle = seg_row[length // 2]
    seg_pieces = []
    for u in range(subs):
        for s in range(groups):
            quarter = lax.rem(late_group + groups - s, groups) * subs + lax.rem(late + u, subs)
            seg_pieces.append(lax.dynamic_slice_in_dim(seg_row, quarter * pos, pos, 0))
    seg_k = jnp.stack(seg_pieces)
    seg_q = seg_k.reshape(length, 1)
    outside = jnp.where(seg_q == middle, 0.0, BLOCKED)
    slot = (jnp.arange(PAIR) % HEAD)[None, :]
    q_mark = jnp.where(slot == 0, 1.0, jnp.where(slot == 1, outside, 0.0)).astype(bf16)
    k_mark = jnp.where(slot == 0, outside, jnp.where(slot == 1, 1.0, 0.0)).astype(bf16)

    w_qkv, b_qkv = gather_columns(
        late, query_weight, key_weight, value_weight, query_bias.reshape(1, -1), value_bias.reshape(1, -1), local
    )
    wo = jnp.concatenate([lax.dynamic_slice_in_dim(out_weight, i * local, local, 0) for i in (late, 1 - late)], axis=0)
    vec = jnp.stack([out_bias, first_gain, first_shift, down_bias, second_gain, second_shift, second_shift, second_shift])
    bu = up_bias.reshape(1, -1)

    prepared = (wo, vec, bu, w_qkv, b_qkv, q_mark, k_mark, seg_q, seg_k, cot_blocks)
    far = [core_swap(toks[0])] + [core_swap(tie(x, prepared)) for x in toks[1:]]
    toks_all = toks + far
    ctx_a, ctx_b, prob, inv, qkv = attention_forward(toks_all, w_qkv, b_qkv, q_mark, k_mark, seg_q, seg_k)
    cots = trade(cot_blocks)
    tok_full = jnp.concatenate(toks_all, axis=0)
    ctx_got = core_swap(ctx_b)
    core = sub.reshape(1).astype(jnp.int32)
    made = feed_forward(core, toks, cots, ctx_a, ctx_got, wo, up_weight, down_weight, vec, bu)
    outs, (slope, r2, n1, inv1, sums_two, down_sent, down_kept) = made[:groups], made[groups:]

    def backward(sent):
        return feed_backward(
            core, tie(r2, sent), slope, n1, inv1, ctx_a, ctx_got, sums_two, wo, up_weight, down_weight, vec
        )

    _, (down_got,), made, down_kept = step((down_sent, core_swap), work=backward, carry=down_kept)
    r1, dctx_a, dctx_b, up_sent, up_kept = made
    _, (dctx_got,), (send_down, down), (up_sent, up_kept) = step(
        (dctx_b, core_swap), work=lambda sent: exchange.halves(0, *tie((down_kept, down_got), sent)), carry=(up_sent, up_kept)
    )
    grads, ctxs = (dctx_a, dctx_got), (ctx_a, ctx_b)
    dqkv, biases = (), []
    for p in range(pairs):

        def work(sent, p=p, dqkv=dqkv):
            return attention_backward(p, tie(grads, sent), ctxs, inv, qkv, prob, dqkv)

        operands = [(send_down, exchange.by(p)), (up_sent, core_swap) if p == 0 else (send_up, up_exchange.by(p - 1))]
        operands += [(outs[1], trade_back)] if p == 0 else []
        kept = (down, up_kept) if p == 0 else (down, up)
        _, got, (made, bias), (down, up) = step(*operands, work=work, carry=kept)
        out_got = got[2] if p == 0 else out_got
        dqkv = (made,)
        biases.append(bias[0])
        if p + 1 < exchange.phases:
            send_down, down = exchange.halves(p + 1, down, got[0])
        else:
            send_down = down = total_of([down, got[0]])
        send_up, up = up_exchange.halves(p, up, got[1])
    dqkv = dqkv[0]
    bias_q = jnp.concatenate([b[:PAIR] for b in biases])
    bias_v = jnp.concatenate([b[2 * PAIR :] for b in biases])
    bias_col = jnp.pad(jnp.concatenate([bias_q, bias_v]).astype(bf16)[:, None], ((0, 0), (0, PAIR - 1)))
    three = jnp.concatenate([dot(tok_full, dqkv, 0, 0).astype(bf16), bias_col], axis=1)
    send_three, three = three_exchange.halves(0, three)

    def share_far(sent):
        d, w = tie((dqkv, w_qkv), sent)
        return dot(d[half:], w, 1, 1).astype(bf16)

    _, (got, up_got, down_got), far, (three, up, down) = step(
        (send_three, three_exchange.by(0)), (send_up, up_exchange.by(2)), (send_down, exchange.by(3)), work=share_far,
        carry=(three, up, down),
    )
    send_three, three = three_exchange.halves(1, three, got)
    up, down = total_of([up, up_got]), exchange.finish(down, down_got)

    def share_near(sent):
        d, w = tie((dqkv, w_qkv), sent)
        return r1 + dot(d[:half], w, 1, 1)

    (_, _, _, far), (got, up_got, down_got, far_got), near, (three, up, down) = step(
        (send_three, three_exchange.by(1)), (up, up_exchange.by(3)), (down, exchange.by(2)), (far, core_swap),
        work=share_near, carry=(three, up, down),
    )
    in_half = near + far_got.astype(f32)
    in_sent = in_half[pos:].astype(bf16)
    send_three, three = three_exchange.halves(2, three, got)
    up, down = up_exchange.finish(up, up_got), joined(down, down_got)
    _, (got, up_got, down_got), output, (three, up, down) = step(
        (send_three, three_exchange.by(2)), (up, up_exchange.by(2)), (down, exchange.by(1)),
        work=lambda sent: place_rows([outs[0], tie(out_got, sent)]), carry=(three, up, down),
    )
    three = total_of([three, got])
    up, down = joined(up, up_got), joined(down, down_got)
    _, (got, up_got, down_got), _, (three, up, down) = step(
        (three, three_exchange.by(3)), (up, up_exchange.by(1)), (down, exchange.by(0)), carry=(three, up, down)
    )
    three = three_exchange.finish(three, got)
    up, down = joined(up, up_got), joined(down, down_got)
    _, (got, up_got, down_got, in_got), _, (three, up, down) = step(
        (three, three_exchange.by(2)), (up, up_exchange.by(0)), (down, core_swap), (in_sent, trade_back),
        carry=(three, up, down),
    )
    three, up = joined(three, got), joined(up, up_got)

    def assemble_down(sent):
        return assemble(exchange.place, [tie(down, sent)], [down_got], [[(0, 0, 0, width)]], True)[0]

    _, (got, up_got), downweight_grad, (three, up) = step(
        (three, three_exchange.by(1)), (up, core_swap), work=assemble_down, carry=(three, up)
    )
    three = joined(three, got)
    hidden = up_bias.shape[0]
    vectors = 6 + hidden // width
    each = (vectors + 1) // 2

    def assemble_up(sent):
        cuts = [[(0, 0, 0, hidden // 2)], [(0, hidden // 2, 0, local)], [(0, hidden // 2 + local, 0, PAIR)]]
        made = assemble(up_exchange.place, [tie(up, sent)], [up_got], cuts, False)
        return made, place_rows([in_half[:pos], tie(in_got, sent).astype(f32)])

    _, (got,), ((upweight_grad, outweight_grad, vector_grads), input_grad), three = step(
        (three, three_exchange.by(0)), work=assemble_up, carry=three
    )
    three = joined(three, got)
    _, (three_got,), _, three = step((three, core_swap), carry=three)
    cuts = [[(0, p * TRIO + i * PAIR, p * PAIR, PAIR) for p in range(pairs)] for i in range(3)]
    queryweight_grad, keyweight_grad, valueweight_grad, bias_out = assemble(
        three_exchange.place, [three], [three_got], cuts + [[(0, 3 * local, 0, PAIR)]], False
    )
    bias_out = bias_out.reshape(2, local, 2, PAIR)[:, :, :, 0]
    query_bias_grad = bias_out[0].T.reshape(width)
    value_bias_grad = bias_out[1].T.reshape(width)

    small = jnp.concatenate([vector_grads[:, :each], vector_grads[:, PAIR : PAIR + each]], axis=1).T
    return (
        output, input_grad, queryweight_grad, query_bias_grad, keyweight_grad, valueweight_grad, value_bias_grad,
        outweight_grad, small[5], small[3], small[4], upweight_grad, small[6:vectors].reshape(-1),
        downweight_grad, small[2], small[0], small[1],
    )


def solution(mesh):
    split = P("rows", "seq", None)
    return jax.shard_map(
        functools.partial(on_device, (mesh.shape["rows"], mesh.shape["seq"])),
        mesh=mesh,
        in_specs=(split, P("rows", None)) + (P(),) * 15 + (split,),
        out_specs=(split, split) + (P(),) * 15,
        check_vma=False,
    )
```

```python
import functools
import math

import jax
import jax.numpy as jnp
from jax import lax
from jax.experimental import pallas as pl
from jax.experimental.pallas import tpu as pltpu
from jax.sharding import PartitionSpec as P

HEAD = 64
PAIR = 2 * HEAD
TRIO = 3 * PAIR
EPSILON = 1e-06
BLOCKED = -(2.0**100)
VMEM_LIMIT = 60 * 2**20
BOTH = ("rows", "seq")
bf16 = jnp.bfloat16
f32 = jnp.float32


def dot(left, right, over_left, over_right):
    return lax.dot_general(
        left, right, (((over_left,), (over_right,)), ((), ())), preferred_element_type=f32
    )


def shape_of(rows, cols, kind):
    return jax.ShapeDtypeStruct((rows, cols), kind)


def params():
    return pltpu.CompilerParams(vmem_limit_bytes=VMEM_LIMIT)


def tie(values, *others):
    return lax.optimization_barrier((values, others))[0]


def piece_specs(block, pieces):
    each = pieces[0].shape[0] // block
    return [
        pl.BlockSpec((block, x.shape[1]), lambda i, _, s=s: (jnp.clip(i - s * each, 0, each - 1), 0))
        for s, x in enumerate(pieces)
    ]


def pick(index, refs):
    value = refs[0][...]
    for s in range(1, len(refs)):
        value = jnp.where(index == s, refs[s][...], value)
    return value


def gather_columns_kernel(place_ref, q_ref, k_ref, v_ref, qb_ref, vb_ref, up_ref, *refs):
    vectors, (w_ref, b_ref, vec_ref, bu_ref) = refs[:-4], refs[-4:]
    width = w_ref.shape[1] // 3
    for i, ref in enumerate(vectors):
        vec_ref[i, :] = ref[...]
    bu_ref[0, :] = up_ref[...]
    for p in range(width // PAIR):
        source = pl.ds(pl.multiple_of(place_ref[0] * width + p * PAIR, PAIR), PAIR)
        for i, (weight, bias) in enumerate(((q_ref, qb_ref), (k_ref, None), (v_ref, vb_ref))):
            target = slice(p * TRIO + i * PAIR, p * TRIO + (i + 1) * PAIR)
            w_ref[:, target] = weight[:, source]
            b_ref[0, target] = jnp.zeros((PAIR,), f32) if bias is None else bias[source]


def gather_columns(sub, wq, wk, wv, bq, bv, up, vectors, local):
    full = lambda x: pl.BlockSpec(x.shape, lambda i, ref: (0,) * len(x.shape))
    width, args = wq.shape[0], (wq, wk, wv, bq, bv, up, *vectors)
    outs = [shape_of(width, 3 * local, bf16), shape_of(1, 3 * local, f32), shape_of(8, width, f32), shape_of(1, up.shape[0], f32)]
    return pl.pallas_call(
        gather_columns_kernel,
        grid_spec=pltpu.PrefetchScalarGridSpec(
            num_scalar_prefetch=1, grid=(1,), in_specs=[full(x) for x in args], out_specs=[full(x) for x in outs]
        ),
        out_shape=outs,
        compiler_params=params(),
        cost_estimate=pl.CostEstimate(flops=0, bytes_accessed=0, transcendentals=0),
        name="gather_columns",
    )(sub.reshape(1).astype(jnp.int32), *args)


def attention_forward_kernel(count, block, piece, *refs):
    tokens = refs[:count]
    (w_ref, b_ref, qmark_ref, kmark_ref, seg_ref, ctx_a_ref, ctx_b_ref, prob_ref, inv_ref, qkv_ref,
     keys, vals, scores_a, scores_b) = refs[count:]
    step = pl.program_id(1)
    lane = lax.broadcasted_iota(jnp.int32, (1, PAIR), 1)
    low = lane < HEAD
    factor = HEAD**-0.5 * math.log2(math.e)

    @pl.when(step == 0)
    def _():
        for s in range(count):
            rows = slice(s * piece, (s + 1) * piece)
            made = (dot(tokens[s][...], w_ref[...], 1, 0) + b_ref[...]).astype(bf16)
            qkv_ref[rows] = made
            k, v, mark = made[:, PAIR : 2 * PAIR], made[:, 2 * PAIR :], kmark_ref[rows]
            one = jnp.ones_like(v)
            keys[0, rows] = jnp.where(low, k, mark)
            keys[1, rows] = jnp.where(low, mark, k)
            vals[0, rows] = jnp.where(low, v, one)
            vals[1, rows] = jnp.where(low, one, v)

    def body(own):
        rows = slice(own * block, (own + 1) * block)
        q, mark = qkv_ref[rows, :PAIR], qmark_ref[...]
        zero = jnp.zeros_like(q)
        piece_of = own * block // piece
        near = slice(piece_of * piece, (piece_of + 1) * piece)
        here = seg_ref[piece_of : piece_of + 1, :]
        first = own * block - near.start
        column = jnp.broadcast_to(here[:, first : first + block], (PAIR, block)).T[:, :1]
        same = column == here
        spans = [x for x in (slice(0, near.start), slice(near.stop, count * piece)) if x.stop > x.start]

        def score(h, scores):
            keep = low if h == 0 else jnp.logical_not(low)
            left = jnp.where(keep, q, mark)
            for span in spans:
                scores[:, span] = dot(left, keys[h, span, :], 1, 1)
            scores[:, near] = jnp.where(same, dot(jnp.where(keep, q, zero), keys[h, near, :], 1, 1), BLOCKED)

        def weigh(h, scores):
            chunks = [slice(s * piece, (s + 1) * piece) for s in range(count)]
            highest = functools.reduce(jnp.maximum, [jnp.max(scores[:, c], axis=1, keepdims=True) for c in chunks]) * factor
            total = 0.0
            for c in chunks:
                prob = jnp.exp2(scores[:, c] * factor - highest).astype(bf16)
                prob_ref[h, :, c] = prob
                total += dot(prob, vals[h, c, :], 1, 0)
            return total

        score(0, scores_a)
        score(1, scores_b)
        sums = [weigh(0, scores_a), weigh(1, scores_b)]
        total = pltpu.roll(jnp.where(low, sums[1], sums[0]), HEAD, 1)
        inverse = 1.0 / total
        inv_ref[...] = inverse
        ctx = ctx_a_ref if 2 * own * block < count * piece else ctx_b_ref
        ctx[...] = (jnp.where(low, sums[0], sums[1]) * inverse).astype(bf16)

    for own in range(count * piece // block):
        pl.when(step == own)(functools.partial(body, own))


def half_specs(block, steps, column):
    near = lambda p, b: (jnp.minimum(b, steps // 2 - 1), column(p))
    far = lambda p, b: (jnp.maximum(b - steps // 2, 0), column(p))
    return [pl.BlockSpec((block, PAIR), near), pl.BlockSpec((block, PAIR), far)]


def attention_forward(tokens, w_qkv, b_qkv, qmark, kmark, segs, block=512):
    piece, width = tokens[0].shape
    length, local = piece * len(tokens), w_qkv.shape[1] // 3
    pairs, steps = local // PAIR, length // block
    once = pl.Buffered(1)
    return pl.pallas_call(
        functools.partial(attention_forward_kernel, len(tokens), block, piece),
        grid=(pairs, steps),
        in_specs=[pl.BlockSpec((piece, width), lambda p, b: (0, 0), pipeline_mode=once) for _ in tokens]
        + [
            pl.BlockSpec((width, TRIO), lambda p, b: (0, p)),
            pl.BlockSpec((1, TRIO), lambda p, b: (0, p)),
            pl.BlockSpec((block, PAIR), lambda p, b: (b, 0)),
            pl.BlockSpec((length, PAIR), lambda p, b: (0, 0), pipeline_mode=once),
            pl.BlockSpec((length // piece, piece), lambda p, b: (0, 0)),
        ],
        out_specs=half_specs(block, steps, lambda p: p)
        + [
            pl.BlockSpec((2, block, length), lambda p, b: (p, b, 0)),
            pl.BlockSpec((block, PAIR), lambda p, b: (b, p)),
            pl.BlockSpec((length, TRIO), lambda p, b: (0, p)),
        ],
        out_shape=[
            shape_of(length // 2, local, bf16),
            shape_of(length // 2, local, bf16),
            jax.ShapeDtypeStruct((local // HEAD, length, length), bf16),
            shape_of(length, local, f32),
            shape_of(length, 3 * local, bf16),
        ],
        scratch_shapes=[
            pltpu.VMEM((2, length, PAIR), bf16),
            pltpu.VMEM((2, length, PAIR), bf16),
            pltpu.VMEM((block, length), f32),
            pltpu.VMEM((block, length), f32),
        ],
        compiler_params=params(),
        cost_estimate=pl.CostEstimate(flops=0, bytes_accessed=0, transcendentals=0),
        name="attention_forward",
    )(*tokens, w_qkv, b_qkv, qmark, kmark, segs)


def attention_backward_kernel(
    chunk, grad_a_ref, grad_b_ref, ctx_a_ref, ctx_b_ref, inv_ref, qkv_ref, prob_ref, *rest
):
    dqkv_ref, sums_ref, vals, dkeys, dvals = rest[-5:]
    step, steps = pl.program_id(0), pl.num_programs(0)
    length = qkv_ref.shape[0]
    block = grad_a_ref.shape[0]
    lane = lax.broadcasted_iota(jnp.int32, (1, PAIR), 1)
    low = lane < HEAD
    slot = jnp.bitwise_and(lane, HEAD - 1)
    scale = HEAD**-0.5

    @pl.when(step == 0)
    def _():
        v = qkv_ref[:, 2 * PAIR :]
        mark = jnp.broadcast_to((slot < 3).astype(f32), v.shape).astype(bf16)
        vals[0] = jnp.where(low, v, mark)
        vals[1] = jnp.where(low, mark, v)
        dkeys[...] = jnp.zeros_like(dkeys)
        dvals[...] = jnp.zeros_like(dvals)
        sums_ref[...] = jnp.zeros_like(sums_ref)

    near = step < steps // 2
    incoming = jnp.where(near, grad_a_ref[...], grad_b_ref[...])
    ctx = jnp.where(near, ctx_a_ref[...], ctx_b_ref[...])
    rows = pl.ds(pl.multiple_of(step * block, block), block)
    grad = (incoming.astype(f32) * inv_ref[...]).astype(bf16)
    product = grad.astype(f32) * ctx.astype(f32)
    grad_t, q_t = grad.T, qkv_ref[rows, :PAIR].T
    dqs = []
    for h in range(2):
        keep = low if h == 0 else jnp.logical_not(low)
        inner = jnp.sum(jnp.where(keep, product, 0.0), axis=1, keepdims=True)
        top = inner.astype(bf16).astype(f32)
        mid = (inner - top).astype(bf16).astype(f32)
        last = inner - top - mid
        mark = jnp.where(slot == 0, -top, jnp.where(slot == 1, -mid, jnp.where(slot == 2, -last, 0.0)))
        left = jnp.where(keep, grad, mark.astype(bf16))
        part = slice(h * HEAD, (h + 1) * HEAD)
        dq = None
        for j in range(length // chunk):
            cols = slice(j * chunk, (j + 1) * chunk)
            prob = prob_ref[h, :, cols]
            ds = prob * dot(left, vals[h, cols, :], 1, 1).astype(bf16)
            dvals[part, cols] += dot(grad_t[part], prob, 1, 0)
            dkeys[part, cols] += dot(q_t[part], ds, 1, 0)
            term = dot(ds, qkv_ref[cols, PAIR : 2 * PAIR], 1, 0)
            dq = term if dq is None else dq + term
        dqs.append(dq)
    dq = (jnp.where(low, dqs[0], dqs[1]) * scale).astype(bf16)
    dqkv_ref[rows, :PAIR] = dq
    sums_ref[0:1, :PAIR] += jnp.sum(dq.astype(f32), axis=0, keepdims=True)

    @pl.when(step == steps - 1)
    def _():
        dqkv_ref[:, PAIR : 2 * PAIR] = (dkeys[...] * scale).T.astype(bf16)
        dv = dvals[...].T.astype(bf16)
        dqkv_ref[:, 2 * PAIR :] = dv
        sums_ref[0:1, 2 * PAIR :] = jnp.sum(dv.astype(f32), axis=0, keepdims=True)


def attention_backward(pair, grads, ctxs, inv, qkv, prob, before, block=256, chunk=2048):
    length = qkv.shape[0]
    steps = length // block
    halves = [pl.BlockSpec(s.block_shape, lambda b, s=s: s.index_map(pair, b)) for s in half_specs(block, steps, lambda p: p)]
    return pl.pallas_call(
        functools.partial(attention_backward_kernel, min(chunk, length)),
        grid=(steps,),
        in_specs=halves
        + halves
        + [
            pl.BlockSpec((block, PAIR), lambda b: (b, pair)),
            pl.BlockSpec((length, TRIO), lambda b: (0, pair)),
            pl.BlockSpec((2, block, length), lambda b: (pair, b, 0)),
        ]
        + [pl.BlockSpec(memory_space=pl.ANY)] * len(before),
        out_specs=[pl.BlockSpec((length, TRIO), lambda b: (0, pair)), pl.BlockSpec((8, TRIO), lambda b: (0, 0))],
        out_shape=[shape_of(length, qkv.shape[1], bf16), shape_of(8, TRIO, f32)],
        scratch_shapes=[
            pltpu.VMEM((2, length, PAIR), bf16),
            pltpu.VMEM((PAIR, length), f32),
            pltpu.VMEM((PAIR, length), f32),
        ],
        input_output_aliases={7: 0} if before else {},
        compiler_params=params(),
        cost_estimate=pl.CostEstimate(flops=0, bytes_accessed=0, transcendentals=0),
        name="attention_backward",
    )(*grads, *ctxs, inv, qkv, prob, *before)


def norm_stats(values):
    centered = values - jnp.mean(values, axis=-1, keepdims=True)
    inverse = lax.rsqrt(jnp.mean(centered * centered, axis=-1, keepdims=True) + EPSILON)
    return centered * inverse, inverse


def norm_backward(grad, gain, normed, inverse):
    t = grad * gain
    return (
        t - jnp.mean(t, axis=-1, keepdims=True) - normed * jnp.mean(t * normed, axis=-1, keepdims=True)
    ) * inverse


def row_sum(values):
    return jnp.sum(values, axis=0, keepdims=True)


def normal(u):
    return 0.5 + 0.5 * lax.erf(u * math.sqrt(0.5)), jnp.exp(u * u * -0.5) * (1.0 / math.sqrt(2.0 * math.pi))


def feed_forward_kernel(count, chunk, core_ref, *refs):
    toks, cots = refs[:count], refs[count : 2 * count]
    (ctx_a_ref, ctx_b_ref, wo_ref, wu_ref, wd_ref, vec_ref, bu_ref) = refs[2 * count : 2 * count + 7]
    outs = refs[2 * count + 7 : 3 * count + 7]
    slope_ref, r2_ref, n1_ref, inv_ref, sums_ref, sent_ref, kept_ref, act, total_down = refs[3 * count + 7 :]
    step, steps = pl.program_id(0), pl.num_programs(0)
    index = step // (steps // count)

    @pl.when(step == 0)
    def _():
        sums_ref[...] = jnp.zeros_like(sums_ref)
        total_down[...] = jnp.zeros_like(total_down)

    bo, g1, s1, bd, g2, s2 = [vec_ref[i : i + 1] for i in range(6)]
    split = ctx_a_ref.shape[1]
    branch = dot(ctx_a_ref[...], wo_ref[:split], 1, 0) + dot(ctx_b_ref[...], wo_ref[split:], 1, 0)
    n1, inv1 = norm_stats(pick(index, toks).astype(f32) + branch + bo)
    hidden = n1 * g1 + s1
    low = hidden.astype(bf16)
    n1_ref[...] = n1
    inv_ref[...] = jnp.broadcast_to(inv1, inv_ref.shape)
    total = hidden + bd
    slices = [slice(j * chunk, (j + 1) * chunk) for j in range(wu_ref.shape[1] // chunk)]
    for cols in slices:
        pre = dot(low, wu_ref[:, cols], 1, 0) + bu_ref[:, cols]
        cdf, phi = normal(pre)
        part = (pre * cdf).astype(bf16)
        act[:, cols] = part
        slope_ref[:, cols] = (cdf + pre * phi).astype(bf16)
        total += dot(part, wd_ref[cols, :], 1, 0)
    n2, inv2 = norm_stats(total)
    result = (n2 * g2 + s2).astype(bf16)
    for s in range(count):

        @pl.when(index == s)
        def _(s=s):
            outs[s][...] = result

    grad = pick(index, cots).astype(f32)
    r2 = norm_backward(grad, g2, n2, inv2)
    feed = r2.astype(bf16)
    r2_ref[...] = r2
    sums_ref[0:1] += row_sum(grad * n2)
    sums_ref[1:2] += row_sum(grad)
    sums_ref[2:3] += row_sum(feed.astype(f32))
    for cols in slices:
        total_down[cols] += dot(act[:, cols], feed, 0, 0)

    @pl.when(step == steps - 1)
    def _():
        half = sent_ref.shape[0]
        for ref, place in ((sent_ref, 1 - core_ref[0]), (kept_ref, core_ref[0])):
            ref[...] = total_down[pl.ds(pl.multiple_of(place * half, half), half)].astype(bf16)


def feed_backward_kernel(
    chunk, core_ref, r2_ref, slope_ref, n1_ref, inv_ref, ctx_a_ref, ctx_b_ref, first_sums_ref,
    wo_ref, wu_ref, wd_ref, vec_ref, r1_ref, dctx_a_ref, dctx_b_ref, sent_ref, kept_ref,
    sums, upsum, total_up, total_out,
):
    step, steps = pl.program_id(0), pl.num_programs(0)

    @pl.when(step == 0)
    def _():
        for ref in (sums, upsum, total_up, total_out):
            ref[...] = jnp.zeros_like(ref)

    width, hidden = wu_ref.shape
    grad, n1 = r2_ref[...], n1_ref[...]
    feed, low = grad.astype(bf16), (n1 * vec_ref[1:2] + vec_ref[2:3]).astype(bf16)
    for j in range(hidden // chunk):
        cols = slice(j * chunk, (j + 1) * chunk)
        pre = (dot(feed, wd_ref[cols, :], 1, 1) * slope_ref[:, cols].astype(f32)).astype(bf16)
        upsum[0:1, cols] += row_sum(pre.astype(f32))
        grad += dot(pre, wu_ref[:, cols], 1, 1)
        total_up[:, cols] += dot(low, pre, 0, 0)
    r1 = norm_backward(grad, vec_ref[1:2], n1, inv_ref[:, :1])
    branch = r1.astype(bf16)
    r1_ref[...] = r1
    split = dctx_a_ref.shape[1]
    dctx_a_ref[...] = dot(branch, wo_ref[:split], 1, 1).astype(bf16)
    dctx_b_ref[...] = dot(branch, wo_ref[split:], 1, 1).astype(bf16)
    total_out[:split] += dot(ctx_a_ref[...], branch, 0, 0)
    total_out[split:] += dot(ctx_b_ref[...], branch, 0, 0)
    sums[0:1] += row_sum(grad * n1)
    sums[1:2] += row_sum(grad)
    sums[2:3] += row_sum(branch.astype(f32))

    @pl.when(step == steps - 1)
    def _():
        core = core_ref[0]
        vectors = [first_sums_ref[i : i + 1] for i in range(3)] + [sums[i : i + 1] for i in range(3)]
        vectors += [upsum[0:1, i * width : (i + 1) * width] for i in range(hidden // width)]
        each = (len(vectors) + 1) // 2
        vectors += [jnp.zeros_like(vectors[0])] * (2 * each - len(vectors))
        blank = jnp.zeros((PAIR - each, width), f32)
        blocks = [jnp.concatenate(vectors[i * each : (i + 1) * each] + [blank], axis=0).T for i in range(2)]
        half = hidden // 2
        for ref, place in ((sent_ref, 1 - core), (kept_ref, core)):
            ref[:, :half] = total_up[:, pl.ds(pl.multiple_of(place * half, PAIR), half)].astype(bf16)
            columns = pl.ds(pl.multiple_of(place * split, PAIR), split)
            for g in range(2):
                rows = pl.ds(pl.multiple_of(jnp.bitwise_xor(core, g) * split, split), split)
                ref[g * split : (g + 1) * split, half : half + split] = total_out[rows, columns].astype(bf16)
            ref[:, half + split :] = jnp.where(place == 0, blocks[0], blocks[1]).astype(bf16)


def whole(values):
    return pl.BlockSpec(values.shape, lambda i, _: (0,) * values.ndim, pipeline_mode=pl.Buffered(1))


def fixed(rows, cols):
    return pl.BlockSpec((rows, cols), lambda i, _: (0, 0))


def row_blocks(block, *widths):
    return [pl.BlockSpec((block, n), lambda i, _: (i, 0)) for n in widths]


def feed_forward(core, toks, cots, ctx_a, ctx_b, wo, wu, wd, vec, bu, block=256):
    width, hidden = wu.shape
    count = ctx_a.shape[0]
    outs = [shape_of(x.shape[0], width, bf16) for x in toks]
    return pl.pallas_call(
        functools.partial(feed_forward_kernel, len(toks), 768),
        grid_spec=pltpu.PrefetchScalarGridSpec(
            num_scalar_prefetch=1,
            grid=(count // block,),
            in_specs=piece_specs(block, toks)
            + piece_specs(block, cots)
            + row_blocks(block, ctx_a.shape[1], ctx_b.shape[1])
            + [whole(x) for x in (wo, wu, wd, vec, bu)],
            out_specs=piece_specs(block, outs)
            + row_blocks(block, hidden, width, width, PAIR)
            + [fixed(8, width), fixed(hidden // 2, width), fixed(hidden // 2, width)],
            scratch_shapes=[pltpu.VMEM((block, hidden), bf16), pltpu.VMEM((hidden, width), f32)],
        ),
        out_shape=outs
        + [
            shape_of(count, hidden, bf16),
            shape_of(count, width, f32),
            shape_of(count, width, f32),
            shape_of(count, PAIR, f32),
            shape_of(8, width, f32),
            shape_of(hidden // 2, width, bf16),
            shape_of(hidden // 2, width, bf16),
        ],
        compiler_params=params(),
        cost_estimate=pl.CostEstimate(flops=0, bytes_accessed=0, transcendentals=0),
        name="feed_forward",
    )(core, *toks, *cots, ctx_a, ctx_b, wo, wu, wd, vec, bu)


def feed_backward(core, r2, slope, n1, inv, ctx_a, ctx_b, first_sums, wo, wu, wd, vec, block=256):
    count, width = r2.shape
    hidden, local = wu.shape[1], ctx_a.shape[1]
    out = hidden // 2 + local + PAIR
    return pl.pallas_call(
        functools.partial(feed_backward_kernel, 768),
        grid_spec=pltpu.PrefetchScalarGridSpec(
            num_scalar_prefetch=1,
            grid=(count // block,),
            in_specs=row_blocks(block, width, hidden, width, PAIR, local, local)
            + [whole(x) for x in (first_sums, wo, wu, wd, vec)],
            out_specs=row_blocks(block, width, local, local) + [fixed(width, out), fixed(width, out)],
            scratch_shapes=[
                pltpu.VMEM((8, width), f32),
                pltpu.VMEM((8, hidden), f32),
                pltpu.VMEM((width, hidden), f32),
                pltpu.VMEM((width, width), f32),
            ],
        ),
        out_shape=[
            shape_of(count, width, f32),
            shape_of(count, local, bf16),
            shape_of(count, local, bf16),
            shape_of(width, out, bf16),
            shape_of(width, out, bf16),
        ],
        compiler_params=params(),
        cost_estimate=pl.CostEstimate(flops=0, bytes_accessed=0, transcendentals=0),
        name="feed_backward",
    )(core, r2, slope, n1, inv, ctx_a, ctx_b, first_sums, wo, wu, wd, vec)


def assemble_kernel(parts, cuts, place_ref, *refs):
    count = (len(refs) - len(cuts)) // 2
    own, got, outs = refs[:count], refs[count : 2 * count], refs[2 * count :]
    low = jnp.bitwise_and(jnp.where(pl.program_id(0) == place_ref[0], place_ref[1], place_ref[2]), parts - 1)
    size = own[0].shape[0] // parts

    def write(sources):
        for t in range(parts):
            start = pl.multiple_of(jnp.bitwise_xor(low, t) * size, 16)
            for out, pieces in zip(outs, cuts, strict=True):
                for which, source, target, width in pieces:
                    out[t * size : (t + 1) * size, target : target + width] = sources[which][
                        pl.ds(start, size), source : source + width
                    ].astype(f32)

    @pl.when(pl.program_id(0) == place_ref[0])
    def _():
        write(own)

    @pl.when(pl.program_id(0) != place_ref[0])
    def _():
        write(got)


def assemble(place, own, got, cuts, by_rows, blocks=2):
    rows, parts = own[0].shape[0], 8 // blocks
    size = rows // blocks
    mine = lambda h, j, ref: (jnp.where(h == ref[0], jnp.bitwise_xor(j, ref[1] // parts), 0), 0)
    other = lambda h, j, ref: (jnp.where(h == ref[0], 0, jnp.bitwise_xor(j, ref[2] // parts)), 0)
    outs, specs = [], []
    for pieces in cuts:
        width = sum(piece[-1] for piece in pieces)
        if by_rows:
            outs.append(shape_of(2 * rows, width, f32))
            specs.append(pl.BlockSpec((size, width), lambda h, j, ref: (blocks * h + j, 0)))
        else:
            outs.append(shape_of(rows, 2 * width, f32))
            specs.append(pl.BlockSpec((size, width), lambda h, j, ref: (j, h)))
    return pl.pallas_call(
        functools.partial(assemble_kernel, parts, cuts),
        grid_spec=pltpu.PrefetchScalarGridSpec(
            num_scalar_prefetch=1,
            grid=(2, blocks),
            in_specs=[pl.BlockSpec((size, x.shape[1]), mine) for x in own]
            + [pl.BlockSpec((size, x.shape[1]), other) for x in got],
            out_specs=specs,
        ),
        out_shape=outs,
        compiler_params=params(),
        cost_estimate=pl.CostEstimate(flops=0, bytes_accessed=0, transcendentals=0),
        name="assemble",
    )(place, *own, *got)


def cut(values, index, axis=0):
    size = values.shape[axis] // 2
    return lax.dynamic_slice_in_dim(values, index * size, size, axis)


def total_of(terms):
    value = terms[0].astype(f32)
    for term in terms[1:]:
        value += term.astype(f32)
    return value.astype(bf16)


class Exchange:
    def __init__(self, row_size, seq_size, *orders):
        seq_bits, row_bits = seq_size.bit_length() - 1, row_size.bit_length() - 1
        x, rows = list(range(1, seq_bits)), list(range(seq_bits, seq_bits + row_bits))
        every = rows[:2] + x + rows[2:]
        first, second = [[every[i] for i in order] for order in orders]
        self.orders = (first, second)
        self.rest = every[3:]
        self.size = row_size * seq_size
        self.phases = len(first)
        here = lax.axis_index("rows") * seq_size + lax.axis_index("seq")
        self.core = jnp.bitwise_and(here, 1)
        bit = lambda k: jnp.bitwise_and(lax.shift_right_logical(here, k), 1)
        self.bits = [jnp.where(self.core == 0, bit(a), bit(b)) for a, b in zip(first, second)]
        places = []
        for order in self.orders:
            place = 0
            for k in order:
                place = 2 * place + bit(k)
            places.append(place)
        own = jnp.where(self.core == 0, places[0], places[1])
        other = jnp.where(self.core == 0, places[1], places[0])
        self.place = jnp.stack([self.core, own, other]).astype(jnp.int32)

    def send(self, values, phase):
        pairs = [(d, d ^ (1 << self.orders[d & 1][phase])) for d in range(self.size)]
        return lax.ppermute(values, BOTH, pairs)

    def halves(self, phase, *terms):
        bit = self.bits[phase]
        return total_of([cut(x, 1 - bit) for x in terms]), total_of([cut(x, bit) for x in terms])

    def finish(self, *terms):
        value = total_of(terms)
        for k in self.rest[1:]:
            value = total_of([value, self.whole(value, k)])
        return value

    def whole(self, values, k):
        return lax.ppermute(values, BOTH, [(d, d ^ (1 << k)) for d in range(self.size)])

    def by(self, phase):
        if phase == self.phases:
            return lambda values: self.whole(values, self.rest[0])
        return lambda values: self.send(values, phase)


def step(*operands, work=None, carry=()):
    values = lax.optimization_barrier(tuple(x for x, _ in operands))
    got = [how(x) for x, (_, how) in zip(values, operands)]
    done = None if work is None else work(values)
    return lax.optimization_barrier((tuple(values), tuple(got), done, carry))


def joined(own, got):
    return jnp.concatenate([own, got], axis=0)


def on_device(
    sizes, tokens, segments, query_weight, query_bias, key_weight, value_weight, value_bias, out_weight, out_bias,
    first_gain, first_shift, up_weight, up_bias, down_weight, down_bias, second_gain, second_shift, cotangent,
):
    row_size, seq_size = sizes
    row_count, pos, width = tokens.shape
    groups = math.gcd(row_count, seq_size)
    subs = seq_size // groups
    if row_count != 2 or groups != 2 or subs != 2:
        raise ValueError("unsupported split")
    me = lax.axis_index("seq")
    group, sub = me // subs, lax.rem(me, subs)
    length = pos * seq_size
    half = length // 2
    local = width // subs
    pairs = local // PAIR
    exchange = Exchange(row_size, seq_size, (0, 2, 1), (1, 0, 2))
    up_exchange = Exchange(row_size, seq_size, (0, 2, 1), (1, 2, 0))
    three_exchange = Exchange(row_size, seq_size, (0, 2, 1), (2, 1, 0))

    def shifted(values, s):
        return lax.ppermute(values, "seq", [(i, (i + s * subs) % seq_size) for i in range(seq_size)])

    def cut_rows(values):
        return [lax.dynamic_index_in_dim(values, lax.rem(group + s, groups), 0, keepdims=False) for s in range(groups)]

    def trade(blocks):
        return blocks[:1] + [shifted(x, s) for s, x in enumerate(blocks[1:], 1)]

    def place_rows(pieces):
        rows = []
        for r in range(groups):
            picked = pieces[0]
            for s in range(1, groups):
                picked = jnp.where(lax.rem(group + s, groups) == r, pieces[s], picked)
            rows.append(picked)
        return jnp.stack(rows)

    def core_swap(values):
        return lax.ppermute(values, "seq", [(i, i ^ 1) for i in range(seq_size)])

    tok_blocks = cut_rows(tokens)
    trade_back = lambda values: shifted(values, 1)
    toks = trade(tok_blocks)
    late_group, late = tie((group, sub), tok_blocks[1:])
    cot_blocks = [lax.dynamic_index_in_dim(cotangent, lax.rem(late_group + s, groups), 0, keepdims=False) for s in range(groups)]

    seg_row = lax.dynamic_index_in_dim(segments, late_group, 0, keepdims=False)
    middle = seg_row[length // 2]
    seg_pieces = []
    for u in range(subs):
        for s in range(groups):
            quarter = lax.rem(late_group + groups - s, groups) * subs + lax.rem(late + u, subs)
            seg_pieces.append(lax.dynamic_slice_in_dim(seg_row, quarter * pos, pos, 0))
    seg_k = jnp.stack(seg_pieces).astype(f32)
    seg_q = seg_k.reshape(length, 1)
    outside = jnp.where(seg_q == middle, 0.0, BLOCKED)
    slot = (jnp.arange(PAIR) % HEAD)[None, :]
    q_mark = jnp.where(slot == 0, 1.0, jnp.where(slot == 1, outside, 0.0)).astype(bf16)
    k_mark = jnp.where(slot == 0, outside, jnp.where(slot == 1, 1.0, 0.0)).astype(bf16)

    w_qkv, b_qkv, vec, bu = gather_columns(
        late, query_weight, key_weight, value_weight, query_bias, value_bias, up_bias,
        (out_bias, first_gain, first_shift, down_bias, second_gain, second_shift), local,
    )
    wo = jnp.concatenate([lax.dynamic_slice_in_dim(out_weight, i * local, local, 0) for i in (late, 1 - late)], axis=0)
    prepared = (wo, vec, bu, w_qkv, b_qkv, q_mark, k_mark, seg_k, cot_blocks)
    far = [core_swap(toks[0])] + [core_swap(tie(x, prepared)) for x in toks[1:]]
    toks_all = toks + far
    ctx_a, ctx_b, prob, inv, qkv = attention_forward(toks_all, w_qkv, b_qkv, q_mark, k_mark, seg_k)
    cots = trade(cot_blocks)
    tok_full = jnp.concatenate(toks_all, axis=0)
    ctx_got = core_swap(ctx_b)
    core = sub.reshape(1).astype(jnp.int32)
    made = feed_forward(core, toks, cots, ctx_a, ctx_got, wo, up_weight, down_weight, vec, bu)
    outs, (slope, r2, n1, inv1, sums_two, down_sent, down_kept) = made[:groups], made[groups:]

    def backward(sent):
        return feed_backward(
            core, tie(r2, sent), slope, n1, inv1, ctx_a, ctx_got, sums_two, wo, up_weight, down_weight, vec
        )

    _, (down_got,), made, down_kept = step((down_sent, core_swap), work=backward, carry=down_kept)
    r1, dctx_a, dctx_b, up_sent, up_kept = made
    _, (dctx_got,), (send_down, down), (up_sent, up_kept) = step(
        (dctx_b, core_swap), work=lambda sent: exchange.halves(0, *tie((down_kept, down_got), sent)), carry=(up_sent, up_kept)
    )
    grads, ctxs = (dctx_a, dctx_got), (ctx_a, ctx_b)
    dqkv, biases = (), []
    for p in range(pairs):

        def work(sent, p=p, dqkv=dqkv):
            return attention_backward(p, tie(grads, sent), ctxs, inv, qkv, prob, dqkv)

        operands = [(send_down, exchange.by(p)), (up_sent, core_swap) if p == 0 else (send_up, up_exchange.by(p - 1))]
        operands += [(outs[1], trade_back)] if p == 0 else []
        kept = (down, up_kept) if p == 0 else (down, up)
        _, got, (made, bias), (down, up) = step(*operands, work=work, carry=kept)
        out_got = got[2] if p == 0 else out_got
        dqkv = (made,)
        biases.append(bias[0])
        if p + 1 < exchange.phases:
            send_down, down = exchange.halves(p + 1, down, got[0])
        else:
            send_down = down = total_of([down, got[0]])
        send_up, up = up_exchange.halves(p, up, got[1])
    dqkv = dqkv[0]
    bias_q = jnp.concatenate([b[:PAIR] for b in biases])
    bias_v = jnp.concatenate([b[2 * PAIR :] for b in biases])
    bias_col = jnp.pad(jnp.concatenate([bias_q, bias_v]).astype(bf16)[:, None], ((0, 0), (0, PAIR - 1)))
    three = jnp.concatenate([dot(tok_full, dqkv, 0, 0).astype(bf16), bias_col], axis=1)
    send_three, three = three_exchange.halves(0, three)

    def share_far(sent):
        d, w = tie((dqkv, w_qkv), sent)
        return dot(d[half:], w, 1, 1).astype(bf16)

    _, (got, up_got, down_got), far, (three, up, down) = step(
        (send_three, three_exchange.by(0)), (send_up, up_exchange.by(2)), (send_down, exchange.by(3)), work=share_far,
        carry=(three, up, down),
    )
    send_three, three = three_exchange.halves(1, three, got)
    up, down = total_of([up, up_got]), exchange.finish(down, down_got)

    def share_near(sent):
        d, w = tie((dqkv, w_qkv), sent)
        return r1 + dot(d[:half], w, 1, 1)

    (_, _, _, far), (got, up_got, down_got, far_got), near, (three, up, down) = step(
        (send_three, three_exchange.by(1)), (up, up_exchange.by(3)), (down, exchange.by(2)), (far, core_swap),
        work=share_near, carry=(three, up, down),
    )
    in_half = near + far_got.astype(f32)
    in_sent = in_half[pos:].astype(bf16)
    send_three, three = three_exchange.halves(2, three, got)
    up, down = up_exchange.finish(up, up_got), joined(down, down_got)
    _, (got, up_got, down_got), output, (three, up, down) = step(
        (send_three, three_exchange.by(2)), (up, up_exchange.by(2)), (down, exchange.by(1)),
        work=lambda sent: place_rows([outs[0], tie(out_got, sent)]), carry=(three, up, down),
    )
    three = total_of([three, got])
    up, down = joined(up, up_got), joined(down, down_got)
    _, (got, up_got, down_got), _, (three, up, down) = step(
        (three, three_exchange.by(3)), (up, up_exchange.by(1)), (down, exchange.by(0)), carry=(three, up, down)
    )
    three = three_exchange.finish(three, got)
    up, down = joined(up, up_got), joined(down, down_got)
    _, (got, up_got, down_got, in_got), _, (three, up, down) = step(
        (three, three_exchange.by(2)), (up, up_exchange.by(0)), (down, core_swap), (in_sent, trade_back),
        carry=(three, up, down),
    )
    three, up = joined(three, got), joined(up, up_got)

    def assemble_down(sent):
        return assemble(exchange.place, [tie(down, sent)], [down_got], [[(0, 0, 0, width)]], True)[0]

    _, (got, up_got), downweight_grad, (three, up) = step(
        (three, three_exchange.by(1)), (up, core_swap), work=assemble_down, carry=(three, up)
    )
    three = joined(three, got)
    hidden = up_bias.shape[0]
    vectors = 6 + hidden // width
    each = (vectors + 1) // 2

    def assemble_up(sent):
        cuts = [[(0, 0, 0, hidden // 2)], [(0, hidden // 2, 0, local)], [(0, hidden // 2 + local, 0, PAIR)]]
        made = assemble(up_exchange.place, [tie(up, sent)], [up_got], cuts, False)
        return made, place_rows([in_half[:pos], tie(in_got, sent).astype(f32)])

    _, (got,), ((upweight_grad, outweight_grad, vector_grads), input_grad), three = step(
        (three, three_exchange.by(0)), work=assemble_up, carry=three
    )
    three = joined(three, got)
    _, (three_got,), _, three = step((three, core_swap), carry=three)
    cuts = [[(0, p * TRIO + i * PAIR, p * PAIR, PAIR) for p in range(pairs)] for i in range(3)]
    queryweight_grad, keyweight_grad, valueweight_grad, bias_out = assemble(
        three_exchange.place, [three], [three_got], cuts + [[(0, 3 * local, 0, PAIR)]], False
    )
    bias_out = bias_out.reshape(2, local, 2, PAIR)[:, :, :, 0]
    query_bias_grad = bias_out[0].T.reshape(width)
    value_bias_grad = bias_out[1].T.reshape(width)

    small = jnp.concatenate([vector_grads[:, :each], vector_grads[:, PAIR : PAIR + each]], axis=1).T
    return (
        output, input_grad, queryweight_grad, query_bias_grad, keyweight_grad, valueweight_grad, value_bias_grad,
        outweight_grad, small[5], small[3], small[4], upweight_grad, small[6:vectors].reshape(-1),
        downweight_grad, small[2], small[0], small[1],
    )


def solution(mesh):
    split = P("rows", "seq", None)
    return jax.shard_map(
        functools.partial(on_device, (mesh.shape["rows"], mesh.shape["seq"])),
        mesh=mesh,
        in_specs=(split, P("rows", None)) + (P(),) * 15 + (split,),
        out_specs=(split, split) + (P(),) * 15,
        check_vma=False,
    )
```
